32 devices in a mesh: gx: 4 (over y, core), gy: 8 (over z, x).
Axes of the slice: x: 2, y: 2, z: 4, core: 2. Of those that a mesh axis runs over, the one named last changes fastest.
Arguments:
- air_forcing_quantities: float32 [8, 65536], P(None, ('gx', 'gy')), may hold values from -6 to 6
- segment_sea_subdomain: int32 [8192, 1], P(('gx', 'gy')), may hold values from 0 to 31; in each aligned block of 256 rows (0 to 255, 256 to 511, ...) at most 16 rows name the same one
- overlay_air_element: int32 [8192, 128], P(('gx', 'gy')), may hold values from 0 to 2047
- overlay_sea_profile: int32 [8192, 128], P(('gx', 'gy')), may hold values from 0 to 16383
- overlay_fraction_share: float32 [8192, 128], P(('gx', 'gy')), may hold values from 0.02 to 0.5
- thermal_deviation: float32 [20, 256, 2048], P(None, 'gy', 'gx'), may hold values from -6 to 6
- saltiness_deviation: float32 [20, 256, 2048], P(None, 'gy', 'gx'), may hold values from -6 to 6
- zonal_interface_speed: float32 [20, 256, 2048], P(None, 'gy', 'gx'), may hold values from -0.3 to 0.3
- poleward_interface_speed: float32 [20, 256, 2048], P(None, 'gy', 'gx'), may hold values from -0.3 to 0.3
- sea_profile_indicator: int32 [256, 2048], P('gy', 'gx'), may hold values 0 or 1
Outputs:
- temperature_out: float32 [20, 256, 2048], P(None, 'gy', 'gx')
- salinity_out: float32 [20, 256, 2048], P(None, 'gy', 'gx')
- back_fields: float32 [4, 65536], P(None, ('gx', 'gy'))
The draws below stay inside these ranges and needn't reach their ends.
Inputs may be any that keep to these rules, and one draw needn't show every extreme that they name: segment_sea_subdomain names a tile as longitude tile times the number of latitude tiles plus latitude tile. Among the rows of one device at most 16 blocks name the same tile, and some device sends exactly 16 to one tile. overlay_air_element index the atmosphere cells of the tile that holds the block. overlay_sea_profile index the destination tile's columns as latitude row times 512 plus longitude column.
All inputs are finite; a program needn't handle non-finite values. No bound on the sum of `sea_profile_indicator` on one device may be relied on, other than what follows from the above.
Results may differ from the reference program's by a relative error of at most 0.00002.
Values sent between devices are 32-bit elements; how exact they have to be, the bound alone decides.
A program may use at most 192 MiB of HBM per device.

```python
import math
import jax
import jax.numpy as jnp
import numpy as np
from jax import lax

FIELDS = 8
A_DEV = 2048
BLK_DEV = 256
ENTRIES = 128
OX = 512
OY = 32
SEA_LAYER_COUNT = 20
CAP = 16
BLOCKS = 8192
A_CELLS = 65536
GRID_MERIDIANS = 2048
GRID_PARALLELS = 256
N_GX = 4
N_GY = 8


def set_ends(entries, rng, low, top_value):
    longest = entries.shape.index(max(entries.shape))
    spots = []
    for shift in (0, 1):
        where = [jax.random.randint(jax.random.fold_in(rng, axis), (), 0, length) for axis, length in enumerate(entries.shape)]
        where[longest] = (where[longest] + shift) % entries.shape[longest]
        spots.append(tuple(where))
    return entries.at[spots[0]].set(low).at[spots[1]].set(top_value)


def level_of(key, dims, cuts, low, top_value):
    def one(axis_at, shards_of):
        steps = jax.random.uniform(jax.random.fold_in(jax.random.fold_in(key, 6), axis_at), (shards_of,), jnp.float32, low / len(cuts), top_value / len(cuts))
        return jnp.repeat(jnp.exp(steps), dims[axis_at] // shards_of).reshape((-1,) + (1,) * (len(dims) - axis_at - 1))

    level = one(*cuts[0])
    for cut in cuts[1:]:
        level = level * one(*cut)
    return level


def deal_out(key, own, number, rows, number_of, top, most, slope):
    order = jax.random.permutation(key, number_of)
    packed, ordinary = portions_of(number_of, rows * top, most, slope, True), portions_of(number_of, rows * top, most, slope, False)
    places = jnp.arange(number_of)

    def named(tallies, turn):
        used = int((tallies > 0).sum())
        fixed = max(1, used // 4)
        moved = fixed + (places - fixed + turn * (used - fixed)) % max(1, number_of - fixed)
        return jnp.zeros((number_of,), jnp.int32).at[order[jnp.where(places < fixed, places, moved)]].set(jnp.asarray(tallies, jnp.int32))

    tallies = jnp.where(number % 4 == 0, named(packed, number // 4), named(ordinary, number - number // 4 - 1))
    mixed = jax.random.permutation(jax.random.fold_in(own, 3), number_of)
    giver, taker = mixed[0:number_of // 2 * 2:2], mixed[1:number_of // 2 * 2:2]
    margin = jnp.minimum(tallies[giver] - 1, most - tallies[taker]) // 2
    margin = jnp.where((giver == order[0]) | (taker == order[0]) | (tallies[taker] == 0), 0, jnp.maximum(margin, 0))
    moved = jax.random.randint(jax.random.fold_in(own, 4), (number_of // 2,), 0, 1 << 20) % (margin + 1)
    tallies = tallies.at[giver].add(-moved).at[taker].add(moved)
    labels = jnp.searchsorted(jnp.cumsum(tallies), jnp.arange(rows * top), side="right").astype(jnp.int32)
    grid = labels.reshape(top, rows).T
    grid = grid[jax.random.permutation(jax.random.fold_in(own, 1), rows)]
    turn = jax.random.randint(jax.random.fold_in(own, 2), (rows, 1), 0, top)
    return jnp.take_along_axis(grid, (jnp.arange(top)[None, :] + turn) % top, axis=1)


def portions_of(amount, total, most, skew, full):
    loads = [(1 << 20) // math.isqrt(grade ** skew) + 1 for grade in range(1, amount + 1)]
    largest = most if full else min(most, max(-(-total // amount), total * loads[0] // sum(loads)))
    least = 1 if total - largest >= amount - 1 else 0
    counts, rest = [largest] + [least] * (amount - 1), total - largest - least * (amount - 1)
    while rest > 0:
        free = [i for i in range(1, amount) if counts[i] < largest] or [i for i in range(1, amount) if counts[i] < most]
        mass, left = sum([loads[i] for i in free]), rest
        for i in free:
            addition = min(most - counts[i], max(1, left * loads[i] // mass), rest)
            counts[i] = counts[i] + addition
            rest = rest - addition
    return np.array(counts)


def gaussian(rng, shape, width, most, cuts=(), kind=jnp.bfloat16):
    array = width * jax.random.normal(rng, shape, jnp.float32)
    if cuts:
        array = array * level_of(rng, shape, cuts, -0.22, 0.18)
    return jnp.clip(array, -most, most).astype(kind)


def setup_inputs(seed: int = 0) -> dict:
    key_list = jax.random.split(jax.random.key(seed), 11)
    air_forcing_quantities = gaussian(key_list[0], (FIELDS, A_CELLS), 1.0, 6.0, ((1, 32),), jnp.float32)
    segment_sea_subdomain_keys = jax.random.split(jax.random.fold_in(key_list[1], 1), BLOCKS // BLK_DEV)
    segment_sea_subdomain_turns = jax.random.permutation(jax.random.fold_in(key_list[1], 3), BLOCKS // BLK_DEV)
    segment_sea_subdomain = jax.vmap(lambda own, number: deal_out(jax.random.fold_in(key_list[1], 2), own, number, BLK_DEV, N_GX * N_GY, 1, CAP, 1))(segment_sea_subdomain_keys, segment_sea_subdomain_turns).reshape((BLOCKS, 1))
    overlay_air_element = set_ends(jax.random.randint(key_list[2], (BLOCKS, ENTRIES), 0, A_DEV), jax.random.fold_in(key_list[2], 1), 0, A_DEV - 1).astype(jnp.int32)
    overlay_sea_profile = set_ends(jax.random.randint(key_list[3], (BLOCKS, ENTRIES), 0, OY * OX), jax.random.fold_in(key_list[3], 1), 0, (OY * OX) - 1).astype(jnp.int32)
    overlay_fraction_share = jnp.clip(jnp.exp(math.log(0.5) - 3.218876 * jax.random.uniform(key_list[4], (BLOCKS, ENTRIES), jnp.float32) ** level_of(key_list[4], (BLOCKS, ENTRIES), ((0, 32),), -0.2, 0.2)), 0.02, 0.5)
    thermal_deviation = gaussian(key_list[5], (SEA_LAYER_COUNT, GRID_PARALLELS, GRID_MERIDIANS), 1.0, 6.0, ((1, 8), (2, 4)), jnp.float32)
    saltiness_deviation = gaussian(key_list[6], (SEA_LAYER_COUNT, GRID_PARALLELS, GRID_MERIDIANS), 1.0, 6.0, ((1, 8), (2, 4)), jnp.float32)
    zonal_interface_speed = jnp.clip(jax.random.uniform(key_list[7], (SEA_LAYER_COUNT, GRID_PARALLELS, GRID_MERIDIANS), jnp.float32, -0.3, 0.3) * level_of(key_list[7], (SEA_LAYER_COUNT, GRID_PARALLELS, GRID_MERIDIANS), ((1, 8), (2, 4)), -0.4, 0.0), -0.3, 0.3)
    poleward_interface_speed = jnp.clip(jax.random.uniform(key_list[8], (SEA_LAYER_COUNT, GRID_PARALLELS, GRID_MERIDIANS), jnp.float32, -0.3, 0.3) * level_of(key_list[8], (SEA_LAYER_COUNT, GRID_PARALLELS, GRID_MERIDIANS), ((1, 8), (2, 4)), -0.4, 0.0), -0.3, 0.3)
    sea_profile_indicator = set_ends((jax.random.randint(key_list[9], (GRID_PARALLELS, GRID_MERIDIANS), 0, 4) < 3).astype(jnp.int32), jax.random.fold_in(key_list[9], 1), 0, 1)
    return {"air_forcing_quantities": air_forcing_quantities, "segment_sea_subdomain": segment_sea_subdomain, "overlay_air_element": overlay_air_element, "overlay_sea_profile": overlay_sea_profile, "overlay_fraction_share": overlay_fraction_share, "thermal_deviation": thermal_deviation, "saltiness_deviation": saltiness_deviation, "zonal_interface_speed": zonal_interface_speed, "poleward_interface_speed": poleward_interface_speed, "sea_profile_indicator": sea_profile_indicator}


diffuse_rate = 0.12
mixing_base = 0.02
mixing_extra = 0.2
heat_factor = 0.5
fresh_factor = 0.5
stress_factor = 0.3


def density(temper_field, saline_field):
    return -0.2 * temper_field - 0.05 * temper_field * temper_field + 0.8 * saline_field + 0.03 * temper_field * saline_field


def face_flux(near_cells, far_cells, velocity, open_faces):
    return open_faces * (velocity * 0.5 * (near_cells + far_cells) - diffuse_rate * (far_cells - near_cells))


def vertical_change(scalar_quantities, ocean_mask):
    heavy = density(scalar_quantities[0], scalar_quantities[1])
    mixing = (mixing_base + mixing_extra * jax.nn.sigmoid(4.0 * (heavy[:-1] - heavy[1:]))) * ocean_mask
    gradients = mixing[None] * (scalar_quantities[:, 1:] - scalar_quantities[:, :-1])
    nothing = jnp.zeros_like(gradients[:, :1])
    return jnp.concatenate([gradients, nothing], axis=1) - jnp.concatenate([nothing, gradients], axis=1)


def ocean_step(scalar_quantities, east_eff, north_eff, ocean_mask, forcing):
    east_cells = jnp.roll(scalar_quantities, -1, axis=3)
    east_open = ocean_mask * jnp.roll(ocean_mask, -1, axis=1)
    east_flux = face_flux(scalar_quantities, east_cells, east_eff, east_open)
    north_cells = jnp.concatenate([scalar_quantities[:, :, 1:], scalar_quantities[:, :, -1:, ::-1]], axis=2)
    north_mask = jnp.concatenate([ocean_mask[1:], ocean_mask[-1:, ::-1]], axis=0)
    row_ids = lax.broadcasted_iota(jnp.int32, ocean_mask.shape, 0)
    active = (row_ids < ocean_mask.shape[0] - 1).astype(jnp.float32)
    north_flux = face_flux(scalar_quantities, north_cells, north_eff * active, ocean_mask * north_mask)
    west_flux = jnp.roll(east_flux, 1, axis=3)
    south_flux = jnp.concatenate([jnp.zeros_like(north_flux[:, :, :1]), north_flux[:, :, :-1]], axis=2)
    change = -(east_flux - west_flux) - (north_flux - south_flux) + vertical_change(scalar_quantities, ocean_mask)
    change = change.at[:, 0].add(forcing)
    return scalar_quantities + ocean_mask * change


def reference(air_forcing_quantities, segment_sea_subdomain, overlay_air_element, overlay_sea_profile, overlay_fraction_share, thermal_deviation, saltiness_deviation, zonal_interface_speed, poleward_interface_speed, sea_profile_indicator):
    blocks = segment_sea_subdomain.shape[0]
    owner = lax.broadcasted_iota(jnp.int32, (blocks, 1), 0) // BLK_DEV
    atm_index = (owner * A_DEV + overlay_air_element).astype(jnp.int32)
    lat_tile = segment_sea_subdomain % N_GY
    lon_tile = segment_sea_subdomain // N_GY
    ocean_index = ((lat_tile * OY + overlay_sea_profile // OX) * GRID_MERIDIANS + lon_tile * OX + overlay_sea_profile % OX).astype(jnp.int32)
    weighted = air_forcing_quantities[:, atm_index] * overlay_fraction_share[None]
    remapped = jnp.zeros((FIELDS, GRID_PARALLELS * GRID_MERIDIANS), jnp.float32).at[:, ocean_index.reshape(-1)].add(weighted.reshape(FIELDS, -1))
    remapped = remapped.reshape(FIELDS, GRID_PARALLELS, GRID_MERIDIANS)
    heat_flux = remapped[0] + remapped[1] + remapped[2] + remapped[3]
    fresh_flux = remapped[5] - remapped[4]
    east_eff = zonal_interface_speed.at[0].add(stress_factor * remapped[6])
    north_eff = poleward_interface_speed.at[0].add(stress_factor * remapped[7])
    ocean_mask = sea_profile_indicator.astype(jnp.float32)
    forcing = jnp.stack([heat_factor * heat_flux, fresh_factor * fresh_flux])
    scalar_quantities = jnp.stack([thermal_deviation, saltiness_deviation])
    for step_number in range(2):
        scalar_quantities = ocean_step(scalar_quantities, east_eff, north_eff, ocean_mask, forcing)
    surface = jnp.stack([scalar_quantities[0, 0], scalar_quantities[1, 0], density(scalar_quantities[0, 0], scalar_quantities[1, 0]), east_eff[0]]) * ocean_mask
    picked = surface.reshape(4, -1)[:, ocean_index] * overlay_fraction_share[None]
    back_fields = jnp.zeros((4, A_CELLS), jnp.float32).at[:, atm_index.reshape(-1)].add(picked.reshape(4, -1))
    return scalar_quantities[0], scalar_quantities[1], back_fields
```

```python
import functools

import jax
import jax.numpy as jnp
from jax import lax
from jax.experimental import pallas as pl
from jax.experimental.pallas import tpu as pltpu
from jax.sharding import PartitionSpec as P

diffuse_rate = 0.12
mixing_base = 0.02
mixing_extra = 0.2
heat_factor = 0.5
fresh_factor = 0.5
stress_factor = 0.3

LANES = 128
GROUP = 8
PAIR = 2
VMEM_BYTES = 48 * 1024 * 1024
CONTRACT_LAST = (((1,), (1,)), ((), ()))

SMEM = pl.BlockSpec(memory_space=pltpu.SMEM)
VMEM = pl.BlockSpec(memory_space=pltpu.VMEM)


def density(temper_field, saline_field):
    return (
        -0.2 * temper_field
        - 0.05 * temper_field * temper_field
        + 0.8 * saline_field
        + 0.03 * temper_field * saline_field
    )


def face_flux(near_cells, far_cells, velocity, open_faces):
    return open_faces * (
        velocity * 0.5 * (near_cells + far_cells) - diffuse_rate * (far_cells - near_cells)
    )


def two_terms(values):
    high = values.astype(jnp.bfloat16).astype(jnp.float32)
    return high, values - high


def one_hot(places, count):
    rows = lax.broadcasted_iota(jnp.int32, (count, places.shape[1]), 0)
    return jnp.where(rows == places, 1.0, 0.0).astype(jnp.bfloat16)


def spread(rows_of, terms, count):
    rows = lax.broadcasted_iota(jnp.int32, (count, rows_of.shape[1]), 0)
    hit = rows == rows_of
    return jnp.concatenate([jnp.where(hit, term, 0.0) for term in terms], axis=0).astype(
        jnp.bfloat16
    )


def picked_rows(rows_of, table, fields, count):
    rows = lax.broadcasted_iota(jnp.int32, (count, rows_of.shape[1]), 0)
    hit = rows == rows_of
    return [
        jnp.sum(
            jnp.where(hit, table[field * count : (field + 1) * count], 0.0), axis=0, keepdims=True
        )
        for field in range(fields)
    ]


def send_kernel(
    capacity, subdomain, table, element, profile, share, out, home, tally, split_table
):
    devices = tally.shape[0]
    blocks = element.shape[0]
    high_rows = table.shape[0] // 4

    def clear(i, carry):
        tally[i] = 0
        return carry

    lax.fori_loop(0, devices, clear, 0)
    out[...] = jnp.full(out.shape, -1.0, jnp.float32)
    high, low = two_terms(table[...])
    split_table[:, :LANES] = high.astype(jnp.bfloat16)
    split_table[:, LANES:] = low.astype(jnp.bfloat16)

    def group(g, carry):
        base = pl.multiple_of(g * GROUP, GROUP)
        cells = element[pl.ds(base, GROUP), :]
        near = cells & (LANES - 1)
        far = cells >> 7
        address = profile[pl.ds(base, GROUP), :].astype(jnp.float32)
        weight = share[pl.ds(base, GROUP), :]
        for first in range(0, GROUP, PAIR):
            names = range(first, first + PAIR)
            hot = jnp.concatenate([one_hot(near[b : b + 1], LANES) for b in names], axis=1)
            found = jnp.dot(
                split_table[...],
                jnp.concatenate([hot, hot], axis=0),
                preferred_element_type=jnp.float32,
            )
            far_row = jnp.concatenate([far[b : b + 1] for b in names], axis=1)
            values = picked_rows(far_row, found, 4, high_rows)
            for turn, b in enumerate(names):
                tile = subdomain[base + b]
                place = tally[tile]
                tally[tile] = place + 1
                home[base + b] = tile * (4 * capacity) + place
                row = tile * (5 * capacity) + place
                for field in range(4):
                    out[pl.ds(row + field * capacity, 1), :] = (
                        values[field][:, turn * LANES : (turn + 1) * LANES] * weight[b : b + 1]
                    )
                out[pl.ds(row + 4 * capacity, 1), :] = address[b : b + 1]
        return carry

    lax.fori_loop(0, blocks // GROUP, group, 0)


def gather_kernel_params(flops):
    return dict(
        compiler_params=pltpu.CompilerParams(vmem_limit_bytes=VMEM_BYTES),
        cost_estimate=pl.CostEstimate(flops=flops, bytes_accessed=4_000_000, transcendentals=0),
    )


def land_kernel(capacity, parallels, meridians, counts, arrived, remapped, places, slots, values, total):
    sources = counts.shape[0]
    last = slots.shape[0] - 1
    shift = meridians.bit_length() - 1
    places[...] = jnp.full(places.shape, -1.0, jnp.float32)
    total[...] = jnp.zeros(total.shape, jnp.float32)

    def from_source(source, count):
        def slot(place, count):
            row = source * (5 * capacity) + place
            for field in range(4):
                values[field, pl.ds(count, 1), :] = arrived[pl.ds(row + field * capacity, 1), :]
            places[pl.ds(count, 1), :] = arrived[pl.ds(row + 4 * capacity, 1), :]
            slots[count] = source * (4 * capacity) + place
            return count + 1

        return lax.fori_loop(0, counts[source], slot, count)

    filled = lax.fori_loop(0, sources, from_source, 0)
    slots[last] = filled

    def group(g, carry):
        base = pl.multiple_of(g * GROUP, GROUP)
        address = places[pl.ds(base, GROUP), :].astype(jnp.int32)
        row = address >> shift
        column = address & (meridians - 1)
        split = [two_terms(values[field, pl.ds(base, GROUP), :]) for field in range(4)]
        terms = [split[field][term] for term in range(2) for field in range(4)]
        sums = None
        for first in range(0, GROUP, PAIR):
            names = range(first, first + PAIR)
            left = jnp.concatenate(
                [
                    spread(row[b : b + 1], [term[b : b + 1] for term in terms], parallels)
                    for b in names
                ],
                axis=1,
            )
            right = jnp.concatenate([one_hot(column[b : b + 1], meridians) for b in names], axis=1)
            part = lax.dot_general(
                left, right, CONTRACT_LAST, preferred_element_type=jnp.float32
            )
            sums = part if sums is None else sums + part
        total[...] += sums
        return carry

    lax.fori_loop(0, (filled + GROUP - 1) // GROUP, group, 0)
    half = 4 * parallels
    remapped[...] = total[:half] + total[half:]


def pick_kernel(capacity, parallels, meridians, slots, surface, places, out, split_table):
    last = slots.shape[0] - 1
    half = 4 * parallels
    shift = meridians.bit_length() - 1
    filled = slots[last]
    high, low = two_terms(surface[...])
    split_table[:half] = high.astype(jnp.bfloat16)
    split_table[half:] = low.astype(jnp.bfloat16)
    out[...] = jnp.zeros(out.shape, jnp.float32)

    def group(g, carry):
        base = pl.multiple_of(g * GROUP, GROUP)
        address = places[pl.ds(base, GROUP), :].astype(jnp.int32)
        row = address >> shift
        column = address & (meridians - 1)
        for first in range(0, GROUP, PAIR):
            names = range(first, first + PAIR)
            hot = jnp.concatenate([one_hot(column[b : b + 1], meridians) for b in names], axis=1)
            found = jnp.dot(split_table[...], hot, preferred_element_type=jnp.float32)
            found = found[:half] + found[half:]
            wide_row = jnp.concatenate([row[b : b + 1] for b in names], axis=1)
            values = picked_rows(wide_row, found, 4, parallels)
            for turn, b in enumerate(names):

                @pl.when(base + b < filled)
                def _():
                    target = slots[base + b]
                    for field in range(4):
                        out[pl.ds(target + field * capacity, 1), :] = values[field][
                            :, turn * LANES : (turn + 1) * LANES
                        ]

        return carry

    lax.fori_loop(0, (filled + GROUP - 1) // GROUP, group, 0)


def back_kernel(capacity, home, returned, element, share, out, total):
    blocks = element.shape[0]
    high_rows = out.shape[0] // 4
    total[...] = jnp.zeros(total.shape, jnp.float32)

    def group(g, carry):
        base = pl.multiple_of(g * GROUP, GROUP)
        cells = element[pl.ds(base, GROUP), :]
        near = cells & (LANES - 1)
        far = cells >> 7
        weight = share[pl.ds(base, GROUP), :]
        sums = None
        for first in range(0, GROUP, PAIR):
            names = range(first, first + PAIR)
            lefts = []
            for b in names:
                row = home[base + b]
                split = [
                    two_terms(returned[pl.ds(row + field * capacity, 1), :] * weight[b : b + 1])
                    for field in range(4)
                ]
                terms = [split[field][term] for term in range(2) for field in range(4)]
                lefts.append(spread(far[b : b + 1], terms, high_rows))
            left = jnp.concatenate(lefts, axis=1)
            right = jnp.concatenate([one_hot(near[b : b + 1], LANES) for b in names], axis=1)
            part = lax.dot_general(
                left, right, CONTRACT_LAST, preferred_element_type=jnp.float32
            )
            sums = part if sums is None else sums + part
        total[...] += sums
        return carry

    lax.fori_loop(0, blocks // GROUP, group, 0)
    half = 4 * high_rows
    out[...] = total[:half] + total[half:]


def ocean_kernel(
    top,
    temper,
    saline,
    east,
    north,
    ocean_mask,
    sides,
    ends,
    remapped,
    remap_sides,
    remap_ends,
    temper_out,
    saline_out,
    surface,
    first_t,
    first_s,
    second_t,
    second_s,
    east_all,
    north_all,
    remap_all,
    opens,
):
    depth, rows, columns = temper.shape
    all_rows, all_columns = first_t.shape[1:]

    def fill(target, source, side, end):
        target[:, :rows, :columns] = source[...]
        target[:, :rows, columns:] = side
        target[:, rows:, :] = end

    for turn, (target, source) in enumerate(
        ((first_t, temper), (first_s, saline), (east_all, east), (north_all, north))
    ):
        part = slice(turn * depth, (turn + 1) * depth)
        fill(target, source, sides[part], ends[part])
    fill(remap_all, remapped, remap_sides[...], remap_ends[...])
    opens[0, :rows, :columns] = ocean_mask[...].astype(jnp.float32)
    opens[0, :rows, columns:] = sides[4 * depth]
    opens[0, rows:, :] = ends[4 * depth]

    def next_column(x):
        return pltpu.roll(x, all_columns - 1, axis=1)

    def next_row(x):
        return pltpu.roll(x, all_rows - 1, axis=0)

    here = opens[0]
    opens[1] = here * next_column(here)
    opens[2] = here * next_row(here)
    row_ids = lax.broadcasted_iota(jnp.int32, (all_rows, all_columns), 0)
    opens[3] = jnp.where((row_ids == rows - 1) & (top[0] == 1), 0.0, 1.0)
    east_all[0] = east_all[0] + stress_factor * remap_all[2]
    north_all[0] = north_all[0] + stress_factor * remap_all[3]
    remap_all[0] = heat_factor * remap_all[0]
    remap_all[1] = fresh_factor * remap_all[1]

    def step(source_t, source_s, keep):
        def level(k, carry):
            gain_t, gain_s = carry
            below = jnp.minimum(k + 1, depth - 1)
            t, s = source_t[k], source_s[k]
            t_below, s_below = source_t[below], source_s[below]
            mask = opens[0]
            mixing = (
                mixing_base
                + mixing_extra
                * jax.nn.sigmoid(4.0 * (density(t, s) - density(t_below, s_below)))
            ) * mask
            east_speed = east_all[k]
            north_speed = north_all[k] * opens[3]
            new_gains = []
            for x, x_below, gain, target, forcing in (
                (t, t_below, gain_t, 0, 0),
                (s, s_below, gain_s, 1, 1),
            ):
                gradient = mixing * (x_below - x)
                east_flux = face_flux(x, next_column(x), east_speed, opens[1])
                north_flux = face_flux(x, next_row(x), north_speed, opens[2])
                change = (
                    -(east_flux - pltpu.roll(east_flux, 1, axis=1))
                    - (north_flux - pltpu.roll(north_flux, 1, axis=0))
                    + (gradient - gain)
                )
                change = change + jnp.where(k == 0, remap_all[forcing], 0.0)
                keep(target, k, x + mask * change)
                new_gains.append(gradient)
            return tuple(new_gains)

        nothing = jnp.zeros((all_rows, all_columns), jnp.float32)
        lax.fori_loop(0, depth, level, (nothing, nothing))

    def keep_first(target, k, value):
        (second_t, second_s)[target][k] = value

    def keep_last(target, k, value):
        (temper_out, saline_out)[target][k] = value[:rows, :columns]

    step(first_t, first_s, keep_first)
    step(second_t, second_s, keep_last)

    mask = opens[0, :rows, :columns]
    t, s = temper_out[0], saline_out[0]
    surface[0] = t * mask
    surface[1] = s * mask
    surface[2] = density(t, s) * mask
    surface[3] = east_all[0, :rows, :columns] * mask


def halo(parts, east_at, north_at):
    rows, columns = parts[0].shape[1:]
    count_gx, count_gy = lax.axis_size("gx"), lax.axis_size("gy")
    head = jnp.concatenate([x[:, :, :2] for x in parts], axis=0)
    tail = jnp.concatenate([x[:, :, -2:] for x in parts], axis=0)
    channels = head.shape[0]
    from_west = lax.ppermute(tail, "gx", [(i, (i + 1) % count_gx) for i in range(count_gx)])
    from_east = lax.ppermute(head, "gx", [((i + 1) % count_gx, i) for i in range(count_gx)])
    sides = jnp.concatenate(
        [from_east, jnp.zeros((channels, rows, LANES - 4), jnp.float32), from_west], axis=2
    )
    low = jnp.concatenate(
        [jnp.concatenate([x[:, :2] for x in parts], axis=0), sides[:, :2]], axis=2
    )
    high = jnp.concatenate(
        [jnp.concatenate([x[:, -2:] for x in parts], axis=0), sides[:, -2:]], axis=2
    )
    from_south = lax.ppermute(high, "gy", [(i, i + 1) for i in range(count_gy - 1)])
    from_north = lax.ppermute(low, "gy", [(i + 1, i) for i in range(count_gy - 1)])
    folded = lax.ppermute(high, "gx", [(i, count_gx - 1 - i) for i in range(count_gx)])
    folded = jnp.concatenate(
        [folded[:, ::-1, columns - 1 :: -1], folded[:, ::-1, : columns - 1 : -1]], axis=2
    )
    e0, e1 = east_at
    n0, n1 = north_at
    east_part = -jnp.concatenate([folded[e0:e1, :, 1:], folded[e0:e1, :, :1]], axis=2)
    north_part = -jnp.concatenate([folded[n0:n1, 1:], folded[n0:n1, :1]], axis=1)
    folded = jnp.concatenate([folded[:e0], east_part, north_part, folded[n1:]], axis=0)
    is_top = lax.axis_index("gy") == count_gy - 1
    above = jnp.where(is_top, folded, from_north)
    ends = jnp.concatenate(
        [above, jnp.zeros((channels, 4, columns + LANES), jnp.float32), from_south], axis=1
    )
    return sides, ends


def body(
    air_forcing_quantities,
    segment_sea_subdomain,
    overlay_air_element,
    overlay_sea_profile,
    overlay_fraction_share,
    thermal_deviation,
    saltiness_deviation,
    zonal_interface_speed,
    poleward_interface_speed,
    sea_profile_indicator,
):
    devices = lax.axis_size("gx") * lax.axis_size("gy")
    blocks = segment_sea_subdomain.shape[0]
    atm_cells = air_forcing_quantities.shape[1]
    depth, parallels, meridians = thermal_deviation.shape
    capacity = max(2, 2 * blocks // devices)
    slot_count = devices * capacity
    f32 = jnp.float32
    air = air_forcing_quantities
    table = jnp.stack([air[0] + air[1] + air[2] + air[3], air[5] - air[4], air[6], air[7]])
    table = table.reshape(4 * atm_cells // LANES, LANES)

    outgoing, home = pl.pallas_call(
        functools.partial(send_kernel, capacity),
        out_shape=(
            jax.ShapeDtypeStruct((slot_count * 5, LANES), f32),
            jax.ShapeDtypeStruct((blocks,), jnp.int32),
        ),
        in_specs=[SMEM, VMEM, VMEM, VMEM, VMEM],
        out_specs=(VMEM, SMEM),
        scratch_shapes=[
            pltpu.SMEM((devices,), jnp.int32),
            pltpu.VMEM((table.shape[0], 2 * LANES), jnp.bfloat16),
        ],
        **gather_kernel_params(10**9),
    )(
        segment_sea_subdomain.reshape(blocks),
        table,
        overlay_air_element,
        overlay_sea_profile,
        overlay_fraction_share,
    )
    arrived = lax.all_to_all(outgoing, ("gx", "gy"), split_axis=0, concat_axis=0, tiled=True)

    ocean_mask = sea_profile_indicator.astype(f32)
    sides, ends = halo(
        [
            thermal_deviation,
            saltiness_deviation,
            zonal_interface_speed,
            poleward_interface_speed,
            ocean_mask[None],
        ],
        (2 * depth, 3 * depth),
        (3 * depth, 4 * depth),
    )

    counts = jnp.sum(
        (arrived.reshape(devices, 5, capacity, LANES)[:, 4, :, 0] >= 0).astype(jnp.int32), axis=1
    )
    remapped, places, slots = pl.pallas_call(
        functools.partial(land_kernel, capacity, parallels, meridians),
        out_shape=(
            jax.ShapeDtypeStruct((4 * parallels, meridians), f32),
            jax.ShapeDtypeStruct((slot_count + GROUP, LANES), f32),
            jax.ShapeDtypeStruct((slot_count + 1,), jnp.int32),
        ),
        in_specs=[SMEM, VMEM],
        out_specs=(VMEM, VMEM, SMEM),
        scratch_shapes=[
            pltpu.VMEM((4, slot_count + GROUP, LANES), f32),
            pltpu.VMEM((8 * parallels, meridians), f32),
        ],
        **gather_kernel_params(2 * 10**10),
    )(counts, arrived)
    remapped = remapped.reshape(4, parallels, meridians)
    remap_sides, remap_ends = halo([remapped], (2, 3), (3, 4))

    top = (lax.axis_index("gy") == lax.axis_size("gy") - 1).astype(jnp.int32).reshape(1)
    wide = (parallels + 8, meridians + LANES)
    cube = jax.ShapeDtypeStruct((depth, parallels, meridians), f32)
    temper, saline, surface = pl.pallas_call(
        ocean_kernel,
        out_shape=(cube, cube, jax.ShapeDtypeStruct((4, parallels, meridians), f32)),
        in_specs=[SMEM] + [VMEM] * 10,
        out_specs=(VMEM, VMEM, VMEM),
        scratch_shapes=[pltpu.VMEM((depth,) + wide, f32)] * 6 + [pltpu.VMEM((4,) + wide, f32)] * 2,
        **gather_kernel_params(10**9),
    )(
        top,
        thermal_deviation,
        saltiness_deviation,
        zonal_interface_speed,
        poleward_interface_speed,
        sea_profile_indicator,
        sides,
        ends,
        remapped,
        remap_sides,
        remap_ends,
    )

    picked = pl.pallas_call(
        functools.partial(pick_kernel, capacity, parallels, meridians),
        out_shape=jax.ShapeDtypeStruct((slot_count * 4, LANES), f32),
        in_specs=[SMEM, VMEM, VMEM],
        out_specs=VMEM,
        scratch_shapes=[pltpu.VMEM((8 * parallels, meridians), jnp.bfloat16)],
        **gather_kernel_params(2 * 10**10),
    )(slots, surface.reshape(4 * parallels, meridians), places)
    returned = lax.all_to_all(picked, ("gx", "gy"), split_axis=0, concat_axis=0, tiled=True)
    back_fields = pl.pallas_call(
        functools.partial(back_kernel, capacity),
        out_shape=jax.ShapeDtypeStruct((4 * atm_cells // LANES, LANES), f32),
        in_specs=[SMEM, VMEM, VMEM, VMEM],
        out_specs=VMEM,
        scratch_shapes=[pltpu.VMEM((8 * atm_cells // LANES, LANES), f32)],
        **gather_kernel_params(2 * 10**9),
    )(home, returned, overlay_air_element, overlay_fraction_share)
    return temper, saline, back_fields.reshape(4, atm_cells)


def solution(mesh):
    return jax.shard_map(
        body,
        mesh=mesh,
        in_specs=(
            P(None, ("gx", "gy")),
            P(("gx", "gy"), None),
            P(("gx", "gy"), None),
            P(("gx", "gy"), None),
            P(("gx", "gy"), None),
            P(None, "gy", "gx"),
            P(None, "gy", "gx"),
            P(None, "gy", "gx"),
            P(None, "gy", "gx"),
            P("gy", "gx"),
        ),
        out_specs=(P(None, "gy", "gx"), P(None, "gy", "gx"), P(None, ("gx", "gy"))),
        check_vma=False,
    )
```

```python
import functools

import jax
import jax.numpy as jnp
from jax import lax
from jax.experimental import pallas as pl
from jax.experimental.pallas import tpu as pltpu
from jax.sharding import PartitionSpec as P

diffuse_rate = 0.12
mixing_base = 0.02
mixing_extra = 0.2
heat_factor = 0.5
fresh_factor = 0.5
stress_factor = 0.3

LANES = 128
GROUP = 8
HALF = 256
PAIR = 2
VMEM_BYTES = 48 * 1024 * 1024
CONTRACT_LAST = (((1,), (1,)), ((), ()))

SMEM = pl.BlockSpec(memory_space=pltpu.SMEM)
VMEM = pl.BlockSpec(memory_space=pltpu.VMEM)


def density(temper_field, saline_field):
    return (
        -0.2 * temper_field
        - 0.05 * temper_field * temper_field
        + 0.8 * saline_field
        + 0.03 * temper_field * saline_field
    )


def face_flux(near_cells, far_cells, velocity, open_faces):
    return open_faces * (
        velocity * 0.5 * (near_cells + far_cells) - diffuse_rate * (far_cells - near_cells)
    )


def two_terms(values):
    high = values.astype(jnp.bfloat16)
    return high, (values - high.astype(jnp.float32)).astype(jnp.bfloat16)


def narrow(places):
    return places.astype(jnp.float32).astype(jnp.bfloat16)


def number_rows(numbers):
    numbers[...] = narrow(lax.broadcasted_iota(jnp.int32, numbers.shape, 0))


def one_hot(places, numbers):
    return jnp.where(numbers == places, jnp.bfloat16(1), jnp.bfloat16(0))


def spread(rows_of, terms, numbers):
    hit = numbers == rows_of
    return jnp.concatenate([jnp.where(hit, term, jnp.bfloat16(0)) for term in terms], axis=0)


def halves_of(column, meridians):
    return [
        narrow(jnp.where(column // HALF == part, column % HALF, -1))
        for part in range(meridians // HALF)
    ]


def wide_one_hot(parts, b, numbers):
    return jnp.concatenate([one_hot(part[b : b + 1], numbers) for part in parts], axis=0)


def picked_rows(rows_of, table, fields, count):
    rows = lax.broadcasted_iota(jnp.int32, (count, rows_of.shape[1]), 0)
    hit = rows == rows_of
    return [
        jnp.sum(
            jnp.where(hit, table[field * count : (field + 1) * count], 0.0), axis=0, keepdims=True
        )
        for field in range(fields)
    ]


def send_kernel(
    capacity, subdomain, table, element, profile, share, out, home, tally, split_table, numbers
):
    devices = tally.shape[0]
    blocks = element.shape[0]
    high_rows = table.shape[0] // 4

    def clear(i, carry):
        tally[i] = 0
        return carry

    lax.fori_loop(0, devices, clear, 0)
    number_rows(numbers)
    out[...] = jnp.full(out.shape, -1.0, jnp.float32)
    high, low = two_terms(table[...])
    split_table[:, :LANES] = high
    split_table[:, LANES:] = low

    def group(g, carry):
        base = pl.multiple_of(g * GROUP, GROUP)
        cells = element[pl.ds(base, GROUP), :]
        near = narrow(cells & (LANES - 1))
        far = cells >> 7
        address = profile[pl.ds(base, GROUP), :].astype(jnp.float32)
        weight = share[pl.ds(base, GROUP), :]
        for first in range(0, GROUP, PAIR):
            names = range(first, first + PAIR)
            hot = jnp.concatenate([one_hot(near[b : b + 1], numbers[...]) for b in names], axis=1)
            found = jnp.dot(
                split_table[...],
                jnp.concatenate([hot, hot], axis=0),
                preferred_element_type=jnp.float32,
            )
            far_row = jnp.concatenate([far[b : b + 1] for b in names], axis=1)
            values = picked_rows(far_row, found, 4, high_rows)
            for turn, b in enumerate(names):
                tile = subdomain[base + b]
                place = tally[tile]
                tally[tile] = place + 1
                home[base + b] = tile * (4 * capacity) + place
                row = tile * (5 * capacity) + place
                for field in range(4):
                    out[pl.ds(row + field * capacity, 1), :] = (
                        values[field][:, turn * LANES : (turn + 1) * LANES] * weight[b : b + 1]
                    )
                out[pl.ds(row + 4 * capacity, 1), :] = address[b : b + 1]
        return carry

    lax.fori_loop(0, blocks // GROUP, group, 0)


def gather_kernel_params(flops):
    return dict(
        compiler_params=pltpu.CompilerParams(vmem_limit_bytes=VMEM_BYTES),
        cost_estimate=pl.CostEstimate(flops=flops, bytes_accessed=4_000_000, transcendentals=0),
    )


def land_kernel(
    capacity,
    parallels,
    meridians,
    counts,
    arrived,
    remapped,
    places,
    slots,
    values,
    total,
    numbers,
):
    sources = counts.shape[0]
    last = slots.shape[0] - 1
    shift = meridians.bit_length() - 1
    places[...] = jnp.full(places.shape, -1.0, jnp.float32)
    total[...] = jnp.zeros(total.shape, jnp.float32)

    def from_source(source, count):
        def slot(place, count):
            row = source * (5 * capacity) + place
            for field in range(4):
                values[field, pl.ds(count, 1), :] = arrived[pl.ds(row + field * capacity, 1), :]
            places[pl.ds(count, 1), :] = arrived[pl.ds(row + 4 * capacity, 1), :]
            slots[count] = source * (4 * capacity) + place
            return count + 1

        return lax.fori_loop(0, counts[source], slot, count)

    filled = lax.fori_loop(0, sources, from_source, 0)
    slots[last] = filled
    for extra in range(GROUP):
        slots[filled + extra] = sources * (4 * capacity)
    number_rows(numbers)

    def group(g, carry):
        base = pl.multiple_of(g * GROUP, GROUP)
        address = places[pl.ds(base, GROUP), :].astype(jnp.int32)
        row = narrow(address >> shift)
        column = halves_of(address & (meridians - 1), meridians)
        split = [two_terms(values[field, pl.ds(base, GROUP), :]) for field in range(4)]
        terms = [split[field][term] for term in range(2) for field in range(4)]
        sums = None
        for first in range(0, GROUP, PAIR):
            names = range(first, first + PAIR)
            left = jnp.concatenate(
                [
                    spread(row[b : b + 1], [term[b : b + 1] for term in terms], numbers[:parallels])
                    for b in names
                ],
                axis=1,
            )
            right = jnp.concatenate([wide_one_hot(column, b, numbers[...]) for b in names], axis=1)
            part = lax.dot_general(
                left, right, CONTRACT_LAST, preferred_element_type=jnp.float32
            )
            sums = part if sums is None else sums + part
        total[...] += sums
        return carry

    lax.fori_loop(0, (filled + GROUP - 1) // GROUP, group, 0)
    half = 4 * parallels
    remapped[...] = total[:half] + total[half:]


def pick_kernel(capacity, parallels, meridians, slots, surface, places, out, split_table, numbers, found_rows):
    last = slots.shape[0] - 1
    half = 4 * parallels
    shift = meridians.bit_length() - 1
    filled = slots[last]
    high, low = two_terms(surface[...])
    split_table[:half] = high
    split_table[half:] = low
    found_rows[...] = jnp.zeros(found_rows.shape, jnp.float32)
    number_rows(numbers)

    def group(g, carry):
        base = pl.multiple_of(g * GROUP, GROUP)
        address = places[pl.ds(base, GROUP), :].astype(jnp.int32)
        row = address >> shift
        column = halves_of(address & (meridians - 1), meridians)
        for first in range(0, GROUP, PAIR):
            names = range(first, first + PAIR)
            hot = jnp.concatenate([wide_one_hot(column, b, numbers[...]) for b in names], axis=1)
            found = jnp.dot(split_table[...], hot, preferred_element_type=jnp.float32)
            found = found[:half] + found[half:]
            wide_row = jnp.concatenate([row[b : b + 1] for b in names], axis=1)
            values = picked_rows(wide_row, found, 4, parallels)
            for turn, b in enumerate(names):
                target = slots[base + b]
                for field in range(4):
                    found_rows[pl.ds(target + field * capacity, 1), :] = values[field][
                        :, turn * LANES : (turn + 1) * LANES
                    ]
        return carry

    lax.fori_loop(0, (filled + GROUP - 1) // GROUP, group, 0)
    out[...] = found_rows[: out.shape[0]]


def back_kernel(capacity, home, returned, element, share, out, total, numbers):
    blocks = element.shape[0]
    high_rows = out.shape[0] // 4
    total[...] = jnp.zeros(total.shape, jnp.float32)
    number_rows(numbers)

    def group(g, carry):
        base = pl.multiple_of(g * GROUP, GROUP)
        cells = element[pl.ds(base, GROUP), :]
        near = narrow(cells & (LANES - 1))
        far = narrow(cells >> 7)
        weight = share[pl.ds(base, GROUP), :]
        sums = None
        for first in range(0, GROUP, PAIR):
            names = range(first, first + PAIR)
            lefts = []
            for b in names:
                row = home[base + b]
                split = [
                    two_terms(returned[pl.ds(row + field * capacity, 1), :] * weight[b : b + 1])
                    for field in range(4)
                ]
                terms = [split[field][term] for term in range(2) for field in range(4)]
                lefts.append(spread(far[b : b + 1], terms, numbers[:high_rows]))
            left = jnp.concatenate(lefts, axis=1)
            right = jnp.concatenate([one_hot(near[b : b + 1], numbers[...]) for b in names], axis=1)
            part = lax.dot_general(
                left, right, CONTRACT_LAST, preferred_element_type=jnp.float32
            )
            sums = part if sums is None else sums + part
        total[...] += sums
        return carry

    lax.fori_loop(0, blocks // GROUP, group, 0)
    half = 4 * high_rows
    out[...] = total[:half] + total[half:]


def next_column(x):
    return pltpu.roll(x, x.shape[1] - 1, axis=1)


def next_row(x):
    return pltpu.roll(x, x.shape[0] - 1, axis=0)


def fill_wide(target, source, side, end):
    rows, columns = source.shape[1:]
    target[:, :rows, :columns] = source[...]
    target[:, :rows, columns:] = side
    target[:, rows:, :] = end


def fill_opens(opens, top, ocean_mask, side, end):
    rows, columns = ocean_mask.shape
    opens[0, :rows, :columns] = ocean_mask[...].astype(jnp.float32)
    opens[0, :rows, columns:] = side
    opens[0, rows:, :] = end
    here = opens[0]
    opens[1] = here * next_column(here)
    opens[2] = here * next_row(here)
    row_ids = lax.broadcasted_iota(jnp.int32, here.shape, 0)
    opens[3] = jnp.where((row_ids == rows - 1) & (top[0] == 1), 0.0, 1.0)


def mixing_at(t, s, t_below, s_below, mask):
    return (
        mixing_base
        + mixing_extra * jax.nn.sigmoid(4.0 * (density(t, s) - density(t_below, s_below)))
    ) * mask


def step(source, speeds, opens, first, stop, floor, keep, forcing=None):
    source_t, source_s = source
    east_all, north_all = speeds

    def level(k, carry):
        below = jnp.minimum(k + 1, floor)
        t, s = source_t[k], source_s[k]
        t_below, s_below = source_t[below], source_s[below]
        mask = opens[0]
        mixing = mixing_at(t, s, t_below, s_below, mask)
        east_speed = east_all[k]
        north_speed = north_all[k] * opens[3]
        new_gains = []
        for turn, (x, x_below) in enumerate(((t, t_below), (s, s_below))):
            gradient = mixing * (x_below - x)
            east_flux = face_flux(x, next_column(x), east_speed, opens[1])
            north_flux = face_flux(x, next_row(x), north_speed, opens[2])
            change = (
                -(east_flux - pltpu.roll(east_flux, 1, axis=1))
                - (north_flux - pltpu.roll(north_flux, 1, axis=0))
                + (gradient - carry[turn])
            )
            if forcing is not None:
                change = change + jnp.where(k == 0, forcing[turn], 0.0)
            keep(turn, k, x + mask * change)
            new_gains.append(gradient)
        return tuple(new_gains)

    if first == 0:
        nothing = jnp.zeros(source_t.shape[1:], jnp.float32)
        gains = (nothing, nothing)
    else:
        t, s, t_below, s_below = (x[k] for k in (first - 1, first) for x in source)
        mixing = mixing_at(t, s, t_below, s_below, opens[0])
        gains = (mixing * (t_below - t), mixing * (s_below - s))
    lax.fori_loop(first, stop, level, gains)


def turned(x):
    back = LANES - 1 - lax.broadcasted_iota(jnp.int32, (x.shape[0], LANES), 1)
    pieces = [
        jnp.take_along_axis(x[:, at : at + LANES], back, axis=1, mode="promise_in_bounds")
        for at in range(0, x.shape[1], LANES)
    ]
    return jnp.concatenate(pieces[-2::-1] + pieces[-1:], axis=1)


def near_kernel(
    depth,
    top,
    temper,
    saline,
    east,
    north,
    ocean_mask,
    sides,
    ends,
    remapped,
    remap_sides,
    from_north,
    from_south,
    folded,
    temper_out,
    saline_out,
    surface,
    first_t,
    first_s,
    second_t,
    second_s,
    east_all,
    north_all,
    remap_all,
    opens,
):
    levels, rows, columns = temper.shape
    for turn, (target, source) in enumerate(
        ((first_t, temper), (first_s, saline), (east_all, east), (north_all, north))
    ):
        part = slice(turn * depth, turn * depth + levels)
        fill_wide(target, source, sides[part], ends[part])
    fill_opens(opens, top, ocean_mask, sides[4 * depth], ends[4 * depth])
    upper = lax.broadcasted_iota(jnp.int32, (8, columns + LANES), 0)
    remap_all[:, :rows, :columns] = remapped[...]
    remap_all[:, :rows, columns:] = remap_sides[...]
    for field in range(4):
        across = turned(folded[field])
        if field == 2:
            across = -next_column(across)
        last_row, row_before = across[7:8], across[6:7]
        if field == 3:
            last_row, row_before = -row_before, -row_before
        across = jnp.where(upper == 0, last_row, row_before)
        above = jnp.where(top[0] == 1, across, from_north[field])
        remap_all[field, rows:, :] = jnp.where(upper < 4, above, from_south[field])
    east_all[0] = east_all[0] + stress_factor * remap_all[2]
    north_all[0] = north_all[0] + stress_factor * remap_all[3]
    remap_all[0] = heat_factor * remap_all[0]
    remap_all[1] = fresh_factor * remap_all[1]
    forcing = (remap_all[0], remap_all[1])

    def keep_first(target, k, value):
        (second_t, second_s)[target][k] = value

    def keep_last(target, k, value):
        (temper_out, saline_out)[target][k] = value[:rows, :columns]

    speeds = (east_all, north_all)
    step((first_t, first_s), speeds, opens, 0, levels - 1, levels - 1, keep_first, forcing)
    step((second_t, second_s), speeds, opens, 0, levels - 2, levels - 1, keep_last, forcing)
    mask = opens[0, :rows, :columns]
    t, s = temper_out[0], saline_out[0]
    surface[0] = t * mask
    surface[1] = s * mask
    surface[2] = density(t, s) * mask
    surface[3] = east_all[0, :rows, :columns] * mask


def deep_kernel(
    top,
    temper,
    saline,
    east,
    north,
    ocean_mask,
    sides,
    ends,
    temper_near,
    saline_near,
    temper_out,
    saline_out,
    first_t,
    first_s,
    second_t,
    second_s,
    east_all,
    north_all,
    opens,
):
    depth, rows, columns = temper.shape
    near = temper_near.shape[0]
    for turn, (target, source) in enumerate(
        ((first_t, temper), (first_s, saline), (east_all, east), (north_all, north))
    ):
        part = slice(turn * depth, (turn + 1) * depth)
        fill_wide(target, source, sides[part], ends[part])
    fill_opens(opens, top, ocean_mask, sides[4 * depth], ends[4 * depth])
    temper_out[:near] = temper_near[...]
    saline_out[:near] = saline_near[...]

    def keep_first(target, k, value):
        (second_t, second_s)[target][k] = value

    def keep_last(target, k, value):
        (temper_out, saline_out)[target][k] = value[:rows, :columns]

    speeds = (east_all, north_all)
    step((first_t, first_s), speeds, opens, near - 1, depth, depth - 1, keep_first)
    step((second_t, second_s), speeds, opens, near, depth, depth - 1, keep_last)


def halo(parts, east_at, north_at):
    rows, columns = parts[0].shape[1:]
    count_gx, count_gy = lax.axis_size("gx"), lax.axis_size("gy")
    head = jnp.concatenate([x[:, :, :2] for x in parts], axis=0)
    tail = jnp.concatenate([x[:, :, -2:] for x in parts], axis=0)
    channels = head.shape[0]
    from_west = lax.ppermute(tail, "gx", [(i, (i + 1) % count_gx) for i in range(count_gx)])
    from_east = lax.ppermute(head, "gx", [((i + 1) % count_gx, i) for i in range(count_gx)])
    sides = jnp.concatenate(
        [from_east, jnp.zeros((channels, rows, LANES - 4), jnp.float32), from_west], axis=2
    )
    low = jnp.concatenate(
        [jnp.concatenate([x[:, :2] for x in parts], axis=0), sides[:, :2]], axis=2
    )
    high = jnp.concatenate(
        [jnp.concatenate([x[:, -2:] for x in parts], axis=0), sides[:, -2:]], axis=2
    )
    from_south = lax.ppermute(high, "gy", [(i, i + 1) for i in range(count_gy - 1)])
    from_north = lax.ppermute(low, "gy", [(i + 1, i) for i in range(count_gy - 1)])
    folded = lax.ppermute(high, "gx", [(i, count_gx - 1 - i) for i in range(count_gx)])
    folded = jnp.concatenate(
        [folded[:, ::-1, columns - 1 :: -1], folded[:, ::-1, : columns - 1 : -1]], axis=2
    )
    e0, e1 = east_at
    n0, n1 = north_at
    east_part = -jnp.concatenate([folded[e0:e1, :, 1:], folded[e0:e1, :, :1]], axis=2)
    north_part = -jnp.concatenate([folded[n0:n1, 1:], folded[n0:n1, :1]], axis=1)
    folded = jnp.concatenate([folded[:e0], east_part, north_part, folded[n1:]], axis=0)
    is_top = lax.axis_index("gy") == count_gy - 1
    above = jnp.where(is_top, folded, from_north)
    ends = jnp.concatenate(
        [above, jnp.zeros((channels, 4, columns + LANES), jnp.float32), from_south], axis=1
    )
    return sides, ends


def tile_halo(x):
    rows, columns = x.shape[1:]
    count_gx, count_gy = lax.axis_size("gx"), lax.axis_size("gy")
    from_west = lax.ppermute(
        x[:, :, -LANES:], "gx", [(i, (i + 1) % count_gx) for i in range(count_gx)]
    )
    from_east = lax.ppermute(
        x[:, :, :LANES], "gx", [((i + 1) % count_gx, i) for i in range(count_gx)]
    )
    lane = lax.broadcasted_iota(jnp.int32, from_west.shape, 2)
    sides = jnp.where(lane < LANES // 2, from_east, from_west)
    low = jnp.concatenate([x[:, :8], sides[:, :8]], axis=2)
    high = jnp.concatenate([x[:, -8:], sides[:, -8:]], axis=2)
    from_south = lax.ppermute(high, "gy", [(i, i + 1) for i in range(count_gy - 1)])
    from_north = lax.ppermute(low, "gy", [(i + 1, i) for i in range(count_gy - 1)])
    folded = lax.ppermute(high, "gx", [(i, count_gx - 1 - i) for i in range(count_gx)])
    return sides, from_north, from_south, folded


def body(
    air_forcing_quantities,
    segment_sea_subdomain,
    overlay_air_element,
    overlay_sea_profile,
    overlay_fraction_share,
    thermal_deviation,
    saltiness_deviation,
    zonal_interface_speed,
    poleward_interface_speed,
    sea_profile_indicator,
):
    devices = lax.axis_size("gx") * lax.axis_size("gy")
    blocks = segment_sea_subdomain.shape[0]
    atm_cells = air_forcing_quantities.shape[1]
    depth, parallels, meridians = thermal_deviation.shape
    capacity = max(2, 2 * blocks // devices)
    slot_count = devices * capacity
    f32 = jnp.float32
    air = air_forcing_quantities
    table = jnp.stack([air[0] + air[1] + air[2] + air[3], air[5] - air[4], air[6], air[7]])
    table = table.reshape(4 * atm_cells // LANES, LANES)

    outgoing, home = pl.pallas_call(
        functools.partial(send_kernel, capacity),
        out_shape=(
            jax.ShapeDtypeStruct((slot_count * 5, LANES), f32),
            jax.ShapeDtypeStruct((blocks,), jnp.int32),
        ),
        in_specs=[SMEM, VMEM, VMEM, VMEM, VMEM],
        out_specs=(VMEM, SMEM),
        scratch_shapes=[
            pltpu.SMEM((devices,), jnp.int32),
            pltpu.VMEM((table.shape[0], 2 * LANES), jnp.bfloat16),
            pltpu.VMEM((LANES, LANES), jnp.bfloat16),
        ],
        **gather_kernel_params(10**9),
    )(
        segment_sea_subdomain.reshape(blocks),
        table,
        overlay_air_element,
        overlay_sea_profile,
        overlay_fraction_share,
    )

    (
        outgoing,
        thermal_deviation,
        saltiness_deviation,
        zonal_interface_speed,
        poleward_interface_speed,
        sea_profile_indicator,
    ) = lax.optimization_barrier(
        (
            outgoing,
            thermal_deviation,
            saltiness_deviation,
            zonal_interface_speed,
            poleward_interface_speed,
            sea_profile_indicator,
        )
    )
    arrived = lax.all_to_all(outgoing, ("gx", "gy"), split_axis=0, concat_axis=0, tiled=True)
    ocean_mask = sea_profile_indicator.astype(f32)
    sides, ends = halo(
        [
            thermal_deviation,
            saltiness_deviation,
            zonal_interface_speed,
            poleward_interface_speed,
            ocean_mask[None],
        ],
        (2 * depth, 3 * depth),
        (3 * depth, 4 * depth),
    )

    counts = jnp.sum(
        (arrived.reshape(devices, 5, capacity, LANES)[:, 4, :, 0] >= 0).astype(jnp.int32), axis=1
    )
    remapped, places, slots = pl.pallas_call(
        functools.partial(land_kernel, capacity, parallels, meridians),
        out_shape=(
            jax.ShapeDtypeStruct((4 * parallels, meridians), f32),
            jax.ShapeDtypeStruct((slot_count + GROUP, LANES), f32),
            jax.ShapeDtypeStruct((slot_count + GROUP + 1,), jnp.int32),
        ),
        in_specs=[SMEM, VMEM],
        out_specs=(VMEM, VMEM, SMEM),
        scratch_shapes=[
            pltpu.VMEM((4, slot_count + GROUP, LANES), f32),
            pltpu.VMEM((8 * parallels, meridians), f32),
            pltpu.VMEM((HALF, LANES), jnp.bfloat16),
        ],
        **gather_kernel_params(2 * 10**10),
    )(counts, arrived)
    remapped = remapped.reshape(4, parallels, meridians)
    around = tile_halo(remapped)

    top = (lax.axis_index("gy") == lax.axis_size("gy") - 1).astype(jnp.int32).reshape(1)
    wide = (parallels + 8, meridians + LANES)
    near, levels = 2, 4
    first_levels = pl.BlockSpec((levels, parallels, meridians), lambda i: (0, 0, 0))
    cube = jax.ShapeDtypeStruct((depth, parallels, meridians), f32)
    slab = jax.ShapeDtypeStruct((near, parallels, meridians), f32)
    temper_near, saline_near, surface = pl.pallas_call(
        functools.partial(near_kernel, depth),
        grid=(1,),
        out_shape=(slab, slab, jax.ShapeDtypeStruct((4, parallels, meridians), f32)),
        in_specs=[SMEM] + [first_levels] * 4 + [VMEM] * 8,
        out_specs=(VMEM, VMEM, VMEM),
        scratch_shapes=[pltpu.VMEM((levels,) + wide, f32)] * 6
        + [pltpu.VMEM((4,) + wide, f32)] * 2,
        **gather_kernel_params(10**8),
    )(
        top,
        thermal_deviation,
        saltiness_deviation,
        zonal_interface_speed,
        poleward_interface_speed,
        sea_profile_indicator,
        sides,
        ends,
        remapped,
        *around,
    )

    picked = pl.pallas_call(
        functools.partial(pick_kernel, capacity, parallels, meridians),
        out_shape=jax.ShapeDtypeStruct((slot_count * 4, LANES), f32),
        in_specs=[SMEM, VMEM, VMEM],
        out_specs=VMEM,
        scratch_shapes=[
            pltpu.VMEM((8 * parallels, meridians), jnp.bfloat16),
            pltpu.VMEM((HALF, LANES), jnp.bfloat16),
            pltpu.VMEM(((slot_count + capacity) * 4, LANES), f32),
        ],
        **gather_kernel_params(2 * 10**10),
    )(slots, surface.reshape(4 * parallels, meridians), places)
    picked, top = lax.optimization_barrier((picked, top))
    returned = lax.all_to_all(picked, ("gx", "gy"), split_axis=0, concat_axis=0, tiled=True)
    temper, saline = pl.pallas_call(
        deep_kernel,
        out_shape=(cube, cube),
        in_specs=[SMEM] + [VMEM] * 9,
        out_specs=(VMEM, VMEM),
        scratch_shapes=[pltpu.VMEM((depth,) + wide, f32)] * 6 + [pltpu.VMEM((4,) + wide, f32)],
        **gather_kernel_params(10**9),
    )(
        top,
        thermal_deviation,
        saltiness_deviation,
        zonal_interface_speed,
        poleward_interface_speed,
        sea_profile_indicator,
        sides,
        ends,
        temper_near,
        saline_near,
    )
    back_fields = pl.pallas_call(
        functools.partial(back_kernel, capacity),
        out_shape=jax.ShapeDtypeStruct((4 * atm_cells // LANES, LANES), f32),
        in_specs=[SMEM, VMEM, VMEM, VMEM],
        out_specs=VMEM,
        scratch_shapes=[
            pltpu.VMEM((8 * atm_cells // LANES, LANES), f32),
            pltpu.VMEM((LANES, LANES), jnp.bfloat16),
        ],
        **gather_kernel_params(2 * 10**9),
    )(home, returned, overlay_air_element, overlay_fraction_share)
    return temper, saline, back_fields.reshape(4, atm_cells)


def solution(mesh):
    return jax.shard_map(
        body,
        mesh=mesh,
        in_specs=(
            P(None, ("gx", "gy")),
            P(("gx", "gy"), None),
            P(("gx", "gy"), None),
            P(("gx", "gy"), None),
            P(("gx", "gy"), None),
            P(None, "gy", "gx"),
            P(None, "gy", "gx"),
            P(None, "gy", "gx"),
            P(None, "gy", "gx"),
            P("gy", "gx"),
        ),
        out_specs=(P(None, "gy", "gx"), P(None, "gy", "gx"), P(None, ("gx", "gy"))),
        check_vma=False,
    )
```

```python
import functools

import jax
import jax.numpy as jnp
from jax import lax
from jax.experimental import pallas as pl
from jax.experimental.pallas import tpu as pltpu
from jax.sharding import PartitionSpec as P

diffuse_rate = 0.12
mixing_base = 0.02
mixing_extra = 0.2
heat_factor = 0.5
fresh_factor = 0.5
stress_factor = 0.3

LANES = 128
GROUP = 8
HALF = 256
PAIR = 2
VMEM_BYTES = 48 * 1024 * 1024
CONTRACT_LAST = (((1,), (1,)), ((), ()))

SMEM = pl.BlockSpec(memory_space=pltpu.SMEM)
VMEM = pl.BlockSpec(memory_space=pltpu.VMEM)


def density(temper_field, saline_field):
    return (
        -0.2 * temper_field
        - 0.05 * temper_field * temper_field
        + 0.8 * saline_field
        + 0.03 * temper_field * saline_field
    )


def face_flux(near_cells, far_cells, velocity, open_faces):
    return open_faces * (
        velocity * 0.5 * (near_cells + far_cells) - diffuse_rate * (far_cells - near_cells)
    )


def two_terms(values):
    high = values.astype(jnp.bfloat16)
    return high, (values - high.astype(jnp.float32)).astype(jnp.bfloat16)


def narrow(places):
    return places.astype(jnp.float32).astype(jnp.bfloat16)


def number_rows(numbers):
    numbers[...] = narrow(lax.broadcasted_iota(jnp.int32, numbers.shape, 0))


def one_hot(places, numbers):
    return jnp.where(numbers == places, jnp.bfloat16(1), jnp.bfloat16(0))


def spread(rows_of, terms, numbers):
    hit = numbers == rows_of
    return jnp.concatenate([jnp.where(hit, term, jnp.bfloat16(0)) for term in terms], axis=0)


def halves_of(column, meridians):
    return [
        narrow(jnp.where(column // HALF == part, column % HALF, -1))
        for part in range(meridians // HALF)
    ]


def wide_one_hot(parts, b, numbers):
    return jnp.concatenate([one_hot(part[b : b + 1], numbers) for part in parts], axis=0)


def picked_rows(rows_of, table, fields, count):
    rows = lax.broadcasted_iota(jnp.int32, (count, rows_of.shape[1]), 0)
    hit = rows == rows_of
    return [
        jnp.sum(
            jnp.where(hit, table[field * count : (field + 1) * count], 0.0), axis=0, keepdims=True
        )
        for field in range(fields)
    ]


def send_kernel(
    capacity, subdomain, table, element, profile, share, out, home, tally, split_table, numbers
):
    devices = tally.shape[0]
    blocks = element.shape[0]
    high_rows = table.shape[0] // 4

    def clear(i, carry):
        tally[i] = 0
        return carry

    lax.fori_loop(0, devices, clear, 0)
    number_rows(numbers)
    out[...] = jnp.full(out.shape, -1.0, jnp.float32)
    high, low = two_terms(table[...])
    split_table[:, :LANES] = high
    split_table[:, LANES:] = low

    def group(g, carry):
        base = pl.multiple_of(g * GROUP, GROUP)
        cells = element[pl.ds(base, GROUP), :]
        near = narrow(cells & (LANES - 1))
        far = cells >> 7
        address = profile[pl.ds(base, GROUP), :].astype(jnp.float32)
        weight = share[pl.ds(base, GROUP), :]
        for first in range(0, GROUP, PAIR):
            names = range(first, first + PAIR)
            hot = jnp.concatenate([one_hot(near[b : b + 1], numbers[...]) for b in names], axis=1)
            found = jnp.dot(
                split_table[...],
                jnp.concatenate([hot, hot], axis=0),
                preferred_element_type=jnp.float32,
            )
            far_row = jnp.concatenate([far[b : b + 1] for b in names], axis=1)
            values = picked_rows(far_row, found, 4, high_rows)
            for turn, b in enumerate(names):
                tile = subdomain[base + b]
                place = tally[tile]
                tally[tile] = place + 1
                home[base + b] = tile * (4 * capacity) + place
                row = tile * (5 * capacity) + place
                for field in range(4):
                    out[pl.ds(row + field * capacity, 1), :] = (
                        values[field][:, turn * LANES : (turn + 1) * LANES] * weight[b : b + 1]
                    )
                out[pl.ds(row + 4 * capacity, 1), :] = address[b : b + 1]
        return carry

    lax.fori_loop(0, blocks // GROUP, group, 0)


def gather_kernel_params(flops):
    return dict(
        compiler_params=pltpu.CompilerParams(vmem_limit_bytes=VMEM_BYTES),
        cost_estimate=pl.CostEstimate(flops=flops, bytes_accessed=4_000_000, transcendentals=0),
    )


def land_kernel(
    capacity,
    parallels,
    meridians,
    counts,
    arrived,
    remapped,
    places,
    slots,
    values,
    total,
    numbers,
):
    sources = counts.shape[0]
    last = slots.shape[0] - 1
    shift = meridians.bit_length() - 1
    places[...] = jnp.full(places.shape, -1.0, jnp.float32)
    total[...] = jnp.zeros(total.shape, jnp.float32)

    def from_source(source, count):
        def slot(place, count):
            row = source * (5 * capacity) + place
            for field in range(4):
                values[field, pl.ds(count, 1), :] = arrived[pl.ds(row + field * capacity, 1), :]
            places[pl.ds(count, 1), :] = arrived[pl.ds(row + 4 * capacity, 1), :]
            slots[count] = source * (4 * capacity) + place
            return count + 1

        return lax.fori_loop(0, counts[source], slot, count)

    filled = lax.fori_loop(0, sources, from_source, 0)
    slots[last] = filled
    for extra in range(GROUP):
        slots[filled + extra] = sources * (4 * capacity)
    number_rows(numbers)

    def group(g, carry):
        base = pl.multiple_of(g * GROUP, GROUP)
        address = places[pl.ds(base, GROUP), :].astype(jnp.int32)
        row = narrow(address >> shift)
        column = halves_of(address & (meridians - 1), meridians)
        split = [two_terms(values[field, pl.ds(base, GROUP), :]) for field in range(4)]
        terms = [split[field][term] for term in range(2) for field in range(4)]
        names = range(GROUP)
        left = jnp.concatenate(
            [
                spread(row[b : b + 1], [term[b : b + 1] for term in terms], numbers[:parallels])
                for b in names
            ],
            axis=1,
        )
        right = jnp.concatenate([wide_one_hot(column, b, numbers[...]) for b in names], axis=1)
        total[...] += lax.dot_general(
            left, right, CONTRACT_LAST, preferred_element_type=jnp.float32
        )
        return carry

    lax.fori_loop(0, (filled + GROUP - 1) // GROUP, group, 0)
    half = 4 * parallels
    remapped[...] = total[:half] + total[half:]


def pick_kernel(capacity, parallels, meridians, slots, surface, places, out, split_table, numbers, found_rows):
    last = slots.shape[0] - 1
    half = 4 * parallels
    shift = meridians.bit_length() - 1
    filled = slots[last]
    high, low = two_terms(surface[...])
    split_table[:half] = high
    split_table[half:] = low
    found_rows[...] = jnp.zeros(found_rows.shape, jnp.float32)
    number_rows(numbers)

    def group(g, carry):
        base = pl.multiple_of(g * GROUP, GROUP)
        address = places[pl.ds(base, GROUP), :].astype(jnp.int32)
        row = address >> shift
        column = halves_of(address & (meridians - 1), meridians)
        for first in range(0, GROUP, PAIR):
            names = range(first, first + PAIR)
            hot = jnp.concatenate([wide_one_hot(column, b, numbers[...]) for b in names], axis=1)
            found = jnp.dot(split_table[...], hot, preferred_element_type=jnp.float32)
            found = found[:half] + found[half:]
            wide_row = jnp.concatenate([row[b : b + 1] for b in names], axis=1)
            values = picked_rows(wide_row, found, 4, parallels)
            for turn, b in enumerate(names):
                target = slots[base + b]
                for field in range(4):
                    found_rows[pl.ds(target + field * capacity, 1), :] = values[field][
                        :, turn * LANES : (turn + 1) * LANES
                    ]
        return carry

    lax.fori_loop(0, (filled + GROUP - 1) // GROUP, group, 0)
    out[...] = found_rows[: out.shape[0]]


def back_kernel(capacity, home, returned, element, share, out, total, numbers):
    blocks = element.shape[0]
    high_rows = out.shape[0] // 4
    total[...] = jnp.zeros(total.shape, jnp.float32)
    number_rows(numbers)

    def group(g, carry):
        base = pl.multiple_of(g * GROUP, GROUP)
        cells = element[pl.ds(base, GROUP), :]
        near = narrow(cells & (LANES - 1))
        far = narrow(cells >> 7)
        weight = share[pl.ds(base, GROUP), :]
        names = range(GROUP)
        lefts = []
        for b in names:
            row = home[base + b]
            split = [
                two_terms(returned[pl.ds(row + field * capacity, 1), :] * weight[b : b + 1])
                for field in range(4)
            ]
            terms = [split[field][term] for term in range(2) for field in range(4)]
            lefts.append(spread(far[b : b + 1], terms, numbers[:high_rows]))
        left = jnp.concatenate(lefts, axis=1)
        right = jnp.concatenate([one_hot(near[b : b + 1], numbers[...]) for b in names], axis=1)
        total[...] += lax.dot_general(
            left, right, CONTRACT_LAST, preferred_element_type=jnp.float32
        )
        return carry

    lax.fori_loop(0, blocks // GROUP, group, 0)
    half = 4 * high_rows
    out[...] = total[:half] + total[half:]


def next_column(x):
    return pltpu.roll(x, x.shape[1] - 1, axis=1)


def next_row(x):
    return pltpu.roll(x, x.shape[0] - 1, axis=0)


EDGE = 2
SIDE_CHANNELS = LANES // EDGE
END_CHANNELS = 8 // EDGE


def edge_kernel(home, temper, saline, east, north, ocean_mask, first, last, low, high):
    depth, rows, columns = temper.shape
    lane = lax.broadcasted_iota(jnp.int32, (rows, LANES), 1)
    heads, tails = [None] * first.shape[0], [None] * first.shape[0]
    mask = ocean_mask[...].astype(jnp.float32)
    for c in range(4 * depth + 1):
        if c < 4 * depth:
            source, k = (temper, saline, east, north)[c // depth], c % depth
            left, right = source[k, :, :LANES], source[k, :, columns - LANES :]
            top_rows, end_rows = source[k, :EDGE, :], source[k, rows - EDGE :, :]
        else:
            left, right = mask[:, :LANES], mask[:, columns - LANES :]
            top_rows, end_rows = mask[:EDGE], mask[rows - EDGE :]
        tile, at = c // SIDE_CHANNELS, EDGE * (c % SIDE_CHANNELS)
        here = (lane >= at) & (lane < at + EDGE)
        head = left if at == 0 else pltpu.roll(left, at, axis=1)
        tail = pltpu.roll(right, (at + EDGE) % LANES, axis=1) if at + EDGE < LANES else right
        heads[tile] = head if at == 0 else jnp.where(here, head, heads[tile])
        tails[tile] = tail if at == 0 else jnp.where(here, tail, tails[tile])
        spot = EDGE * (c % END_CHANNELS)
        low[c // END_CHANNELS, spot : spot + EDGE, :] = top_rows
        high[c // END_CHANNELS, spot : spot + EDGE, :] = end_rows
    for c in range(4 * depth + 1, END_CHANNELS * low.shape[0]):
        spot = EDGE * (c % END_CHANNELS)
        low[c // END_CHANNELS, spot : spot + EDGE, :] = jnp.zeros((EDGE, columns), jnp.float32)
        high[c // END_CHANNELS, spot : spot + EDGE, :] = jnp.zeros((EDGE, columns), jnp.float32)
    for tile in range(first.shape[0]):
        first[tile] = heads[tile]
        last[tile] = tails[tile]


def rolled(x, shift, axis):
    shift = shift % x.shape[axis]
    return x if shift == 0 else pltpu.roll(x, shift, axis=axis)


def side_of(channel, from_east, from_west):
    at = EDGE * (channel % SIDE_CHANNELS)
    lane = lax.broadcasted_iota(jnp.int32, from_east.shape, 1)
    return jnp.where(
        lane < LANES // 2, rolled(from_east, -at, 1), rolled(from_west, LANES - EDGE - at, 1)
    )


def mirrored(across, kind):
    across = turned(across)
    if kind == 2:
        across = -next_column(across)
    last_row, row_before = across[7:8], across[6:7]
    if kind == 3:
        last_row, row_before = -row_before, -row_before
    upper = lax.broadcasted_iota(jnp.int32, across.shape, 0)
    return jnp.where(upper == 0, last_row, row_before)


def fill_channel(target, k, channel, kind, halo, top):
    from_east, from_west, from_north, from_south, folded, corner_n, corner_s, corner_f = halo
    rows = from_east.shape[1]
    columns = from_north.shape[2]
    tile, group = channel // SIDE_CHANNELS, channel // END_CHANNELS
    spot = EDGE * (channel % END_CHANNELS)
    tiles = from_east.shape[0]
    target[k, :rows, columns:] = side_of(channel, from_east[tile], from_west[tile])

    def end_of(part, corner, shift):
        return jnp.concatenate(
            [
                rolled(part[group], shift, 0),
                side_of(channel, corner[tile], corner[tiles + tile]),
            ],
            axis=1,
        )

    upper = lax.broadcasted_iota(jnp.int32, (8, columns + LANES), 0)
    above = end_of(from_north, corner_n, -spot)
    across = mirrored(end_of(folded, corner_f, 8 - EDGE - spot), kind)
    above = jnp.where(top[0] == 1, across, above)
    below = end_of(from_south, corner_s, 8 - EDGE - spot)
    target[k, rows:, :] = jnp.where(upper < 4, above, below)


def fill_wide(targets, sources, depth, halo, top):
    for kind, (target, source) in enumerate(zip(targets, sources)):
        levels, rows, columns = source.shape
        target[:, :rows, :columns] = source[...]
        for k in range(levels):
            fill_channel(target, k, kind * depth + k, kind, halo, top)


def fill_opens(opens, top, ocean_mask, channel, halo):
    rows, columns = ocean_mask.shape
    opens[0, :rows, :columns] = ocean_mask[...].astype(jnp.float32)
    fill_channel(opens, 0, channel, 0, halo, top)
    here = opens[0]
    opens[1] = here * next_column(here)
    opens[2] = here * next_row(here)
    row_ids = lax.broadcasted_iota(jnp.int32, here.shape, 0)
    opens[3] = jnp.where((row_ids == rows - 1) & (top[0] == 1), 0.0, 1.0)


def mixing_at(t, s, t_below, s_below, mask):
    return (
        mixing_base
        + mixing_extra * jax.nn.sigmoid(4.0 * (density(t, s) - density(t_below, s_below)))
    ) * mask


def step(source, speeds, opens, first, stop, floor, keep, forcing=None):
    source_t, source_s = source
    east_all, north_all = speeds

    def level(k, carry):
        below = jnp.minimum(k + 1, floor)
        t, s = source_t[k], source_s[k]
        t_below, s_below = source_t[below], source_s[below]
        mask = opens[0]
        mixing = mixing_at(t, s, t_below, s_below, mask)
        east_speed = east_all[k]
        north_speed = north_all[k] * opens[3]
        new_gains = []
        for turn, (x, x_below) in enumerate(((t, t_below), (s, s_below))):
            gradient = mixing * (x_below - x)
            east_flux = face_flux(x, next_column(x), east_speed, opens[1])
            north_flux = face_flux(x, next_row(x), north_speed, opens[2])
            change = (
                -(east_flux - pltpu.roll(east_flux, 1, axis=1))
                - (north_flux - pltpu.roll(north_flux, 1, axis=0))
                + (gradient - carry[turn])
            )
            if forcing is not None:
                change = change + jnp.where(k == 0, forcing[turn], 0.0)
            keep(turn, k, x + mask * change)
            new_gains.append(gradient)
        return tuple(new_gains)

    if first == 0:
        nothing = jnp.zeros(source_t.shape[1:], jnp.float32)
        gains = (nothing, nothing)
    else:
        t, s, t_below, s_below = (x[k] for k in (first - 1, first) for x in source)
        mixing = mixing_at(t, s, t_below, s_below, opens[0])
        gains = (mixing * (t_below - t), mixing * (s_below - s))
    lax.fori_loop(first, stop, level, gains)


def turned(x):
    back = LANES - 1 - lax.broadcasted_iota(jnp.int32, (x.shape[0], LANES), 1)
    pieces = [
        jnp.take_along_axis(x[:, at : at + LANES], back, axis=1, mode="promise_in_bounds")
        for at in range(0, x.shape[1], LANES)
    ]
    return jnp.concatenate(pieces[-2::-1] + pieces[-1:], axis=1)


def near_kernel(
    depth,
    top,
    temper,
    saline,
    east,
    north,
    ocean_mask,
    from_east,
    from_west,
    from_north_all,
    from_south_all,
    folded_all,
    corner_n,
    corner_s,
    corner_f,
    remapped,
    remap_sides,
    from_north,
    from_south,
    folded,
    temper_out,
    saline_out,
    surface,
    first_t,
    first_s,
    second_t,
    second_s,
    east_all,
    north_all,
    remap_all,
    opens,
):
    levels, rows, columns = temper.shape
    halo = (
        from_east,
        from_west,
        from_north_all,
        from_south_all,
        folded_all,
        corner_n,
        corner_s,
        corner_f,
    )
    targets, sources = (first_t, first_s, east_all, north_all), (temper, saline, east, north)
    fill_wide(targets, sources, depth, halo, top)
    fill_opens(opens, top, ocean_mask, 4 * depth, halo)
    upper = lax.broadcasted_iota(jnp.int32, (8, columns + LANES), 0)
    remap_all[:, :rows, :columns] = remapped[...]
    remap_all[:, :rows, columns:] = remap_sides[...]
    for field in range(4):
        across = mirrored(folded[field], field)
        above = jnp.where(top[0] == 1, across, from_north[field])
        remap_all[field, rows:, :] = jnp.where(upper < 4, above, from_south[field])
    east_all[0] = east_all[0] + stress_factor * remap_all[2]
    north_all[0] = north_all[0] + stress_factor * remap_all[3]
    remap_all[0] = heat_factor * remap_all[0]
    remap_all[1] = fresh_factor * remap_all[1]
    forcing = (remap_all[0], remap_all[1])

    def keep_first(target, k, value):
        (second_t, second_s)[target][k] = value

    def keep_last(target, k, value):
        (temper_out, saline_out)[target][k] = value[:rows, :columns]

    speeds = (east_all, north_all)
    step((first_t, first_s), speeds, opens, 0, levels - 1, levels - 1, keep_first, forcing)
    step((second_t, second_s), speeds, opens, 0, levels - 2, levels - 1, keep_last, forcing)
    mask = opens[0, :rows, :columns]
    t, s = temper_out[0], saline_out[0]
    surface[0] = t * mask
    surface[1] = s * mask
    surface[2] = density(t, s) * mask
    surface[3] = east_all[0, :rows, :columns] * mask


def deep_kernel(
    top,
    temper,
    saline,
    east,
    north,
    ocean_mask,
    from_east,
    from_west,
    from_north,
    from_south,
    folded,
    corner_n,
    corner_s,
    corner_f,
    temper_near,
    saline_near,
    temper_out,
    saline_out,
    first_t,
    first_s,
    second_t,
    second_s,
    east_all,
    north_all,
    opens,
):
    depth, rows, columns = temper.shape
    near = temper_near.shape[0]
    halo = (from_east, from_west, from_north, from_south, folded, corner_n, corner_s, corner_f)
    targets, sources = (first_t, first_s, east_all, north_all), (temper, saline, east, north)
    fill_wide(targets, sources, depth, halo, top)
    fill_opens(opens, top, ocean_mask, 4 * depth, halo)
    temper_out[:near] = temper_near[...]
    saline_out[:near] = saline_near[...]

    def keep_first(target, k, value):
        (second_t, second_s)[target][k] = value

    def keep_last(target, k, value):
        (temper_out, saline_out)[target][k] = value[:rows, :columns]

    speeds = (east_all, north_all)
    step((first_t, first_s), speeds, opens, near - 1, depth, depth - 1, keep_first)
    step((second_t, second_s), speeds, opens, near, depth, depth - 1, keep_last)


def edge_halo(first, last, low, high):
    count_gx, count_gy = lax.axis_size("gx"), lax.axis_size("gy")
    north_of = [(i + 1, i) for i in range(count_gy - 1)]
    south_of = [(i, i + 1) for i in range(count_gy - 1)]
    across = [(i, count_gx - 1 - i) for i in range(count_gx)]
    from_west = lax.ppermute(last, "gx", [(i, (i + 1) % count_gx) for i in range(count_gx)])
    from_east = lax.ppermute(first, "gx", [((i + 1) % count_gx, i) for i in range(count_gx)])
    from_south = lax.ppermute(high, "gy", south_of)
    from_north = lax.ppermute(low, "gy", north_of)
    folded = lax.ppermute(high, "gx", across)
    corner_low = jnp.concatenate([from_east[:, :8], from_west[:, :8]], axis=0)
    corner_high = jnp.concatenate([from_east[:, -8:], from_west[:, -8:]], axis=0)
    return (
        from_east,
        from_west,
        from_north,
        from_south,
        folded,
        lax.ppermute(corner_low, "gy", north_of),
        lax.ppermute(corner_high, "gy", south_of),
        lax.ppermute(corner_high, "gx", across),
    )


def tile_halo(x):
    rows, columns = x.shape[1:]
    count_gx, count_gy = lax.axis_size("gx"), lax.axis_size("gy")
    from_west = lax.ppermute(
        x[:, :, -LANES:], "gx", [(i, (i + 1) % count_gx) for i in range(count_gx)]
    )
    from_east = lax.ppermute(
        x[:, :, :LANES], "gx", [((i + 1) % count_gx, i) for i in range(count_gx)]
    )
    lane = lax.broadcasted_iota(jnp.int32, from_west.shape, 2)
    sides = jnp.where(lane < LANES // 2, from_east, from_west)
    low = jnp.concatenate([x[:, :8], sides[:, :8]], axis=2)
    high = jnp.concatenate([x[:, -8:], sides[:, -8:]], axis=2)
    from_south = lax.ppermute(high, "gy", [(i, i + 1) for i in range(count_gy - 1)])
    from_north = lax.ppermute(low, "gy", [(i + 1, i) for i in range(count_gy - 1)])
    folded = lax.ppermute(high, "gx", [(i, count_gx - 1 - i) for i in range(count_gx)])
    return sides, from_north, from_south, folded


def body(
    air_forcing_quantities,
    segment_sea_subdomain,
    overlay_air_element,
    overlay_sea_profile,
    overlay_fraction_share,
    thermal_deviation,
    saltiness_deviation,
    zonal_interface_speed,
    poleward_interface_speed,
    sea_profile_indicator,
):
    devices = lax.axis_size("gx") * lax.axis_size("gy")
    blocks = segment_sea_subdomain.shape[0]
    atm_cells = air_forcing_quantities.shape[1]
    depth, parallels, meridians = thermal_deviation.shape
    capacity = max(2, 2 * blocks // devices)
    slot_count = devices * capacity
    f32 = jnp.float32
    air = air_forcing_quantities
    table = jnp.stack([air[0] + air[1] + air[2] + air[3], air[5] - air[4], air[6], air[7]])
    table = table.reshape(4 * atm_cells // LANES, LANES)

    outgoing, home = pl.pallas_call(
        functools.partial(send_kernel, capacity),
        out_shape=(
            jax.ShapeDtypeStruct((slot_count * 5, LANES), f32),
            jax.ShapeDtypeStruct((blocks,), jnp.int32),
        ),
        in_specs=[SMEM, VMEM, VMEM, VMEM, VMEM],
        out_specs=(VMEM, SMEM),
        scratch_shapes=[
            pltpu.SMEM((devices,), jnp.int32),
            pltpu.VMEM((table.shape[0], 2 * LANES), jnp.bfloat16),
            pltpu.VMEM((LANES, LANES), jnp.bfloat16),
        ],
        **gather_kernel_params(10**9),
    )(
        segment_sea_subdomain.reshape(blocks),
        table,
        overlay_air_element,
        overlay_sea_profile,
        overlay_fraction_share,
    )

    arrived = lax.all_to_all(outgoing, ("gx", "gy"), split_axis=0, concat_axis=0, tiled=True)
    channels = 4 * depth + 1
    packed = jax.ShapeDtypeStruct((-(-channels // SIDE_CHANNELS), parallels, LANES), f32)
    stacked = jax.ShapeDtypeStruct((-(-channels // END_CHANNELS), 8, meridians), f32)
    edges = pl.pallas_call(
        edge_kernel,
        out_shape=(packed, packed, stacked, stacked),
        in_specs=[SMEM] + [VMEM] * 5,
        out_specs=(VMEM,) * 4,
        **gather_kernel_params(10**7),
    )(
        home,
        thermal_deviation,
        saltiness_deviation,
        zonal_interface_speed,
        poleward_interface_speed,
        sea_profile_indicator,
    )
    halo = edge_halo(*edges)

    counts = jnp.sum(
        (arrived.reshape(devices, 5, capacity, LANES)[:, 4, :, 0] >= 0).astype(jnp.int32), axis=1
    )
    remapped, places, slots = pl.pallas_call(
        functools.partial(land_kernel, capacity, parallels, meridians),
        out_shape=(
            jax.ShapeDtypeStruct((4 * parallels, meridians), f32),
            jax.ShapeDtypeStruct((slot_count + GROUP, LANES), f32),
            jax.ShapeDtypeStruct((slot_count + GROUP + 1,), jnp.int32),
        ),
        in_specs=[SMEM, VMEM],
        out_specs=(VMEM, VMEM, SMEM),
        scratch_shapes=[
            pltpu.VMEM((4, slot_count + GROUP, LANES), f32),
            pltpu.VMEM((8 * parallels, meridians), f32),
            pltpu.VMEM((HALF, LANES), jnp.bfloat16),
        ],
        **gather_kernel_params(2 * 10**10),
    )(counts, arrived)
    remapped = remapped.reshape(4, parallels, meridians)
    around = tile_halo(remapped)

    top = (lax.axis_index("gy") == lax.axis_size("gy") - 1).astype(jnp.int32).reshape(1)
    wide = (parallels + 8, meridians + LANES)
    near, levels = 2, 4
    first_levels = pl.BlockSpec((levels, parallels, meridians), lambda i: (0, 0, 0))
    cube = jax.ShapeDtypeStruct((depth, parallels, meridians), f32)
    slab = jax.ShapeDtypeStruct((near, parallels, meridians), f32)
    temper_near, saline_near, surface = pl.pallas_call(
        functools.partial(near_kernel, depth),
        grid=(1,),
        out_shape=(slab, slab, jax.ShapeDtypeStruct((4, parallels, meridians), f32)),
        in_specs=[SMEM] + [first_levels] * 4 + [VMEM] * 14,
        out_specs=(VMEM, VMEM, VMEM),
        scratch_shapes=[pltpu.VMEM((levels,) + wide, f32)] * 6
        + [pltpu.VMEM((4,) + wide, f32)] * 2,
        **gather_kernel_params(10**8),
    )(
        top,
        thermal_deviation,
        saltiness_deviation,
        zonal_interface_speed,
        poleward_interface_speed,
        sea_profile_indicator,
        *halo,
        remapped,
        *around,
    )

    picked = pl.pallas_call(
        functools.partial(pick_kernel, capacity, parallels, meridians),
        out_shape=jax.ShapeDtypeStruct((slot_count * 4, LANES), f32),
        in_specs=[SMEM, VMEM, VMEM],
        out_specs=VMEM,
        scratch_shapes=[
            pltpu.VMEM((8 * parallels, meridians), jnp.bfloat16),
            pltpu.VMEM((HALF, LANES), jnp.bfloat16),
            pltpu.VMEM(((slot_count + capacity) * 4, LANES), f32),
        ],
        **gather_kernel_params(2 * 10**10),
    )(slots, surface.reshape(4 * parallels, meridians), places)
    picked, top = lax.optimization_barrier((picked, top))
    returned = lax.all_to_all(picked, ("gx", "gy"), split_axis=0, concat_axis=0, tiled=True)
    temper, saline = pl.pallas_call(
        deep_kernel,
        out_shape=(cube, cube),
        in_specs=[SMEM] + [VMEM] * 15,
        out_specs=(VMEM, VMEM),
        scratch_shapes=[pltpu.VMEM((depth,) + wide, f32)] * 6 + [pltpu.VMEM((4,) + wide, f32)],
        **gather_kernel_params(10**9),
    )(
        top,
        thermal_deviation,
        saltiness_deviation,
        zonal_interface_speed,
        poleward_interface_speed,
        sea_profile_indicator,
        *halo,
        temper_near,
        saline_near,
    )
    back_fields = pl.pallas_call(
        functools.partial(back_kernel, capacity),
        out_shape=jax.ShapeDtypeStruct((4 * atm_cells // LANES, LANES), f32),
        in_specs=[SMEM, VMEM, VMEM, VMEM],
        out_specs=VMEM,
        scratch_shapes=[
            pltpu.VMEM((8 * atm_cells // LANES, LANES), f32),
            pltpu.VMEM((LANES, LANES), jnp.bfloat16),
        ],
        **gather_kernel_params(2 * 10**9),
    )(home, returned, overlay_air_element, overlay_fraction_share)
    return temper, saline, back_fields.reshape(4, atm_cells)


def solution(mesh):
    return jax.shard_map(
        body,
        mesh=mesh,
        in_specs=(
            P(None, ("gx", "gy")),
            P(("gx", "gy"), None),
            P(("gx", "gy"), None),
            P(("gx", "gy"), None),
            P(("gx", "gy"), None),
            P(None, "gy", "gx"),
            P(None, "gy", "gx"),
            P(None, "gy", "gx"),
            P(None, "gy", "gx"),
            P("gy", "gx"),
        ),
        out_specs=(P(None, "gy", "gx"), P(None, "gy", "gx"), P(None, ("gx", "gy"))),
        check_vma=False,
    )
```

```python
import functools

import jax
import jax.numpy as jnp
from jax import lax
from jax.experimental import pallas as pl
from jax.experimental.pallas import tpu as pltpu
from jax.sharding import PartitionSpec as P

diffuse_rate = 0.12
mixing_base = 0.02
mixing_extra = 0.2
heat_factor = 0.5
fresh_factor = 0.5
stress_factor = 0.3

LANES = 128
SEND_GROUP = 32
LAND_GROUP = 16
PICK_GROUP = 16
BACK_GROUP = 32
HALF = 256
PAIR = 2
VMEM_BYTES = 48 * 1024 * 1024
CONTRACT_LAST = (((1,), (1,)), ((), ()))

SMEM = pl.BlockSpec(memory_space=pltpu.SMEM)
VMEM = pl.BlockSpec(memory_space=pltpu.VMEM)


def density(temper_field, saline_field):
    return (
        -0.2 * temper_field
        - 0.05 * temper_field * temper_field
        + 0.8 * saline_field
        + 0.03 * temper_field * saline_field
    )


def face_flux(near_cells, far_cells, velocity, open_faces):
    return open_faces * (
        velocity * 0.5 * (near_cells + far_cells) - diffuse_rate * (far_cells - near_cells)
    )


def two_terms(values):
    high = values.astype(jnp.bfloat16)
    return high, (values - high.astype(jnp.float32)).astype(jnp.bfloat16)


def narrow(places):
    return places.astype(jnp.float32).astype(jnp.bfloat16)


def number_rows(numbers):
    numbers[...] = narrow(lax.broadcasted_iota(jnp.int32, numbers.shape, 0))


def one_hot(places, numbers):
    return jnp.where(numbers == places, jnp.bfloat16(1), jnp.bfloat16(0))


def spread(rows_of, terms, numbers):
    hit = numbers == rows_of
    return jnp.concatenate([jnp.where(hit, term, jnp.bfloat16(0)) for term in terms], axis=0)


def halves_of(address, parallels, meridians):
    shift = meridians.bit_length() - 1
    column = address & (meridians - 1)
    row = (address >> shift) + parallels * (column // HALF)
    return jnp.where(address < 0, -1, row), column % HALF


def picked_rows(rows_of, table, fields, count):
    rows = lax.broadcasted_iota(jnp.int32, (count, rows_of.shape[1]), 0)
    hit = rows == rows_of
    return [
        jnp.sum(
            jnp.where(hit, table[field * count : (field + 1) * count], 0.0), axis=0, keepdims=True
        )
        for field in range(fields)
    ]


def send_kernel(
    capacity, subdomain, table, element, profile, share, out, home, tally, split_table, numbers
):
    devices = tally.shape[0]
    blocks = element.shape[0]
    high_rows = table.shape[0] // 4

    def clear(i, carry):
        tally[i] = 0
        return carry

    lax.fori_loop(0, devices, clear, 0)
    number_rows(numbers)
    out[...] = jnp.full(out.shape, -1.0, jnp.float32)
    high, low = two_terms(table[...])
    split_table[:, :LANES] = high
    split_table[:, LANES:] = low

    def group(g, carry):
        base = pl.multiple_of(g * SEND_GROUP, SEND_GROUP)
        cells = element[pl.ds(base, SEND_GROUP), :]
        near = narrow(cells & (LANES - 1))
        far = cells >> 7
        address = profile[pl.ds(base, SEND_GROUP), :].astype(jnp.float32)
        weight = share[pl.ds(base, SEND_GROUP), :]
        for first in range(0, SEND_GROUP, PAIR):
            names = range(first, first + PAIR)
            hot = jnp.concatenate([one_hot(near[b : b + 1], numbers[...]) for b in names], axis=1)
            found = jnp.dot(
                split_table[...],
                jnp.concatenate([hot, hot], axis=0),
                preferred_element_type=jnp.float32,
            )
            far_row = jnp.concatenate([far[b : b + 1] for b in names], axis=1)
            values = picked_rows(far_row, found, 4, high_rows)
            for turn, b in enumerate(names):
                tile = subdomain[base + b]
                place = tally[tile]
                tally[tile] = place + 1
                home[base + b] = tile * (4 * capacity) + place
                row = tile * (5 * capacity) + place
                for field in range(4):
                    out[pl.ds(row + field * capacity, 1), :] = (
                        values[field][:, turn * LANES : (turn + 1) * LANES] * weight[b : b + 1]
                    )
                out[pl.ds(row + 4 * capacity, 1), :] = address[b : b + 1]
        return carry

    lax.fori_loop(0, blocks // SEND_GROUP, group, 0)


def gather_kernel_params(flops):
    return dict(
        compiler_params=pltpu.CompilerParams(vmem_limit_bytes=VMEM_BYTES),
        cost_estimate=pl.CostEstimate(flops=flops, bytes_accessed=4_000_000, transcendentals=0),
    )


def land_kernel(
    capacity,
    parallels,
    meridians,
    counts,
    arrived,
    remapped,
    places,
    slots,
    values,
    total,
    numbers,
):
    sources = counts.shape[0]
    last = slots.shape[0] - 1
    long_rows = parallels * (meridians // HALF)
    places[...] = jnp.full(places.shape, -1.0, jnp.float32)
    total[...] = jnp.zeros(total.shape, jnp.float32)

    def from_source(source, count):
        row = source * (5 * capacity)
        for field in range(4):
            values[field, pl.ds(count, capacity), :] = arrived[
                pl.ds(row + field * capacity, capacity), :
            ]
        places[pl.ds(count, capacity), :] = arrived[pl.ds(row + 4 * capacity, capacity), :]
        for place in range(capacity):
            slots[count + place] = source * (4 * capacity) + place
        return count + counts[source]

    filled = lax.fori_loop(0, sources, from_source, 0)
    slots[last] = filled
    for extra in range(LAND_GROUP):
        slots[filled + extra] = sources * (4 * capacity)
    number_rows(numbers)

    def group(g, carry):
        base = pl.multiple_of(g * LAND_GROUP, LAND_GROUP)
        address = places[pl.ds(base, LAND_GROUP), :].astype(jnp.int32)
        row, column = halves_of(address, parallels, meridians)
        row, column = narrow(row), narrow(column)
        split = [two_terms(values[field, pl.ds(base, LAND_GROUP), :]) for field in range(4)]
        terms = [split[field][term] for term in range(2) for field in range(4)]
        names = range(LAND_GROUP)
        left = jnp.concatenate(
            [
                spread(row[b : b + 1], [term[b : b + 1] for term in terms], numbers[:long_rows])
                for b in names
            ],
            axis=1,
        )
        right = jnp.concatenate([one_hot(column[b : b + 1], numbers[...]) for b in names], axis=1)
        total[...] += lax.dot_general(
            left, right, CONTRACT_LAST, preferred_element_type=jnp.float32
        )
        return carry

    lax.fori_loop(0, (filled + LAND_GROUP - 1) // LAND_GROUP, group, 0)
    for field in range(4):
        for part in range(meridians // HALF):
            at = field * long_rows + part * parallels
            remapped[field * parallels : (field + 1) * parallels, part * HALF : (part + 1) * HALF] = (
                total[at : at + parallels]
                + total[4 * long_rows + at : 4 * long_rows + at + parallels]
            )


def pick_kernel(capacity, parallels, meridians, slots, surface, places, out, split_table, numbers, found_rows):
    last = slots.shape[0] - 1
    long_rows = parallels * (meridians // HALF)
    half = 4 * long_rows
    filled = slots[last]
    for field in range(4):
        for part in range(meridians // HALF):
            high, low = two_terms(
                surface[
                    field * parallels : (field + 1) * parallels, part * HALF : (part + 1) * HALF
                ]
            )
            at = field * long_rows + part * parallels
            split_table[at : at + parallels] = high
            split_table[half + at : half + at + parallels] = low
    found_rows[...] = jnp.zeros(found_rows.shape, jnp.float32)
    number_rows(numbers)

    def group(g, carry):
        base = pl.multiple_of(g * PICK_GROUP, PICK_GROUP)
        address = places[pl.ds(base, PICK_GROUP), :].astype(jnp.int32)
        row, column = halves_of(address, parallels, meridians)
        column = narrow(column)
        for first in range(0, PICK_GROUP, PAIR):
            names = range(first, first + PAIR)
            hot = jnp.concatenate([one_hot(column[b : b + 1], numbers[...]) for b in names], axis=1)
            found = jnp.dot(split_table[...], hot, preferred_element_type=jnp.float32)
            found = found[:half] + found[half:]
            wide_row = jnp.concatenate([row[b : b + 1] for b in names], axis=1)
            values = picked_rows(wide_row, found, 4, long_rows)
            for turn, b in enumerate(names):
                target = slots[base + b]
                for field in range(4):
                    found_rows[pl.ds(target + field * capacity, 1), :] = values[field][
                        :, turn * LANES : (turn + 1) * LANES
                    ]
        return carry

    lax.fori_loop(0, (filled + PICK_GROUP - 1) // PICK_GROUP, group, 0)
    out[...] = found_rows[: out.shape[0]]


def back_kernel(capacity, home, returned, element, share, out, total, numbers):
    blocks = element.shape[0]
    high_rows = out.shape[0] // 4
    total[...] = jnp.zeros(total.shape, jnp.float32)
    number_rows(numbers)

    def group(g, carry):
        base = pl.multiple_of(g * BACK_GROUP, BACK_GROUP)
        cells = element[pl.ds(base, BACK_GROUP), :]
        near = narrow(cells & (LANES - 1))
        far = narrow(cells >> 7)
        weight = share[pl.ds(base, BACK_GROUP), :]
        names = range(BACK_GROUP)
        lefts = []
        for b in names:
            row = home[base + b]
            split = [
                two_terms(returned[pl.ds(row + field * capacity, 1), :] * weight[b : b + 1])
                for field in range(4)
            ]
            terms = [split[field][term] for term in range(2) for field in range(4)]
            lefts.append(spread(far[b : b + 1], terms, numbers[:high_rows]))
        left = jnp.concatenate(lefts, axis=1)
        right = jnp.concatenate([one_hot(near[b : b + 1], numbers[...]) for b in names], axis=1)
        total[...] += lax.dot_general(
            left, right, CONTRACT_LAST, preferred_element_type=jnp.float32
        )
        return carry

    lax.fori_loop(0, blocks // BACK_GROUP, group, 0)
    half = 4 * high_rows
    out[...] = total[:half] + total[half:]


def next_column(x):
    return pltpu.roll(x, x.shape[1] - 1, axis=1)


def next_row(x):
    return pltpu.roll(x, x.shape[0] - 1, axis=0)


EDGE = 2
SIDE_CHANNELS = LANES // EDGE
END_CHANNELS = 8 // EDGE


def edge_kernel(home, temper, saline, east, north, ocean_mask, first, last, low, high):
    depth, rows, columns = temper.shape
    lane = lax.broadcasted_iota(jnp.int32, (rows, LANES), 1)
    heads, tails = [None] * first.shape[0], [None] * first.shape[0]
    mask = ocean_mask[...].astype(jnp.float32)
    for c in range(4 * depth + 1):
        if c < 4 * depth:
            source, k = (temper, saline, east, north)[c // depth], c % depth
            left, right = source[k, :, :LANES], source[k, :, columns - LANES :]
            top_rows, end_rows = source[k, :EDGE, :], source[k, rows - EDGE :, :]
        else:
            left, right = mask[:, :LANES], mask[:, columns - LANES :]
            top_rows, end_rows = mask[:EDGE], mask[rows - EDGE :]
        tile, at = c // SIDE_CHANNELS, EDGE * (c % SIDE_CHANNELS)
        here = (lane >= at) & (lane < at + EDGE)
        head = left if at == 0 else pltpu.roll(left, at, axis=1)
        tail = pltpu.roll(right, (at + EDGE) % LANES, axis=1) if at + EDGE < LANES else right
        heads[tile] = head if at == 0 else jnp.where(here, head, heads[tile])
        tails[tile] = tail if at == 0 else jnp.where(here, tail, tails[tile])
        spot = EDGE * (c % END_CHANNELS)
        low[c // END_CHANNELS, spot : spot + EDGE, :] = top_rows
        high[c // END_CHANNELS, spot : spot + EDGE, :] = end_rows
    for c in range(4 * depth + 1, END_CHANNELS * low.shape[0]):
        spot = EDGE * (c % END_CHANNELS)
        low[c // END_CHANNELS, spot : spot + EDGE, :] = jnp.zeros((EDGE, columns), jnp.float32)
        high[c // END_CHANNELS, spot : spot + EDGE, :] = jnp.zeros((EDGE, columns), jnp.float32)
    for tile in range(first.shape[0]):
        first[tile] = heads[tile]
        last[tile] = tails[tile]


def rolled(x, shift, axis):
    shift = shift % x.shape[axis]
    return x if shift == 0 else pltpu.roll(x, shift, axis=axis)


def side_of(channel, from_east, from_west):
    at = EDGE * (channel % SIDE_CHANNELS)
    lane = lax.broadcasted_iota(jnp.int32, from_east.shape, 1)
    return jnp.where(
        lane < LANES // 2, rolled(from_east, -at, 1), rolled(from_west, LANES - EDGE - at, 1)
    )


def mirrored(across, kind):
    across = turned(across)
    if kind == 2:
        across = -next_column(across)
    last_row, row_before = across[7:8], across[6:7]
    if kind == 3:
        last_row, row_before = -row_before, -row_before
    upper = lax.broadcasted_iota(jnp.int32, across.shape, 0)
    return jnp.where(upper == 0, last_row, row_before)


def fill_channel(target, k, channel, kind, halo, top):
    from_east, from_west, from_north, from_south, folded, corner_n, corner_s, corner_f = halo
    rows = from_east.shape[1]
    columns = from_north.shape[2]
    tile, group = channel // SIDE_CHANNELS, channel // END_CHANNELS
    spot = EDGE * (channel % END_CHANNELS)
    tiles = from_east.shape[0]
    target[k, :rows, columns:] = side_of(channel, from_east[tile], from_west[tile])

    def end_of(part, corner, shift):
        return jnp.concatenate(
            [
                rolled(part[group], shift, 0),
                side_of(channel, corner[tile], corner[tiles + tile]),
            ],
            axis=1,
        )

    upper = lax.broadcasted_iota(jnp.int32, (8, columns + LANES), 0)
    above = end_of(from_north, corner_n, -spot)
    across = mirrored(end_of(folded, corner_f, 8 - EDGE - spot), kind)
    above = jnp.where(top[0] == 1, across, above)
    below = end_of(from_south, corner_s, 8 - EDGE - spot)
    target[k, rows:, :] = jnp.where(upper < 4, above, below)


def fill_wide(targets, sources, depth, halo, top):
    for kind, (target, source) in enumerate(zip(targets, sources)):
        levels, rows, columns = source.shape
        target[:, :rows, :columns] = source[...]
        for k in range(levels):
            fill_channel(target, k, kind * depth + k, kind, halo, top)


def fill_opens(opens, top, ocean_mask, channel, halo):
    rows, columns = ocean_mask.shape
    opens[0, :rows, :columns] = ocean_mask[...].astype(jnp.float32)
    fill_channel(opens, 0, channel, 0, halo, top)
    here = opens[0]
    opens[1] = here * next_column(here)
    opens[2] = here * next_row(here)
    row_ids = lax.broadcasted_iota(jnp.int32, here.shape, 0)
    opens[3] = jnp.where((row_ids == rows - 1) & (top[0] == 1), 0.0, 1.0)


def mixing_at(t, s, t_below, s_below, mask):
    return (
        mixing_base
        + mixing_extra * jax.nn.sigmoid(4.0 * (density(t, s) - density(t_below, s_below)))
    ) * mask


def step(source, speeds, opens, first, stop, floor, keep, forcing=None):
    source_t, source_s = source
    east_all, north_all = speeds

    def level(k, carry):
        below = jnp.minimum(k + 1, floor)
        t, s = source_t[k], source_s[k]
        t_below, s_below = source_t[below], source_s[below]
        mask = opens[0]
        mixing = mixing_at(t, s, t_below, s_below, mask)
        east_speed = east_all[k]
        north_speed = north_all[k] * opens[3]
        new_gains = []
        for turn, (x, x_below) in enumerate(((t, t_below), (s, s_below))):
            gradient = mixing * (x_below - x)
            east_flux = face_flux(x, next_column(x), east_speed, opens[1])
            north_flux = face_flux(x, next_row(x), north_speed, opens[2])
            change = (
                -(east_flux - pltpu.roll(east_flux, 1, axis=1))
                - (north_flux - pltpu.roll(north_flux, 1, axis=0))
                + (gradient - carry[turn])
            )
            if forcing is not None:
                change = change + jnp.where(k == 0, forcing[turn], 0.0)
            keep(turn, k, x + mask * change)
            new_gains.append(gradient)
        return tuple(new_gains)

    if first == 0:
        nothing = jnp.zeros(source_t.shape[1:], jnp.float32)
        gains = (nothing, nothing)
    else:
        t, s, t_below, s_below = (x[k] for k in (first - 1, first) for x in source)
        mixing = mixing_at(t, s, t_below, s_below, opens[0])
        gains = (mixing * (t_below - t), mixing * (s_below - s))
    lax.fori_loop(first, stop, level, gains)


def turned(x):
    back = LANES - 1 - lax.broadcasted_iota(jnp.int32, (x.shape[0], LANES), 1)
    pieces = [
        jnp.take_along_axis(x[:, at : at + LANES], back, axis=1, mode="promise_in_bounds")
        for at in range(0, x.shape[1], LANES)
    ]
    return jnp.concatenate(pieces[-2::-1] + pieces[-1:], axis=1)


def near_kernel(
    depth,
    top,
    temper,
    saline,
    east,
    north,
    ocean_mask,
    from_east,
    from_west,
    from_north_all,
    from_south_all,
    folded_all,
    corner_n,
    corner_s,
    corner_f,
    remapped,
    remap_sides,
    from_north,
    from_south,
    folded,
    temper_out,
    saline_out,
    surface,
    first_t,
    first_s,
    second_t,
    second_s,
    east_all,
    north_all,
    remap_all,
    opens,
):
    levels, rows, columns = temper.shape
    halo = (
        from_east,
        from_west,
        from_north_all,
        from_south_all,
        folded_all,
        corner_n,
        corner_s,
        corner_f,
    )
    targets, sources = (first_t, first_s, east_all, north_all), (temper, saline, east, north)
    fill_wide(targets, sources, depth, halo, top)
    fill_opens(opens, top, ocean_mask, 4 * depth, halo)
    upper = lax.broadcasted_iota(jnp.int32, (8, columns + LANES), 0)
    remap_all[:, :rows, :columns] = remapped[...]
    remap_all[:, :rows, columns:] = remap_sides[...]
    for field in range(4):
        across = mirrored(folded[field], field)
        above = jnp.where(top[0] == 1, across, from_north[field])
        remap_all[field, rows:, :] = jnp.where(upper < 4, above, from_south[field])
    east_all[0] = east_all[0] + stress_factor * remap_all[2]
    north_all[0] = north_all[0] + stress_factor * remap_all[3]
    remap_all[0] = heat_factor * remap_all[0]
    remap_all[1] = fresh_factor * remap_all[1]
    forcing = (remap_all[0], remap_all[1])

    def keep_first(target, k, value):
        (second_t, second_s)[target][k] = value

    def keep_last(target, k, value):
        (temper_out, saline_out)[target][k] = value[:rows, :columns]

    speeds = (east_all, north_all)
    step((first_t, first_s), speeds, opens, 0, levels - 1, levels - 1, keep_first, forcing)
    step((second_t, second_s), speeds, opens, 0, levels - 2, levels - 1, keep_last, forcing)
    mask = opens[0, :rows, :columns]
    t, s = temper_out[0], saline_out[0]
    surface[0] = t * mask
    surface[1] = s * mask
    surface[2] = density(t, s) * mask
    surface[3] = east_all[0, :rows, :columns] * mask


def deep_kernel(
    top,
    temper,
    saline,
    east,
    north,
    ocean_mask,
    from_east,
    from_west,
    from_north,
    from_south,
    folded,
    corner_n,
    corner_s,
    corner_f,
    temper_near,
    saline_near,
    temper_out,
    saline_out,
    first_t,
    first_s,
    second_t,
    second_s,
    east_all,
    north_all,
    opens,
):
    depth, rows, columns = temper.shape
    near = temper_near.shape[0]
    halo = (from_east, from_west, from_north, from_south, folded, corner_n, corner_s, corner_f)
    targets, sources = (first_t, first_s, east_all, north_all), (temper, saline, east, north)
    fill_wide(targets, sources, depth, halo, top)
    fill_opens(opens, top, ocean_mask, 4 * depth, halo)
    temper_out[:near] = temper_near[...]
    saline_out[:near] = saline_near[...]

    def keep_first(target, k, value):
        (second_t, second_s)[target][k] = value

    def keep_last(target, k, value):
        (temper_out, saline_out)[target][k] = value[:rows, :columns]

    speeds = (east_all, north_all)
    step((first_t, first_s), speeds, opens, near - 1, depth, depth - 1, keep_first)
    step((second_t, second_s), speeds, opens, near, depth, depth - 1, keep_last)


def edge_halo(first, last, low, high):
    count_gx, count_gy = lax.axis_size("gx"), lax.axis_size("gy")
    north_of = [(i + 1, i) for i in range(count_gy - 1)]
    south_of = [(i, i + 1) for i in range(count_gy - 1)]
    across = [(i, count_gx - 1 - i) for i in range(count_gx)]
    from_west = lax.ppermute(last, "gx", [(i, (i + 1) % count_gx) for i in range(count_gx)])
    from_east = lax.ppermute(first, "gx", [((i + 1) % count_gx, i) for i in range(count_gx)])
    from_south = lax.ppermute(high, "gy", south_of)
    from_north = lax.ppermute(low, "gy", north_of)
    folded = lax.ppermute(high, "gx", across)
    corner_low = jnp.concatenate([from_east[:, :8], from_west[:, :8]], axis=0)
    corner_high = jnp.concatenate([from_east[:, -8:], from_west[:, -8:]], axis=0)
    return (
        from_east,
        from_west,
        from_north,
        from_south,
        folded,
        lax.ppermute(corner_low, "gy", north_of),
        lax.ppermute(corner_high, "gy", south_of),
        lax.ppermute(corner_high, "gx", across),
    )


def tile_halo(x):
    rows, columns = x.shape[1:]
    count_gx, count_gy = lax.axis_size("gx"), lax.axis_size("gy")
    from_west = lax.ppermute(
        x[:, :, -LANES:], "gx", [(i, (i + 1) % count_gx) for i in range(count_gx)]
    )
    from_east = lax.ppermute(
        x[:, :, :LANES], "gx", [((i + 1) % count_gx, i) for i in range(count_gx)]
    )
    lane = lax.broadcasted_iota(jnp.int32, from_west.shape, 2)
    sides = jnp.where(lane < LANES // 2, from_east, from_west)
    low = jnp.concatenate([x[:, :8], sides[:, :8]], axis=2)
    high = jnp.concatenate([x[:, -8:], sides[:, -8:]], axis=2)
    from_south = lax.ppermute(high, "gy", [(i, i + 1) for i in range(count_gy - 1)])
    from_north = lax.ppermute(low, "gy", [(i + 1, i) for i in range(count_gy - 1)])
    folded = lax.ppermute(high, "gx", [(i, count_gx - 1 - i) for i in range(count_gx)])
    return sides, from_north, from_south, folded


def body(
    air_forcing_quantities,
    segment_sea_subdomain,
    overlay_air_element,
    overlay_sea_profile,
    overlay_fraction_share,
    thermal_deviation,
    saltiness_deviation,
    zonal_interface_speed,
    poleward_interface_speed,
    sea_profile_indicator,
):
    devices = lax.axis_size("gx") * lax.axis_size("gy")
    blocks = segment_sea_subdomain.shape[0]
    atm_cells = air_forcing_quantities.shape[1]
    depth, parallels, meridians = thermal_deviation.shape
    capacity = max(2, 2 * blocks // devices)
    slot_count = devices * capacity
    spare = max(LAND_GROUP, PICK_GROUP, capacity)
    f32 = jnp.float32
    air = air_forcing_quantities
    table = jnp.stack([air[0] + air[1] + air[2] + air[3], air[5] - air[4], air[6], air[7]])
    table = table.reshape(4 * atm_cells // LANES, LANES)

    outgoing, home = pl.pallas_call(
        functools.partial(send_kernel, capacity),
        out_shape=(
            jax.ShapeDtypeStruct((slot_count * 5, LANES), f32),
            jax.ShapeDtypeStruct((blocks,), jnp.int32),
        ),
        in_specs=[SMEM, VMEM, VMEM, VMEM, VMEM],
        out_specs=(VMEM, SMEM),
        scratch_shapes=[
            pltpu.SMEM((devices,), jnp.int32),
            pltpu.VMEM((table.shape[0], 2 * LANES), jnp.bfloat16),
            pltpu.VMEM((LANES, LANES), jnp.bfloat16),
        ],
        **gather_kernel_params(10**9),
    )(
        segment_sea_subdomain.reshape(blocks),
        table,
        overlay_air_element,
        overlay_sea_profile,
        overlay_fraction_share,
    )

    arrived = lax.all_to_all(outgoing, ("gx", "gy"), split_axis=0, concat_axis=0, tiled=True)
    channels = 4 * depth + 1
    packed = jax.ShapeDtypeStruct((-(-channels // SIDE_CHANNELS), parallels, LANES), f32)
    stacked = jax.ShapeDtypeStruct((-(-channels // END_CHANNELS), 8, meridians), f32)
    edges = pl.pallas_call(
        edge_kernel,
        out_shape=(packed, packed, stacked, stacked),
        in_specs=[SMEM] + [VMEM] * 5,
        out_specs=(VMEM,) * 4,
        **gather_kernel_params(10**7),
    )(
        home,
        thermal_deviation,
        saltiness_deviation,
        zonal_interface_speed,
        poleward_interface_speed,
        sea_profile_indicator,
    )
    halo = edge_halo(*edges)

    counts = jnp.sum(
        (arrived.reshape(devices, 5, capacity, LANES)[:, 4, :, 0] >= 0).astype(jnp.int32), axis=1
    )
    remapped, places, slots = pl.pallas_call(
        functools.partial(land_kernel, capacity, parallels, meridians),
        out_shape=(
            jax.ShapeDtypeStruct((4 * parallels, meridians), f32),
            jax.ShapeDtypeStruct((slot_count + spare, LANES), f32),
            jax.ShapeDtypeStruct((slot_count + spare + 1,), jnp.int32),
        ),
        in_specs=[SMEM, VMEM],
        out_specs=(VMEM, VMEM, SMEM),
        scratch_shapes=[
            pltpu.VMEM((4, slot_count + spare, LANES), f32),
            pltpu.VMEM((8 * parallels * (meridians // HALF), HALF), f32),
            pltpu.VMEM((HALF, LANES), jnp.bfloat16),
        ],
        **gather_kernel_params(2 * 10**10),
    )(counts, arrived)
    remapped = remapped.reshape(4, parallels, meridians)
    around = tile_halo(remapped)

    top = (lax.axis_index("gy") == lax.axis_size("gy") - 1).astype(jnp.int32).reshape(1)
    wide = (parallels + 8, meridians + LANES)
    near, levels = 2, 4
    first_levels = pl.BlockSpec((levels, parallels, meridians), lambda i: (0, 0, 0))
    cube = jax.ShapeDtypeStruct((depth, parallels, meridians), f32)
    slab = jax.ShapeDtypeStruct((near, parallels, meridians), f32)
    temper_near, saline_near, surface = pl.pallas_call(
        functools.partial(near_kernel, depth),
        grid=(1,),
        out_shape=(slab, slab, jax.ShapeDtypeStruct((4, parallels, meridians), f32)),
        in_specs=[SMEM] + [first_levels] * 4 + [VMEM] * 14,
        out_specs=(VMEM, VMEM, VMEM),
        scratch_shapes=[pltpu.VMEM((levels,) + wide, f32)] * 6
        + [pltpu.VMEM((4,) + wide, f32)] * 2,
        **gather_kernel_params(10**8),
    )(
        top,
        thermal_deviation,
        saltiness_deviation,
        zonal_interface_speed,
        poleward_interface_speed,
        sea_profile_indicator,
        *halo,
        remapped,
        *around,
    )

    picked = pl.pallas_call(
        functools.partial(pick_kernel, capacity, parallels, meridians),
        out_shape=jax.ShapeDtypeStruct((slot_count * 4, LANES), f32),
        in_specs=[SMEM, VMEM, VMEM],
        out_specs=VMEM,
        scratch_shapes=[
            pltpu.VMEM((8 * parallels * (meridians // HALF), HALF), jnp.bfloat16),
            pltpu.VMEM((HALF, LANES), jnp.bfloat16),
            pltpu.VMEM(((slot_count + capacity) * 4, LANES), f32),
        ],
        **gather_kernel_params(2 * 10**10),
    )(slots, surface.reshape(4 * parallels, meridians), places)
    picked, top = lax.optimization_barrier((picked, top))
    returned = lax.all_to_all(picked, ("gx", "gy"), split_axis=0, concat_axis=0, tiled=True)
    temper, saline = pl.pallas_call(
        deep_kernel,
        out_shape=(cube, cube),
        in_specs=[SMEM] + [VMEM] * 15,
        out_specs=(VMEM, VMEM),
        scratch_shapes=[pltpu.VMEM((depth,) + wide, f32)] * 6 + [pltpu.VMEM((4,) + wide, f32)],
        **gather_kernel_params(10**9),
    )(
        top,
        thermal_deviation,
        saltiness_deviation,
        zonal_interface_speed,
        poleward_interface_speed,
        sea_profile_indicator,
        *halo,
        temper_near,
        saline_near,
    )
    back_fields = pl.pallas_call(
        functools.partial(back_kernel, capacity),
        out_shape=jax.ShapeDtypeStruct((4 * atm_cells // LANES, LANES), f32),
        in_specs=[SMEM, VMEM, VMEM, VMEM],
        out_specs=VMEM,
        scratch_shapes=[
            pltpu.VMEM((8 * atm_cells // LANES, LANES), f32),
            pltpu.VMEM((LANES, LANES), jnp.bfloat16),
        ],
        **gather_kernel_params(2 * 10**9),
    )(home, returned, overlay_air_element, overlay_fraction_share)
    return temper, saline, back_fields.reshape(4, atm_cells)


def solution(mesh):
    return jax.shard_map(
        body,
        mesh=mesh,
        in_specs=(
            P(None, ("gx", "gy")),
            P(("gx", "gy"), None),
            P(("gx", "gy"), None),
            P(("gx", "gy"), None),
            P(("gx", "gy"), None),
            P(None, "gy", "gx"),
            P(None, "gy", "gx"),
            P(None, "gy", "gx"),
            P(None, "gy", "gx"),
            P("gy", "gx"),
        ),
        out_specs=(P(None, "gy", "gx"), P(None, "gy", "gx"), P(None, ("gx", "gy"))),
        check_vma=False,
    )
```

```python
import functools

import jax
import jax.numpy as jnp
from jax import lax
from jax.experimental import pallas as pl
from jax.experimental.pallas import tpu as pltpu
from jax.sharding import PartitionSpec as P

diffuse_rate = 0.12
mixing_base = 0.02
mixing_extra = 0.2
heat_factor = 0.5
fresh_factor = 0.5
stress_factor = 0.3

LANES = 128
SEND_GROUP = 32
LAND_GROUP = 16
PICK_GROUP = 16
BACK_GROUP = 32
HALF = 256
PAIR = 2
VMEM_BYTES = 48 * 1024 * 1024
CONTRACT_LAST = (((1,), (1,)), ((), ()))

SMEM = pl.BlockSpec(memory_space=pltpu.SMEM)
VMEM = pl.BlockSpec(memory_space=pltpu.VMEM)


def density(temper_field, saline_field):
    return (
        -0.2 * temper_field
        - 0.05 * temper_field * temper_field
        + 0.8 * saline_field
        + 0.03 * temper_field * saline_field
    )


def two_terms(values):
    high = values.astype(jnp.bfloat16)
    return high, (values - high.astype(jnp.float32)).astype(jnp.bfloat16)


def narrow(places):
    return places.astype(jnp.float32).astype(jnp.bfloat16)


def number_rows(numbers):
    numbers[...] = narrow(lax.broadcasted_iota(jnp.int32, numbers.shape, 0))


def one_hot(places, numbers):
    return jnp.where(numbers == places, jnp.bfloat16(1), jnp.bfloat16(0))


def spread(rows_of, terms, numbers):
    hit = numbers == rows_of
    return jnp.concatenate([jnp.where(hit, term, jnp.bfloat16(0)) for term in terms], axis=0)


def halves_of(address, parallels, meridians):
    shift = meridians.bit_length() - 1
    column = address & (meridians - 1)
    row = (address >> shift) + parallels * (column // HALF)
    return jnp.where(address < 0, -1, row), column % HALF


def picked_rows(rows_of, table, fields, count):
    rows = lax.broadcasted_iota(jnp.int32, (count, rows_of.shape[1]), 0)
    hit = rows == rows_of
    return [
        jnp.sum(
            jnp.where(hit, table[field * count : (field + 1) * count], 0.0), axis=0, keepdims=True
        )
        for field in range(fields)
    ]


def send_kernel(
    capacity, subdomain, table, element, profile, share, out, home, tally, split_table, numbers
):
    devices = tally.shape[0]
    blocks = element.shape[0]
    high_rows = table.shape[0] // 4

    def clear(i, carry):
        tally[i] = 0
        return carry

    lax.fori_loop(0, devices, clear, 0)
    number_rows(numbers)
    out[...] = jnp.full(out.shape, -1.0, jnp.float32)
    high, low = two_terms(table[...])
    split_table[:, :LANES] = high
    split_table[:, LANES:] = low

    def group(g, carry):
        base = pl.multiple_of(g * SEND_GROUP, SEND_GROUP)
        cells = element[pl.ds(base, SEND_GROUP), :]
        near = narrow(cells & (LANES - 1))
        far = cells >> 7
        address = profile[pl.ds(base, SEND_GROUP), :].astype(jnp.float32)
        weight = share[pl.ds(base, SEND_GROUP), :]
        for first in range(0, SEND_GROUP, PAIR):
            names = range(first, first + PAIR)
            hot = jnp.concatenate([one_hot(near[b : b + 1], numbers[...]) for b in names], axis=1)
            found = jnp.dot(
                split_table[...],
                jnp.concatenate([hot, hot], axis=0),
                preferred_element_type=jnp.float32,
            )
            far_row = jnp.concatenate([far[b : b + 1] for b in names], axis=1)
            values = picked_rows(far_row, found, 4, high_rows)
            for turn, b in enumerate(names):
                tile = subdomain[base + b]
                place = tally[tile]
                tally[tile] = place + 1
                home[base + b] = tile * (4 * capacity) + place
                row = tile * (5 * capacity) + place
                for field in range(4):
                    out[pl.ds(row + field * capacity, 1), :] = (
                        values[field][:, turn * LANES : (turn + 1) * LANES] * weight[b : b + 1]
                    )
                out[pl.ds(row + 4 * capacity, 1), :] = address[b : b + 1]
        return carry

    lax.fori_loop(0, blocks // SEND_GROUP, group, 0)


def gather_kernel_params(flops):
    return dict(
        compiler_params=pltpu.CompilerParams(vmem_limit_bytes=VMEM_BYTES),
        cost_estimate=pl.CostEstimate(flops=flops, bytes_accessed=4_000_000, transcendentals=0),
    )


def land_kernel(
    capacity,
    parallels,
    meridians,
    counts,
    arrived,
    remapped,
    places,
    slots,
    values,
    total,
    numbers,
):
    sources = counts.shape[0]
    last = slots.shape[0] - 1
    long_rows = parallels * (meridians // HALF)
    places[...] = jnp.full(places.shape, -1.0, jnp.float32)
    total[...] = jnp.zeros(total.shape, jnp.float32)

    def from_source(source, count):
        row = source * (5 * capacity)
        for field in range(4):
            values[field, pl.ds(count, capacity), :] = arrived[
                pl.ds(row + field * capacity, capacity), :
            ]
        places[pl.ds(count, capacity), :] = arrived[pl.ds(row + 4 * capacity, capacity), :]
        for place in range(capacity):
            slots[count + place] = source * (4 * capacity) + place
        return count + counts[source]

    filled = lax.fori_loop(0, sources, from_source, 0)
    slots[last] = filled
    for extra in range(LAND_GROUP):
        slots[filled + extra] = sources * (4 * capacity)
    number_rows(numbers)

    def group(g, carry):
        base = pl.multiple_of(g * LAND_GROUP, LAND_GROUP)
        address = places[pl.ds(base, LAND_GROUP), :].astype(jnp.int32)
        row, column = halves_of(address, parallels, meridians)
        row, column = narrow(row), narrow(column)
        split = [two_terms(values[field, pl.ds(base, LAND_GROUP), :]) for field in range(4)]
        terms = [split[field][term] for term in range(2) for field in range(4)]
        names = range(LAND_GROUP)
        left = jnp.concatenate(
            [
                spread(row[b : b + 1], [term[b : b + 1] for term in terms], numbers[:long_rows])
                for b in names
            ],
            axis=1,
        )
        right = jnp.concatenate([one_hot(column[b : b + 1], numbers[...]) for b in names], axis=1)
        total[...] += lax.dot_general(
            left, right, CONTRACT_LAST, preferred_element_type=jnp.float32
        )
        return carry

    lax.fori_loop(0, (filled + LAND_GROUP - 1) // LAND_GROUP, group, 0)
    for field in range(4):
        for part in range(meridians // HALF):
            at = field * long_rows + part * parallels
            remapped[field * parallels : (field + 1) * parallels, part * HALF : (part + 1) * HALF] = (
                total[at : at + parallels]
                + total[4 * long_rows + at : 4 * long_rows + at + parallels]
            )


def pick_kernel(capacity, parallels, meridians, slots, surface, places, out, split_table, numbers, found_rows):
    last = slots.shape[0] - 1
    long_rows = parallels * (meridians // HALF)
    half = 4 * long_rows
    filled = slots[last]
    for field in range(4):
        for part in range(meridians // HALF):
            high, low = two_terms(
                surface[
                    field * parallels : (field + 1) * parallels, part * HALF : (part + 1) * HALF
                ]
            )
            at = field * long_rows + part * parallels
            split_table[at : at + parallels] = high
            split_table[half + at : half + at + parallels] = low
    found_rows[...] = jnp.zeros(found_rows.shape, jnp.float32)
    number_rows(numbers)

    def group(g, carry):
        base = pl.multiple_of(g * PICK_GROUP, PICK_GROUP)
        address = places[pl.ds(base, PICK_GROUP), :].astype(jnp.int32)
        row, column = halves_of(address, parallels, meridians)
        column = narrow(column)
        for first in range(0, PICK_GROUP, PAIR):
            names = range(first, first + PAIR)
            hot = jnp.concatenate([one_hot(column[b : b + 1], numbers[...]) for b in names], axis=1)
            found = jnp.dot(split_table[...], hot, preferred_element_type=jnp.float32)
            found = found[:half] + found[half:]
            wide_row = jnp.concatenate([row[b : b + 1] for b in names], axis=1)
            values = picked_rows(wide_row, found, 4, long_rows)
            for turn, b in enumerate(names):
                target = slots[base + b]
                for field in range(4):
                    found_rows[pl.ds(target + field * capacity, 1), :] = values[field][
                        :, turn * LANES : (turn + 1) * LANES
                    ]
        return carry

    lax.fori_loop(0, (filled + PICK_GROUP - 1) // PICK_GROUP, group, 0)
    out[...] = found_rows[: out.shape[0]]


def back_kernel(capacity, home, returned, element, share, out, total, numbers):
    blocks = element.shape[0]
    high_rows = out.shape[0] // 4
    total[...] = jnp.zeros(total.shape, jnp.float32)
    number_rows(numbers)

    def group(g, carry):
        base = pl.multiple_of(g * BACK_GROUP, BACK_GROUP)
        cells = element[pl.ds(base, BACK_GROUP), :]
        near = narrow(cells & (LANES - 1))
        far = narrow(cells >> 7)
        weight = share[pl.ds(base, BACK_GROUP), :]
        names = range(BACK_GROUP)
        lefts = []
        for b in names:
            row = home[base + b]
            split = [
                two_terms(returned[pl.ds(row + field * capacity, 1), :] * weight[b : b + 1])
                for field in range(4)
            ]
            terms = [split[field][term] for term in range(2) for field in range(4)]
            lefts.append(spread(far[b : b + 1], terms, numbers[:high_rows]))
        left = jnp.concatenate(lefts, axis=1)
        right = jnp.concatenate([one_hot(near[b : b + 1], numbers[...]) for b in names], axis=1)
        total[...] += lax.dot_general(
            left, right, CONTRACT_LAST, preferred_element_type=jnp.float32
        )
        return carry

    lax.fori_loop(0, blocks // BACK_GROUP, group, 0)
    half = 4 * high_rows
    out[...] = total[:half] + total[half:]


def next_column(x):
    return pltpu.roll(x, x.shape[1] - 1, axis=1)


def next_row(x):
    return pltpu.roll(x, x.shape[0] - 1, axis=0)


EDGE = 2
SIDE_CHANNELS = LANES // EDGE
END_CHANNELS = 8 // EDGE


def edge_kernel(home, temper, saline, east, north, ocean_mask, first, last, low, high):
    depth, rows, columns = temper.shape
    lane = lax.broadcasted_iota(jnp.int32, (rows, LANES), 1)
    heads, tails = [None] * first.shape[0], [None] * first.shape[0]
    mask = ocean_mask[...].astype(jnp.float32)
    for c in range(4 * depth + 1):
        if c < 4 * depth:
            source, k = (temper, saline, east, north)[c // depth], c % depth
            left, right = source[k, :, :LANES], source[k, :, columns - LANES :]
            top_rows, end_rows = source[k, :EDGE, :], source[k, rows - EDGE :, :]
        else:
            left, right = mask[:, :LANES], mask[:, columns - LANES :]
            top_rows, end_rows = mask[:EDGE], mask[rows - EDGE :]
        tile, at = c // SIDE_CHANNELS, EDGE * (c % SIDE_CHANNELS)
        here = (lane >= at) & (lane < at + EDGE)
        head = left if at == 0 else pltpu.roll(left, at, axis=1)
        tail = pltpu.roll(right, (at + EDGE) % LANES, axis=1) if at + EDGE < LANES else right
        heads[tile] = head if at == 0 else jnp.where(here, head, heads[tile])
        tails[tile] = tail if at == 0 else jnp.where(here, tail, tails[tile])
        spot = EDGE * (c % END_CHANNELS)
        low[c // END_CHANNELS, spot : spot + EDGE, :] = top_rows
        high[c // END_CHANNELS, spot : spot + EDGE, :] = end_rows
    for c in range(4 * depth + 1, END_CHANNELS * low.shape[0]):
        spot = EDGE * (c % END_CHANNELS)
        low[c // END_CHANNELS, spot : spot + EDGE, :] = jnp.zeros((EDGE, columns), jnp.float32)
        high[c // END_CHANNELS, spot : spot + EDGE, :] = jnp.zeros((EDGE, columns), jnp.float32)
    for tile in range(first.shape[0]):
        first[tile] = heads[tile]
        last[tile] = tails[tile]


def rolled(x, shift, axis):
    shift = shift % x.shape[axis]
    return x if shift == 0 else pltpu.roll(x, shift, axis=axis)


def side_of(channel, from_east, from_west):
    at = EDGE * (channel % SIDE_CHANNELS)
    lane = lax.broadcasted_iota(jnp.int32, from_east.shape, 1)
    return jnp.where(
        lane < LANES // 2, rolled(from_east, -at, 1), rolled(from_west, LANES - EDGE - at, 1)
    )


def reversed_tiles(x):
    back = LANES - 1 - lax.broadcasted_iota(jnp.int32, (x.shape[0], LANES), 1)
    pieces = [
        jnp.take_along_axis(x[:, at : at + LANES], back, axis=1, mode="promise_in_bounds")
        for at in range(0, x.shape[1], LANES)
    ]
    return jnp.concatenate(pieces[::-1], axis=1)


def mirrored(across, kind):
    if kind == 2:
        across = -next_column(across)
    last_row, row_before = across[7:8], across[6:7]
    if kind == 3:
        last_row, row_before = -row_before, -row_before
    upper = lax.broadcasted_iota(jnp.int32, across.shape, 0)
    return jnp.where(upper == 0, last_row, row_before)


def turned_corners(corner_f):
    return [reversed_tiles(corner_f[tile]) for tile in range(corner_f.shape[0])]


def fill_channel(target, k, channel, kind, halo, top, turned_rows, turned_ends):
    from_east, from_west, from_north, from_south, _, corner_n, corner_s, _ = halo
    rows = from_east.shape[1]
    columns = from_north.shape[2]
    tile, group = channel // SIDE_CHANNELS, channel // END_CHANNELS
    spot = EDGE * (channel % END_CHANNELS)
    at = EDGE * (channel % SIDE_CHANNELS)
    tiles = from_east.shape[0]
    target[k, :rows, columns:] = side_of(channel, from_east[tile], from_west[tile])

    def end_of(part, corner, shift):
        return jnp.concatenate(
            [
                rolled(part[group], shift, 0),
                side_of(channel, corner[tile], corner[tiles + tile]),
            ],
            axis=1,
        )

    upper = lax.broadcasted_iota(jnp.int32, (8, columns + LANES), 0)
    lane = lax.broadcasted_iota(jnp.int32, (8, LANES), 1)
    above = end_of(from_north, corner_n, -spot)
    turned_side = jnp.where(
        lane < LANES // 2,
        rolled(turned_ends[tiles + tile], EDGE + at - LANES, 1),
        rolled(turned_ends[tile], at, 1),
    )
    across = mirrored(
        jnp.concatenate([rolled(turned_rows, 8 - EDGE - spot, 0), turned_side], axis=1), kind
    )
    above = jnp.where(top[0] == 1, across, above)
    below = end_of(from_south, corner_s, 8 - EDGE - spot)
    target[k, rows:, :] = jnp.where(upper < 4, above, below)


def fill_wide(targets, sources, depth, halo, top):
    turned_ends = turned_corners(halo[7])
    for kind, (target, source) in enumerate(zip(targets, sources)):
        levels, rows, columns = source.shape
        target[:, :rows, :columns] = source[...]
        turned_rows, group = None, None
        for k in range(levels):
            channel = kind * depth + k
            if channel // END_CHANNELS != group:
                group = channel // END_CHANNELS
                turned_rows = reversed_tiles(halo[4][group])
            fill_channel(target, k, channel, kind, halo, top, turned_rows, turned_ends)


def fill_opens(opens, top, ocean_mask, channel, halo):
    rows, columns = ocean_mask.shape
    opens[0, :rows, :columns] = ocean_mask[...].astype(jnp.float32)
    turned_rows = reversed_tiles(halo[4][channel // END_CHANNELS])
    fill_channel(opens, 0, channel, 0, halo, top, turned_rows, turned_corners(halo[7]))
    here = opens[0]
    opens[1] = here * next_column(here)
    opens[2] = here * next_row(here)
    row_ids = lax.broadcasted_iota(jnp.int32, here.shape, 0)
    opens[3] = jnp.where((row_ids == rows - 1) & (top[0] == 1), 0.0, 1.0)


def mixing_at(t, s, t_below, s_below, mask):
    return (
        mixing_base
        + mixing_extra * jax.nn.sigmoid(4.0 * (density(t, s) - density(t_below, s_below)))
    ) * mask


def step(source, speeds, opens, first, stop, floor, keep, forcing=None, shape=None):
    source_t, source_s = source
    east_all, north_all = speeds
    rows, columns = shape or source_t.shape[1:]

    def kept(x):
        return x[:rows, :columns]

    def weights(speed, open_faces):
        return open_faces * (0.5 * speed + diffuse_rate), open_faces * (0.5 * speed - diffuse_rate)

    def level(k, carry):
        below = jnp.minimum(k + 1, floor)
        pair = (source_t[k], source_s[k])
        mask = opens[0, :rows, :columns]
        t, s = kept(pair[0]), kept(pair[1])
        t_below, s_below = source_t[below, :rows, :columns], source_s[below, :rows, :columns]
        mixing = mixing_at(t, s, t_below, s_below, mask)
        east_near, east_far = weights(east_all[k], opens[1])
        north_near, north_far = weights(north_all[k] * opens[3], opens[2])
        new_gains = []
        for turn, (x, own, x_below) in enumerate(
            ((pair[0], t, t_below), (pair[1], s, s_below))
        ):
            gradient = mixing * (x_below - own)
            east_flux = east_near * x + east_far * next_column(x)
            north_flux = north_near * x + north_far * next_row(x)
            change = (
                kept(pltpu.roll(east_flux, 1, axis=1))
                - kept(east_flux)
                + kept(pltpu.roll(north_flux, 1, axis=0))
                - kept(north_flux)
                + (gradient - carry[turn])
            )
            if forcing is not None:
                change = change + jnp.where(k == 0, kept(forcing[turn]), 0.0)
            keep(turn, k, own + mask * change)
            new_gains.append(gradient)
        return tuple(new_gains)

    if first == 0:
        nothing = jnp.zeros((rows, columns), jnp.float32)
        gains = (nothing, nothing)
    else:
        t, s, t_below, s_below = (
            x[k, :rows, :columns] for k in (first - 1, first) for x in source
        )
        mixing = mixing_at(t, s, t_below, s_below, opens[0, :rows, :columns])
        gains = (mixing * (t_below - t), mixing * (s_below - s))
    lax.fori_loop(first, stop, level, gains)


def turned(x):
    columns = x.shape[1] - LANES
    return jnp.concatenate([reversed_tiles(x[:, :columns]), reversed_tiles(x[:, columns:])], axis=1)


def near_kernel(
    depth,
    top,
    temper,
    saline,
    east,
    north,
    ocean_mask,
    from_east,
    from_west,
    from_north_all,
    from_south_all,
    folded_all,
    corner_n,
    corner_s,
    corner_f,
    remapped,
    remap_sides,
    from_north,
    from_south,
    folded,
    temper_out,
    saline_out,
    surface,
    first_t,
    first_s,
    second_t,
    second_s,
    east_all,
    north_all,
    remap_all,
    opens,
):
    levels, rows, columns = temper.shape
    halo = (
        from_east,
        from_west,
        from_north_all,
        from_south_all,
        folded_all,
        corner_n,
        corner_s,
        corner_f,
    )
    targets, sources = (first_t, first_s, east_all, north_all), (temper, saline, east, north)
    fill_wide(targets, sources, depth, halo, top)
    fill_opens(opens, top, ocean_mask, 4 * depth, halo)
    upper = lax.broadcasted_iota(jnp.int32, (8, columns + LANES), 0)
    remap_all[:, :rows, :columns] = remapped[...]
    remap_all[:, :rows, columns:] = remap_sides[...]
    for field in range(4):
        across = mirrored(turned(folded[field]), field)
        above = jnp.where(top[0] == 1, across, from_north[field])
        remap_all[field, rows:, :] = jnp.where(upper < 4, above, from_south[field])
    east_all[0] = east_all[0] + stress_factor * remap_all[2]
    north_all[0] = north_all[0] + stress_factor * remap_all[3]
    remap_all[0] = heat_factor * remap_all[0]
    remap_all[1] = fresh_factor * remap_all[1]
    forcing = (remap_all[0], remap_all[1])

    def keep_first(target, k, value):
        (second_t, second_s)[target][k] = value

    def keep_last(target, k, value):
        (temper_out, saline_out)[target][k] = value

    speeds = (east_all, north_all)
    step((first_t, first_s), speeds, opens, 0, levels - 1, levels - 1, keep_first, forcing)
    step((second_t, second_s), speeds, opens, 0, levels - 2, levels - 1, keep_last, forcing, (rows, columns))
    mask = opens[0, :rows, :columns]
    t, s = temper_out[0], saline_out[0]
    surface[0] = t * mask
    surface[1] = s * mask
    surface[2] = density(t, s) * mask
    surface[3] = east_all[0, :rows, :columns] * mask


def deep_kernel(
    top,
    temper,
    saline,
    east,
    north,
    ocean_mask,
    from_east,
    from_west,
    from_north,
    from_south,
    folded,
    corner_n,
    corner_s,
    corner_f,
    temper_near,
    saline_near,
    temper_out,
    saline_out,
    first_t,
    first_s,
    second_t,
    second_s,
    east_all,
    north_all,
    opens,
):
    depth, rows, columns = temper.shape
    near = temper_near.shape[0]
    halo = (from_east, from_west, from_north, from_south, folded, corner_n, corner_s, corner_f)
    targets, sources = (first_t, first_s, east_all, north_all), (temper, saline, east, north)
    fill_wide(targets, sources, depth, halo, top)
    fill_opens(opens, top, ocean_mask, 4 * depth, halo)
    temper_out[:near] = temper_near[...]
    saline_out[:near] = saline_near[...]

    def keep_first(target, k, value):
        (second_t, second_s)[target][k] = value

    def keep_last(target, k, value):
        (temper_out, saline_out)[target][k] = value

    speeds = (east_all, north_all)
    step((first_t, first_s), speeds, opens, near - 1, depth, depth - 1, keep_first)
    step((second_t, second_s), speeds, opens, near, depth, depth - 1, keep_last, None, (rows, columns))


def across_fold(count_gx, count_gy):
    return [
        (i * count_gy + count_gy - 1, (count_gx - 1 - i) * count_gy + count_gy - 1)
        for i in range(count_gx)
    ]


def edge_halo(first, last, low, high):
    count_gx, count_gy = lax.axis_size("gx"), lax.axis_size("gy")
    north_of = [(i + 1, i) for i in range(count_gy - 1)]
    south_of = [(i, i + 1) for i in range(count_gy - 1)]
    across = across_fold(count_gx, count_gy)
    from_west = lax.ppermute(last, "gx", [(i, (i + 1) % count_gx) for i in range(count_gx)])
    from_east = lax.ppermute(first, "gx", [((i + 1) % count_gx, i) for i in range(count_gx)])
    from_south = lax.ppermute(high, "gy", south_of)
    from_north = lax.ppermute(low, "gy", north_of)
    folded = lax.ppermute(high, ("gx", "gy"), across)
    corner_low = jnp.concatenate([from_east[:, :8], from_west[:, :8]], axis=0)
    corner_high = jnp.concatenate([from_east[:, -8:], from_west[:, -8:]], axis=0)
    return (
        from_east,
        from_west,
        from_north,
        from_south,
        folded,
        lax.ppermute(corner_low, "gy", north_of),
        lax.ppermute(corner_high, "gy", south_of),
        lax.ppermute(corner_high, ("gx", "gy"), across),
    )


def tile_halo(x):
    rows, columns = x.shape[1:]
    count_gx, count_gy = lax.axis_size("gx"), lax.axis_size("gy")
    from_west = lax.ppermute(
        x[:, :, -LANES:], "gx", [(i, (i + 1) % count_gx) for i in range(count_gx)]
    )
    from_east = lax.ppermute(
        x[:, :, :LANES], "gx", [((i + 1) % count_gx, i) for i in range(count_gx)]
    )
    lane = lax.broadcasted_iota(jnp.int32, from_west.shape, 2)
    sides = jnp.where(lane < LANES // 2, from_east, from_west)
    low = jnp.concatenate([x[:, :8], sides[:, :8]], axis=2)
    high = jnp.concatenate([x[:, -8:], sides[:, -8:]], axis=2)
    from_south = lax.ppermute(high, "gy", [(i, i + 1) for i in range(count_gy - 1)])
    from_north = lax.ppermute(low, "gy", [(i + 1, i) for i in range(count_gy - 1)])
    folded = lax.ppermute(high, ("gx", "gy"), across_fold(count_gx, count_gy))
    return sides, from_north, from_south, folded


def body(
    air_forcing_quantities,
    segment_sea_subdomain,
    overlay_air_element,
    overlay_sea_profile,
    overlay_fraction_share,
    thermal_deviation,
    saltiness_deviation,
    zonal_interface_speed,
    poleward_interface_speed,
    sea_profile_indicator,
):
    devices = lax.axis_size("gx") * lax.axis_size("gy")
    blocks = segment_sea_subdomain.shape[0]
    atm_cells = air_forcing_quantities.shape[1]
    depth, parallels, meridians = thermal_deviation.shape
    capacity = max(2, 2 * blocks // devices)
    slot_count = devices * capacity
    spare = max(LAND_GROUP, PICK_GROUP, capacity)
    f32 = jnp.float32
    air = air_forcing_quantities
    table = jnp.stack([air[0] + air[1] + air[2] + air[3], air[5] - air[4], air[6], air[7]])
    table = table.reshape(4 * atm_cells // LANES, LANES)

    outgoing, home = pl.pallas_call(
        functools.partial(send_kernel, capacity),
        out_shape=(
            jax.ShapeDtypeStruct((slot_count * 5, LANES), f32),
            jax.ShapeDtypeStruct((blocks,), jnp.int32),
        ),
        in_specs=[SMEM, VMEM, VMEM, VMEM, VMEM],
        out_specs=(VMEM, SMEM),
        scratch_shapes=[
            pltpu.SMEM((devices,), jnp.int32),
            pltpu.VMEM((table.shape[0], 2 * LANES), jnp.bfloat16),
            pltpu.VMEM((LANES, LANES), jnp.bfloat16),
        ],
        **gather_kernel_params(10**9),
    )(
        segment_sea_subdomain.reshape(blocks),
        table,
        overlay_air_element,
        overlay_sea_profile,
        overlay_fraction_share,
    )

    arrived = lax.all_to_all(outgoing, ("gx", "gy"), split_axis=0, concat_axis=0, tiled=True)
    channels = 4 * depth + 1
    packed = jax.ShapeDtypeStruct((-(-channels // SIDE_CHANNELS), parallels, LANES), f32)
    stacked = jax.ShapeDtypeStruct((-(-channels // END_CHANNELS), 8, meridians), f32)
    edges = pl.pallas_call(
        edge_kernel,
        out_shape=(packed, packed, stacked, stacked),
        in_specs=[SMEM] + [VMEM] * 5,
        out_specs=(VMEM,) * 4,
        **gather_kernel_params(10**7),
    )(
        home,
        thermal_deviation,
        saltiness_deviation,
        zonal_interface_speed,
        poleward_interface_speed,
        sea_profile_indicator,
    )
    halo = edge_halo(*edges)

    counts = jnp.sum(
        (arrived.reshape(devices, 5, capacity, LANES)[:, 4, :, 0] >= 0).astype(jnp.int32), axis=1
    )
    remapped, places, slots = pl.pallas_call(
        functools.partial(land_kernel, capacity, parallels, meridians),
        out_shape=(
            jax.ShapeDtypeStruct((4 * parallels, meridians), f32),
            jax.ShapeDtypeStruct((slot_count + spare, LANES), f32),
            jax.ShapeDtypeStruct((slot_count + spare + 1,), jnp.int32),
        ),
        in_specs=[SMEM, VMEM],
        out_specs=(VMEM, VMEM, SMEM),
        scratch_shapes=[
            pltpu.VMEM((4, slot_count + spare, LANES), f32),
            pltpu.VMEM((8 * parallels * (meridians // HALF), HALF), f32),
            pltpu.VMEM((HALF, LANES), jnp.bfloat16),
        ],
        **gather_kernel_params(2 * 10**10),
    )(counts, arrived)
    remapped = remapped.reshape(4, parallels, meridians)
    around = tile_halo(remapped)

    top = (lax.axis_index("gy") == lax.axis_size("gy") - 1).astype(jnp.int32).reshape(1)
    wide = (parallels + 8, meridians + LANES)
    near, levels = 2, 4
    first_levels = pl.BlockSpec((levels, parallels, meridians), lambda i: (0, 0, 0))
    cube = jax.ShapeDtypeStruct((depth, parallels, meridians), f32)
    slab = jax.ShapeDtypeStruct((near, parallels, meridians), f32)
    temper_near, saline_near, surface = pl.pallas_call(
        functools.partial(near_kernel, depth),
        grid=(1,),
        out_shape=(slab, slab, jax.ShapeDtypeStruct((4, parallels, meridians), f32)),
        in_specs=[SMEM] + [first_levels] * 4 + [VMEM] * 14,
        out_specs=(VMEM, VMEM, VMEM),
        scratch_shapes=[pltpu.VMEM((levels,) + wide, f32)] * 6
        + [pltpu.VMEM((4,) + wide, f32)] * 2,
        **gather_kernel_params(10**8),
    )(
        top,
        thermal_deviation,
        saltiness_deviation,
        zonal_interface_speed,
        poleward_interface_speed,
        sea_profile_indicator,
        *halo,
        remapped,
        *around,
    )

    picked = pl.pallas_call(
        functools.partial(pick_kernel, capacity, parallels, meridians),
        out_shape=jax.ShapeDtypeStruct((slot_count * 4, LANES), f32),
        in_specs=[SMEM, VMEM, VMEM],
        out_specs=VMEM,
        scratch_shapes=[
            pltpu.VMEM((8 * parallels * (meridians // HALF), HALF), jnp.bfloat16),
            pltpu.VMEM((HALF, LANES), jnp.bfloat16),
            pltpu.VMEM(((slot_count + capacity) * 4, LANES), f32),
        ],
        **gather_kernel_params(2 * 10**10),
    )(slots, surface.reshape(4 * parallels, meridians), places)
    picked, top = lax.optimization_barrier((picked, top))
    returned = lax.all_to_all(picked, ("gx", "gy"), split_axis=0, concat_axis=0, tiled=True)
    temper, saline = pl.pallas_call(
        deep_kernel,
        out_shape=(cube, cube),
        in_specs=[SMEM] + [VMEM] * 15,
        out_specs=(VMEM, VMEM),
        scratch_shapes=[pltpu.VMEM((depth,) + wide, f32)] * 6 + [pltpu.VMEM((4,) + wide, f32)],
        **gather_kernel_params(10**9),
    )(
        top,
        thermal_deviation,
        saltiness_deviation,
        zonal_interface_speed,
        poleward_interface_speed,
        sea_profile_indicator,
        *halo,
        temper_near,
        saline_near,
    )
    back_fields = pl.pallas_call(
        functools.partial(back_kernel, capacity),
        out_shape=jax.ShapeDtypeStruct((4 * atm_cells // LANES, LANES), f32),
        in_specs=[SMEM, VMEM, VMEM, VMEM],
        out_specs=VMEM,
        scratch_shapes=[
            pltpu.VMEM((8 * atm_cells // LANES, LANES), f32),
            pltpu.VMEM((LANES, LANES), jnp.bfloat16),
        ],
        **gather_kernel_params(2 * 10**9),
    )(home, returned, overlay_air_element, overlay_fraction_share)
    return temper, saline, back_fields.reshape(4, atm_cells)


def solution(mesh):
    return jax.shard_map(
        body,
        mesh=mesh,
        in_specs=(
            P(None, ("gx", "gy")),
            P(("gx", "gy"), None),
            P(("gx", "gy"), None),
            P(("gx", "gy"), None),
            P(("gx", "gy"), None),
            P(None, "gy", "gx"),
            P(None, "gy", "gx"),
            P(None, "gy", "gx"),
            P(None, "gy", "gx"),
            P("gy", "gx"),
        ),
        out_specs=(P(None, "gy", "gx"), P(None, "gy", "gx"), P(None, ("gx", "gy"))),
        check_vma=False,
    )
```

```python
import functools

import jax
import jax.numpy as jnp
from jax import lax
from jax.experimental import pallas as pl
from jax.experimental.pallas import tpu as pltpu
from jax.sharding import PartitionSpec as P

diffuse_rate = 0.12
mixing_base = 0.02
mixing_extra = 0.2
heat_factor = 0.5
fresh_factor = 0.5
stress_factor = 0.3

LANES = 128
SEND_GROUP = 32
LAND_GROUP = 16
PICK_GROUP = 16
BACK_GROUP = 32
HALF = 256
PAIR = 2
VMEM_BYTES = 48 * 1024 * 1024
CONTRACT_LAST = (((1,), (1,)), ((), ()))

SMEM = pl.BlockSpec(memory_space=pltpu.SMEM)
VMEM = pl.BlockSpec(memory_space=pltpu.VMEM)


def density(temper_field, saline_field):
    return (
        -0.2 * temper_field
        - 0.05 * temper_field * temper_field
        + 0.8 * saline_field
        + 0.03 * temper_field * saline_field
    )


def two_terms(values):
    high = values.astype(jnp.bfloat16)
    return high, (values - high.astype(jnp.float32)).astype(jnp.bfloat16)


def narrow(places):
    return places.astype(jnp.float32).astype(jnp.bfloat16)


def number_rows(numbers):
    numbers[...] = narrow(lax.broadcasted_iota(jnp.int32, numbers.shape, 0))


def one_hot(places, numbers):
    return jnp.where(numbers == places, jnp.bfloat16(1), jnp.bfloat16(0))


def spread(rows_of, terms, numbers):
    hit = numbers == rows_of
    return jnp.concatenate([jnp.where(hit, term, jnp.bfloat16(0)) for term in terms], axis=0)


def halves_of(address, parallels, meridians):
    shift = meridians.bit_length() - 1
    column = address & (meridians - 1)
    row = (address >> shift) + parallels * (column // HALF)
    return jnp.where(address < 0, -1, row), column % HALF


def picked_rows(rows_of, table, fields, count):
    rows = lax.broadcasted_iota(jnp.int32, (count, rows_of.shape[1]), 0)
    hit = rows == rows_of
    return [
        jnp.sum(
            jnp.where(hit, table[field * count : (field + 1) * count], 0.0), axis=0, keepdims=True
        )
        for field in range(fields)
    ]


def send_kernel(
    half,
    subdomain,
    table,
    element,
    profile,
    share,
    early,
    late,
    home,
    tally,
    split_table,
    numbers,
    out,
):
    devices = tally.shape[0]
    blocks = element.shape[0]
    high_rows = table.shape[0] // 4

    def clear(i, carry):
        tally[i] = 0
        return carry

    lax.fori_loop(0, devices, clear, 0)
    number_rows(numbers)
    out[...] = jnp.full(out.shape, -1.0, jnp.float32)
    high, low = two_terms(table[...])
    split_table[:, :LANES] = high
    split_table[:, LANES:] = low

    def group(g, carry):
        base = pl.multiple_of(g * SEND_GROUP, SEND_GROUP)
        cells = element[pl.ds(base, SEND_GROUP), :]
        near = narrow(cells & (LANES - 1))
        far = cells >> 7
        address = profile[pl.ds(base, SEND_GROUP), :].astype(jnp.float32)
        weight = share[pl.ds(base, SEND_GROUP), :]
        for first in range(0, SEND_GROUP, PAIR):
            names = range(first, first + PAIR)
            hot = jnp.concatenate([one_hot(near[b : b + 1], numbers[...]) for b in names], axis=1)
            found = jnp.dot(
                split_table[...],
                jnp.concatenate([hot, hot], axis=0),
                preferred_element_type=jnp.float32,
            )
            far_row = jnp.concatenate([far[b : b + 1] for b in names], axis=1)
            values = picked_rows(far_row, found, 4, high_rows)
            for turn, b in enumerate(names):
                tile = subdomain[base + b]
                place = tally[tile]
                tally[tile] = place + 1
                part = place // half
                spot = (part * devices + tile) * half
                home[base + b] = 4 * spot + place - part * half
                row = 5 * spot + place - part * half
                for field in range(4):
                    out[pl.ds(row + field * half, 1), :] = (
                        values[field][:, turn * LANES : (turn + 1) * LANES] * weight[b : b + 1]
                    )
                out[pl.ds(row + 4 * half, 1), :] = address[b : b + 1]
        return carry

    lax.fori_loop(0, blocks // SEND_GROUP, group, 0)
    early[...] = out[: early.shape[0]]
    late[...] = out[early.shape[0] :]


def gather_kernel_params(flops):
    return dict(
        compiler_params=pltpu.CompilerParams(vmem_limit_bytes=VMEM_BYTES),
        cost_estimate=pl.CostEstimate(flops=flops, bytes_accessed=4_000_000, transcendentals=0),
    )


def land_kernel(
    capacity,
    parallels,
    meridians,
    counts,
    arrived,
    remapped,
    places,
    slots,
    values,
    total,
    numbers,
):
    sources = counts.shape[0]
    last = slots.shape[0] - 1
    long_rows = parallels * (meridians // HALF)
    places[...] = jnp.full(places.shape, -1.0, jnp.float32)
    total[...] = jnp.zeros(total.shape, jnp.float32)

    def from_source(source, count):
        row = source * (5 * capacity)
        for field in range(4):
            values[field, pl.ds(count, capacity), :] = arrived[
                pl.ds(row + field * capacity, capacity), :
            ]
        places[pl.ds(count, capacity), :] = arrived[pl.ds(row + 4 * capacity, capacity), :]
        for place in range(capacity):
            slots[count + place] = source * (4 * capacity) + place
        return count + counts[source]

    filled = lax.fori_loop(0, sources, from_source, 0)
    slots[last] = filled
    for extra in range(LAND_GROUP):
        slots[filled + extra] = sources * (4 * capacity)
    number_rows(numbers)

    def group(g, carry):
        base = pl.multiple_of(g * LAND_GROUP, LAND_GROUP)
        address = places[pl.ds(base, LAND_GROUP), :].astype(jnp.int32)
        row, column = halves_of(address, parallels, meridians)
        row, column = narrow(row), narrow(column)
        split = [two_terms(values[field, pl.ds(base, LAND_GROUP), :]) for field in range(4)]
        terms = [split[field][term] for term in range(2) for field in range(4)]
        names = range(LAND_GROUP)
        left = jnp.concatenate(
            [
                spread(row[b : b + 1], [term[b : b + 1] for term in terms], numbers[:long_rows])
                for b in names
            ],
            axis=1,
        )
        right = jnp.concatenate([one_hot(column[b : b + 1], numbers[...]) for b in names], axis=1)
        total[...] += lax.dot_general(
            left, right, CONTRACT_LAST, preferred_element_type=jnp.float32
        )
        return carry

    lax.fori_loop(0, (filled + LAND_GROUP - 1) // LAND_GROUP, group, 0)
    for field in range(4):
        for part in range(meridians // HALF):
            at = field * long_rows + part * parallels
            remapped[field * parallels : (field + 1) * parallels, part * HALF : (part + 1) * HALF] = (
                total[at : at + parallels]
                + total[4 * long_rows + at : 4 * long_rows + at + parallels]
            )


def pick_kernel(capacity, parallels, meridians, slots, surface, places, out, split_table, numbers, found_rows):
    last = slots.shape[0] - 1
    long_rows = parallels * (meridians // HALF)
    half = 4 * long_rows
    filled = slots[last]
    for field in range(4):
        for part in range(meridians // HALF):
            high, low = two_terms(
                surface[
                    field * parallels : (field + 1) * parallels, part * HALF : (part + 1) * HALF
                ]
            )
            at = field * long_rows + part * parallels
            split_table[at : at + parallels] = high
            split_table[half + at : half + at + parallels] = low
    found_rows[...] = jnp.zeros(found_rows.shape, jnp.float32)
    number_rows(numbers)

    def group(g, carry):
        base = pl.multiple_of(g * PICK_GROUP, PICK_GROUP)
        address = places[pl.ds(base, PICK_GROUP), :].astype(jnp.int32)
        row, column = halves_of(address, parallels, meridians)
        column = narrow(column)
        for first in range(0, PICK_GROUP, PAIR):
            names = range(first, first + PAIR)
            hot = jnp.concatenate([one_hot(column[b : b + 1], numbers[...]) for b in names], axis=1)
            found = jnp.dot(split_table[...], hot, preferred_element_type=jnp.float32)
            found = found[:half] + found[half:]
            wide_row = jnp.concatenate([row[b : b + 1] for b in names], axis=1)
            values = picked_rows(wide_row, found, 4, long_rows)
            for turn, b in enumerate(names):
                target = slots[base + b]
                for field in range(4):
                    found_rows[pl.ds(target + field * capacity, 1), :] = values[field][
                        :, turn * LANES : (turn + 1) * LANES
                    ]
        return carry

    lax.fori_loop(0, (filled + PICK_GROUP - 1) // PICK_GROUP, group, 0)
    out[...] = found_rows[: out.shape[0]]


def back_kernel(half, home, early, late, element, share, out, total, numbers, returned):
    blocks = element.shape[0]
    high_rows = out.shape[0] // 4
    total[...] = jnp.zeros(total.shape, jnp.float32)
    number_rows(numbers)
    returned[: early.shape[0]] = early[...]
    returned[early.shape[0] :] = late[...]

    def group(g, carry):
        base = pl.multiple_of(g * BACK_GROUP, BACK_GROUP)
        cells = element[pl.ds(base, BACK_GROUP), :]
        near = narrow(cells & (LANES - 1))
        far = narrow(cells >> 7)
        weight = share[pl.ds(base, BACK_GROUP), :]
        names = range(BACK_GROUP)
        lefts = []
        for b in names:
            row = home[base + b]
            split = [
                two_terms(returned[pl.ds(row + field * half, 1), :] * weight[b : b + 1])
                for field in range(4)
            ]
            terms = [split[field][term] for term in range(2) for field in range(4)]
            lefts.append(spread(far[b : b + 1], terms, numbers[:high_rows]))
        left = jnp.concatenate(lefts, axis=1)
        right = jnp.concatenate([one_hot(near[b : b + 1], numbers[...]) for b in names], axis=1)
        total[...] += lax.dot_general(
            left, right, CONTRACT_LAST, preferred_element_type=jnp.float32
        )
        return carry

    lax.fori_loop(0, blocks // BACK_GROUP, group, 0)
    out[...] = total[: 4 * high_rows] + total[4 * high_rows :]


def next_column(x):
    return pltpu.roll(x, x.shape[1] - 1, axis=1)


def next_row(x):
    return pltpu.roll(x, x.shape[0] - 1, axis=0)


EDGE = 2
SIDE_CHANNELS = LANES // EDGE
END_CHANNELS = 8 // EDGE


def edge_kernel(home, temper, saline, east, north, ocean_mask, first, last, low, high):
    depth, rows, columns = temper.shape
    lane = lax.broadcasted_iota(jnp.int32, (rows, LANES), 1)
    heads, tails = [None] * first.shape[0], [None] * first.shape[0]
    mask = ocean_mask[...].astype(jnp.float32)
    for c in range(4 * depth + 1):
        if c < 4 * depth:
            source, k = (temper, saline, east, north)[c // depth], c % depth
            left, right = source[k, :, :LANES], source[k, :, columns - LANES :]
            top_rows, end_rows = source[k, :EDGE, :], source[k, rows - EDGE :, :]
        else:
            left, right = mask[:, :LANES], mask[:, columns - LANES :]
            top_rows, end_rows = mask[:EDGE], mask[rows - EDGE :]
        tile, at = c // SIDE_CHANNELS, EDGE * (c % SIDE_CHANNELS)
        here = (lane >= at) & (lane < at + EDGE)
        head = left if at == 0 else pltpu.roll(left, at, axis=1)
        tail = pltpu.roll(right, (at + EDGE) % LANES, axis=1) if at + EDGE < LANES else right
        heads[tile] = head if at == 0 else jnp.where(here, head, heads[tile])
        tails[tile] = tail if at == 0 else jnp.where(here, tail, tails[tile])
        spot = EDGE * (c % END_CHANNELS)
        low[c // END_CHANNELS, spot : spot + EDGE, :] = top_rows
        high[c // END_CHANNELS, spot : spot + EDGE, :] = end_rows
    for c in range(4 * depth + 1, END_CHANNELS * low.shape[0]):
        spot = EDGE * (c % END_CHANNELS)
        low[c // END_CHANNELS, spot : spot + EDGE, :] = jnp.zeros((EDGE, columns), jnp.float32)
        high[c // END_CHANNELS, spot : spot + EDGE, :] = jnp.zeros((EDGE, columns), jnp.float32)
    for tile in range(first.shape[0]):
        first[tile] = heads[tile]
        last[tile] = tails[tile]


def rolled(x, shift, axis):
    shift = shift % x.shape[axis]
    return x if shift == 0 else pltpu.roll(x, shift, axis=axis)


def side_of(channel, from_east, from_west):
    at = EDGE * (channel % SIDE_CHANNELS)
    lane = lax.broadcasted_iota(jnp.int32, from_east.shape, 1)
    return jnp.where(
        lane < LANES // 2, rolled(from_east, -at, 1), rolled(from_west, LANES - EDGE - at, 1)
    )


def reversed_tiles(x):
    back = LANES - 1 - lax.broadcasted_iota(jnp.int32, (x.shape[0], LANES), 1)
    pieces = [
        jnp.take_along_axis(x[:, at : at + LANES], back, axis=1, mode="promise_in_bounds")
        for at in range(0, x.shape[1], LANES)
    ]
    return jnp.concatenate(pieces[::-1], axis=1)


def mirrored(across, kind):
    if kind == 2:
        across = -next_column(across)
    last_row, row_before = across[7:8], across[6:7]
    if kind == 3:
        last_row, row_before = -row_before, -row_before
    upper = lax.broadcasted_iota(jnp.int32, across.shape, 0)
    return jnp.where(upper == 0, last_row, row_before)


def turned_corners(corner_f):
    return [reversed_tiles(corner_f[tile]) for tile in range(corner_f.shape[0])]


def fill_channel(target, k, channel, kind, halo, top, turned_rows, turned_ends):
    from_east, from_west, from_north, from_south, _, corner_n, corner_s, _ = halo
    rows = from_east.shape[1]
    columns = from_north.shape[2]
    tile, group = channel // SIDE_CHANNELS, channel // END_CHANNELS
    spot = EDGE * (channel % END_CHANNELS)
    at = EDGE * (channel % SIDE_CHANNELS)
    tiles = from_east.shape[0]
    target[k, :rows, columns:] = side_of(channel, from_east[tile], from_west[tile])

    def end_of(part, corner, shift):
        return jnp.concatenate(
            [
                rolled(part[group], shift, 0),
                side_of(channel, corner[tile], corner[tiles + tile]),
            ],
            axis=1,
        )

    upper = lax.broadcasted_iota(jnp.int32, (8, columns + LANES), 0)
    lane = lax.broadcasted_iota(jnp.int32, (8, LANES), 1)
    above = end_of(from_north, corner_n, -spot)
    turned_side = jnp.where(
        lane < LANES // 2,
        rolled(turned_ends[tiles + tile], EDGE + at - LANES, 1),
        rolled(turned_ends[tile], at, 1),
    )
    across = mirrored(
        jnp.concatenate([rolled(turned_rows, 8 - EDGE - spot, 0), turned_side], axis=1), kind
    )
    above = jnp.where(top[0] == 1, across, above)
    below = end_of(from_south, corner_s, 8 - EDGE - spot)
    target[k, rows:, :] = jnp.where(upper < 4, above, below)


def fill_wide(targets, sources, depth, halo, top):
    turned_ends = turned_corners(halo[7])
    for kind, (target, source) in enumerate(zip(targets, sources)):
        levels, rows, columns = source.shape
        target[:, :rows, :columns] = source[...]
        turned_rows, group = None, None
        for k in range(levels):
            channel = kind * depth + k
            if channel // END_CHANNELS != group:
                group = channel // END_CHANNELS
                turned_rows = reversed_tiles(halo[4][group])
            fill_channel(target, k, channel, kind, halo, top, turned_rows, turned_ends)


def fill_opens(opens, top, ocean_mask, channel, halo):
    rows, columns = ocean_mask.shape
    opens[0, :rows, :columns] = ocean_mask[...].astype(jnp.float32)
    turned_rows = reversed_tiles(halo[4][channel // END_CHANNELS])
    fill_channel(opens, 0, channel, 0, halo, top, turned_rows, turned_corners(halo[7]))
    here = opens[0]
    opens[1] = here * next_column(here)
    opens[2] = here * next_row(here)
    row_ids = lax.broadcasted_iota(jnp.int32, here.shape, 0)
    opens[3] = jnp.where((row_ids == rows - 1) & (top[0] == 1), 0.0, 1.0)


def mixing_at(t, s, t_below, s_below, mask):
    return (
        mixing_base
        + mixing_extra * jax.nn.sigmoid(4.0 * (density(t, s) - density(t_below, s_below)))
    ) * mask


def step(source, speeds, opens, first, stop, floor, keep, forcing=None, shape=None):
    source_t, source_s = source
    east_all, north_all = speeds
    rows, columns = shape or source_t.shape[1:]

    def kept(x):
        return x[:rows, :columns]

    def weights(speed, open_faces):
        return open_faces * (0.5 * speed + diffuse_rate), open_faces * (0.5 * speed - diffuse_rate)

    def level(k, carry):
        below = jnp.minimum(k + 1, floor)
        pair = (source_t[k], source_s[k])
        mask = opens[0, :rows, :columns]
        t, s = kept(pair[0]), kept(pair[1])
        t_below, s_below = source_t[below, :rows, :columns], source_s[below, :rows, :columns]
        mixing = mixing_at(t, s, t_below, s_below, mask)
        east_near, east_far = weights(east_all[k], opens[1])
        north_near, north_far = weights(north_all[k] * opens[3], opens[2])
        new_gains = []
        for turn, (x, own, x_below) in enumerate(
            ((pair[0], t, t_below), (pair[1], s, s_below))
        ):
            gradient = mixing * (x_below - own)
            east_flux = east_near * x + east_far * next_column(x)
            north_flux = north_near * x + north_far * next_row(x)
            change = (
                kept(pltpu.roll(east_flux, 1, axis=1))
                - kept(east_flux)
                + kept(pltpu.roll(north_flux, 1, axis=0))
                - kept(north_flux)
                + (gradient - carry[turn])
            )
            if forcing is not None:
                change = change + jnp.where(k == 0, kept(forcing[turn]), 0.0)
            keep(turn, k, own + mask * change)
            new_gains.append(gradient)
        return tuple(new_gains)

    if first == 0:
        nothing = jnp.zeros((rows, columns), jnp.float32)
        gains = (nothing, nothing)
    else:
        t, s, t_below, s_below = (
            x[k, :rows, :columns] for k in (first - 1, first) for x in source
        )
        mixing = mixing_at(t, s, t_below, s_below, opens[0, :rows, :columns])
        gains = (mixing * (t_below - t), mixing * (s_below - s))
    lax.fori_loop(first, stop, level, gains)


def turned(x):
    columns = x.shape[1] - LANES
    return jnp.concatenate([reversed_tiles(x[:, :columns]), reversed_tiles(x[:, columns:])], axis=1)


def near_kernel(
    depth,
    top,
    temper,
    saline,
    east,
    north,
    ocean_mask,
    from_east,
    from_west,
    from_north_all,
    from_south_all,
    folded_all,
    corner_n,
    corner_s,
    corner_f,
    remapped,
    remap_sides,
    from_north,
    from_south,
    folded,
    temper_out,
    saline_out,
    surface,
    first_t,
    first_s,
    second_t,
    second_s,
    east_all,
    north_all,
    remap_all,
    opens,
):
    levels, rows, columns = temper.shape
    halo = (
        from_east,
        from_west,
        from_north_all,
        from_south_all,
        folded_all,
        corner_n,
        corner_s,
        corner_f,
    )
    targets, sources = (first_t, first_s, east_all, north_all), (temper, saline, east, north)
    fill_wide(targets, sources, depth, halo, top)
    fill_opens(opens, top, ocean_mask, 4 * depth, halo)
    upper = lax.broadcasted_iota(jnp.int32, (8, columns + LANES), 0)
    remap_all[:, :rows, :columns] = remapped[...]
    remap_all[:, :rows, columns:] = remap_sides[...]
    for field in range(4):
        across = mirrored(turned(folded[field]), field)
        above = jnp.where(top[0] == 1, across, from_north[field])
        remap_all[field, rows:, :] = jnp.where(upper < 4, above, from_south[field])
    east_all[0] = east_all[0] + stress_factor * remap_all[2]
    north_all[0] = north_all[0] + stress_factor * remap_all[3]
    remap_all[0] = heat_factor * remap_all[0]
    remap_all[1] = fresh_factor * remap_all[1]
    forcing = (remap_all[0], remap_all[1])

    def keep_first(target, k, value):
        (second_t, second_s)[target][k] = value

    def keep_last(target, k, value):
        (temper_out, saline_out)[target][k] = value

    speeds = (east_all, north_all)
    step((first_t, first_s), speeds, opens, 0, levels - 1, levels - 1, keep_first, forcing)
    step((second_t, second_s), speeds, opens, 0, levels - 2, levels - 1, keep_last, forcing, (rows, columns))
    mask = opens[0, :rows, :columns]
    t, s = temper_out[0], saline_out[0]
    surface[0] = t * mask
    surface[1] = s * mask
    surface[2] = density(t, s) * mask
    surface[3] = east_all[0, :rows, :columns] * mask


def deep_kernel(
    top,
    temper,
    saline,
    east,
    north,
    ocean_mask,
    from_east,
    from_west,
    from_north,
    from_south,
    folded,
    corner_n,
    corner_s,
    corner_f,
    temper_near,
    saline_near,
    temper_out,
    saline_out,
    first_t,
    first_s,
    second_t,
    second_s,
    east_all,
    north_all,
    opens,
):
    depth, rows, columns = temper.shape
    near = temper_near.shape[0]
    halo = (from_east, from_west, from_north, from_south, folded, corner_n, corner_s, corner_f)
    targets, sources = (first_t, first_s, east_all, north_all), (temper, saline, east, north)
    fill_wide(targets, sources, depth, halo, top)
    fill_opens(opens, top, ocean_mask, 4 * depth, halo)
    temper_out[:near] = temper_near[...]
    saline_out[:near] = saline_near[...]

    def keep_first(target, k, value):
        (second_t, second_s)[target][k] = value

    def keep_last(target, k, value):
        (temper_out, saline_out)[target][k] = value

    speeds = (east_all, north_all)
    step((first_t, first_s), speeds, opens, near - 1, depth, depth - 1, keep_first)
    step((second_t, second_s), speeds, opens, near, depth, depth - 1, keep_last, None, (rows, columns))


def across_fold(count_gx, count_gy):
    return [
        (i * count_gy + count_gy - 1, (count_gx - 1 - i) * count_gy + count_gy - 1)
        for i in range(count_gx)
    ]


def edge_halo(first, last, low, high):
    count_gx, count_gy = lax.axis_size("gx"), lax.axis_size("gy")
    north_of = [(i + 1, i) for i in range(count_gy - 1)]
    south_of = [(i, i + 1) for i in range(count_gy - 1)]
    across = across_fold(count_gx, count_gy)
    from_west = lax.ppermute(last, "gx", [(i, (i + 1) % count_gx) for i in range(count_gx)])
    from_east = lax.ppermute(first, "gx", [((i + 1) % count_gx, i) for i in range(count_gx)])
    from_south = lax.ppermute(high, "gy", south_of)
    from_north = lax.ppermute(low, "gy", north_of)
    folded = lax.ppermute(high, ("gx", "gy"), across)
    corner_low = jnp.concatenate([from_east[:, :8], from_west[:, :8]], axis=0)
    corner_high = jnp.concatenate([from_east[:, -8:], from_west[:, -8:]], axis=0)
    return (
        from_east,
        from_west,
        from_north,
        from_south,
        folded,
        lax.ppermute(corner_low, "gy", north_of),
        lax.ppermute(corner_high, "gy", south_of),
        lax.ppermute(corner_high, ("gx", "gy"), across),
    )


def tile_halo(x):
    rows, columns = x.shape[1:]
    count_gx, count_gy = lax.axis_size("gx"), lax.axis_size("gy")
    from_west = lax.ppermute(
        x[:, :, -LANES:], "gx", [(i, (i + 1) % count_gx) for i in range(count_gx)]
    )
    from_east = lax.ppermute(
        x[:, :, :LANES], "gx", [((i + 1) % count_gx, i) for i in range(count_gx)]
    )
    lane = lax.broadcasted_iota(jnp.int32, from_west.shape, 2)
    sides = jnp.where(lane < LANES // 2, from_east, from_west)
    low = jnp.concatenate([x[:, :8], sides[:, :8]], axis=2)
    high = jnp.concatenate([x[:, -8:], sides[:, -8:]], axis=2)
    from_south = lax.ppermute(high, "gy", [(i, i + 1) for i in range(count_gy - 1)])
    from_north = lax.ppermute(low, "gy", [(i + 1, i) for i in range(count_gy - 1)])
    folded = lax.ppermute(high, ("gx", "gy"), across_fold(count_gx, count_gy))
    return sides, from_north, from_south, folded


def body(
    air_forcing_quantities,
    segment_sea_subdomain,
    overlay_air_element,
    overlay_sea_profile,
    overlay_fraction_share,
    thermal_deviation,
    saltiness_deviation,
    zonal_interface_speed,
    poleward_interface_speed,
    sea_profile_indicator,
):
    devices = lax.axis_size("gx") * lax.axis_size("gy")
    blocks = segment_sea_subdomain.shape[0]
    atm_cells = air_forcing_quantities.shape[1]
    depth, parallels, meridians = thermal_deviation.shape
    capacity = max(2, 2 * blocks // devices)
    half = -(-capacity // 2)
    slot_count = devices * half
    spare = max(LAND_GROUP, PICK_GROUP, half)
    f32 = jnp.float32
    air = air_forcing_quantities
    table = jnp.stack([air[0] + air[1] + air[2] + air[3], air[5] - air[4], air[6], air[7]])
    table = table.reshape(4 * atm_cells // LANES, LANES)

    outgoing = jax.ShapeDtypeStruct((slot_count * 5, LANES), f32)
    early, late, home = pl.pallas_call(
        functools.partial(send_kernel, half),
        out_shape=(
            outgoing,
            outgoing,
            jax.ShapeDtypeStruct((blocks,), jnp.int32),
        ),
        in_specs=[SMEM, VMEM, VMEM, VMEM, VMEM],
        out_specs=(VMEM, VMEM, SMEM),
        scratch_shapes=[
            pltpu.SMEM((devices,), jnp.int32),
            pltpu.VMEM((table.shape[0], 2 * LANES), jnp.bfloat16),
            pltpu.VMEM((LANES, LANES), jnp.bfloat16),
            pltpu.VMEM((slot_count * 10, LANES), f32),
        ],
        **gather_kernel_params(10**9),
    )(
        segment_sea_subdomain.reshape(blocks),
        table,
        overlay_air_element,
        overlay_sea_profile,
        overlay_fraction_share,
    )

    arrivals = [
        lax.all_to_all(x, ("gx", "gy"), split_axis=0, concat_axis=0, tiled=True)
        for x in (early, late)
    ]
    channels = 4 * depth + 1
    packed = jax.ShapeDtypeStruct((-(-channels // SIDE_CHANNELS), parallels, LANES), f32)
    stacked = jax.ShapeDtypeStruct((-(-channels // END_CHANNELS), 8, meridians), f32)
    edges = pl.pallas_call(
        edge_kernel,
        out_shape=(packed, packed, stacked, stacked),
        in_specs=[SMEM] + [VMEM] * 5,
        out_specs=(VMEM,) * 4,
        **gather_kernel_params(10**7),
    )(
        home,
        thermal_deviation,
        saltiness_deviation,
        zonal_interface_speed,
        poleward_interface_speed,
        sea_profile_indicator,
    )
    halo = edge_halo(*edges)

    landed = []
    for arrived in arrivals:
        counts = jnp.sum(
            (arrived.reshape(devices, 5, half, LANES)[:, 4, :, 0] >= 0).astype(jnp.int32), axis=1
        )
        landed.append(
            pl.pallas_call(
                functools.partial(land_kernel, half, parallels, meridians),
                out_shape=(
                    jax.ShapeDtypeStruct((4 * parallels, meridians), f32),
                    jax.ShapeDtypeStruct((slot_count + spare, LANES), f32),
                    jax.ShapeDtypeStruct((slot_count + spare + 1,), jnp.int32),
                ),
                in_specs=[SMEM, VMEM],
                out_specs=(VMEM, VMEM, SMEM),
                scratch_shapes=[
                    pltpu.VMEM((4, slot_count + spare, LANES), f32),
                    pltpu.VMEM((8 * parallels * (meridians // HALF), HALF), f32),
                    pltpu.VMEM((HALF, LANES), jnp.bfloat16),
                ],
                **gather_kernel_params(10**10),
            )(counts, arrived)
        )
    remapped = landed[0][0] + landed[1][0]
    remapped = remapped.reshape(4, parallels, meridians)
    around = tile_halo(remapped)

    top = (lax.axis_index("gy") == lax.axis_size("gy") - 1).astype(jnp.int32).reshape(1)
    wide = (parallels + 8, meridians + LANES)
    near, levels = 2, 4
    first_levels = pl.BlockSpec((levels, parallels, meridians), lambda i: (0, 0, 0))
    cube = jax.ShapeDtypeStruct((depth, parallels, meridians), f32)
    slab = jax.ShapeDtypeStruct((near, parallels, meridians), f32)
    temper_near, saline_near, surface = pl.pallas_call(
        functools.partial(near_kernel, depth),
        grid=(1,),
        out_shape=(slab, slab, jax.ShapeDtypeStruct((4, parallels, meridians), f32)),
        in_specs=[SMEM] + [first_levels] * 4 + [VMEM] * 14,
        out_specs=(VMEM, VMEM, VMEM),
        scratch_shapes=[pltpu.VMEM((levels,) + wide, f32)] * 6
        + [pltpu.VMEM((4,) + wide, f32)] * 2,
        **gather_kernel_params(10**8),
    )(
        top,
        thermal_deviation,
        saltiness_deviation,
        zonal_interface_speed,
        poleward_interface_speed,
        sea_profile_indicator,
        *halo,
        remapped,
        *around,
    )

    returns = []
    for _, places, slots in landed:
        picked = pl.pallas_call(
            functools.partial(pick_kernel, half, parallels, meridians),
            out_shape=jax.ShapeDtypeStruct((slot_count * 4, LANES), f32),
            in_specs=[SMEM, VMEM, VMEM],
            out_specs=VMEM,
            scratch_shapes=[
                pltpu.VMEM((8 * parallels * (meridians // HALF), HALF), jnp.bfloat16),
                pltpu.VMEM((HALF, LANES), jnp.bfloat16),
                pltpu.VMEM(((slot_count + half) * 4, LANES), f32),
            ],
            **gather_kernel_params(10**10),
        )(slots, surface.reshape(4 * parallels, meridians), places)
        picked, top = lax.optimization_barrier((picked, top))
        returns.append(
            lax.all_to_all(picked, ("gx", "gy"), split_axis=0, concat_axis=0, tiled=True)
        )
    temper, saline = pl.pallas_call(
        deep_kernel,
        out_shape=(cube, cube),
        in_specs=[SMEM] + [VMEM] * 15,
        out_specs=(VMEM, VMEM),
        scratch_shapes=[pltpu.VMEM((depth,) + wide, f32)] * 6 + [pltpu.VMEM((4,) + wide, f32)],
        **gather_kernel_params(10**9),
    )(
        top,
        thermal_deviation,
        saltiness_deviation,
        zonal_interface_speed,
        poleward_interface_speed,
        sea_profile_indicator,
        *halo,
        temper_near,
        saline_near,
    )
    back_fields = pl.pallas_call(
        functools.partial(back_kernel, half),
        out_shape=jax.ShapeDtypeStruct((4 * atm_cells // LANES, LANES), f32),
        in_specs=[SMEM, VMEM, VMEM, VMEM, VMEM],
        out_specs=VMEM,
        scratch_shapes=[
            pltpu.VMEM((8 * atm_cells // LANES, LANES), f32),
            pltpu.VMEM((LANES, LANES), jnp.bfloat16),
            pltpu.VMEM((slot_count * 8, LANES), f32),
        ],
        **gather_kernel_params(2 * 10**9),
    )(home, *returns, overlay_air_element, overlay_fraction_share)
    return temper, saline, back_fields.reshape(4, atm_cells)


def solution(mesh):
    return jax.shard_map(
        body,
        mesh=mesh,
        in_specs=(
            P(None, ("gx", "gy")),
            P(("gx", "gy"), None),
            P(("gx", "gy"), None),
            P(("gx", "gy"), None),
            P(("gx", "gy"), None),
            P(None, "gy", "gx"),
            P(None, "gy", "gx"),
            P(None, "gy", "gx"),
            P(None, "gy", "gx"),
            P("gy", "gx"),
        ),
        out_specs=(P(None, "gy", "gx"), P(None, "gy", "gx"), P(None, ("gx", "gy"))),
        check_vma=False,
    )
```

```python
import functools

import jax
import jax.numpy as jnp
from jax import lax
from jax.experimental import pallas as pl
from jax.experimental.pallas import tpu as pltpu
from jax.sharding import PartitionSpec as P

diffuse_rate = 0.12
mixing_base = 0.02
mixing_extra = 0.2
heat_factor = 0.5
fresh_factor = 0.5
stress_factor = 0.3

LANES = 128
SEND_GROUP = 32
LAND_GROUP = 32
PICK_GROUP = 32
BACK_GROUP = 32
HALF = 256
PAIR = 2
VMEM_BYTES = 48 * 1024 * 1024
CONTRACT_LAST = (((1,), (1,)), ((), ()))

SMEM = pl.BlockSpec(memory_space=pltpu.SMEM)
VMEM = pl.BlockSpec(memory_space=pltpu.VMEM)


def density(temper_field, saline_field):
    return (
        -0.2 * temper_field
        - 0.05 * temper_field * temper_field
        + 0.8 * saline_field
        + 0.03 * temper_field * saline_field
    )


def two_terms(values):
    high = values.astype(jnp.bfloat16)
    return high, (values - high.astype(jnp.float32)).astype(jnp.bfloat16)


def narrow(places):
    return places.astype(jnp.float32).astype(jnp.bfloat16)


def number_rows(numbers):
    numbers[...] = narrow(lax.broadcasted_iota(jnp.int32, numbers.shape, 0))


def one_hot(places, numbers):
    return jnp.where(numbers == places, jnp.bfloat16(1), jnp.bfloat16(0))


def spread(rows_of, terms, numbers):
    hit = numbers == rows_of
    return jnp.concatenate([jnp.where(hit, term, jnp.bfloat16(0)) for term in terms], axis=0)


def halves_of(address, parallels, meridians):
    shift = meridians.bit_length() - 1
    column = address & (meridians - 1)
    row = (address >> shift) + parallels * (column // HALF)
    return jnp.where(address < 0, -1, row), column % HALF


def picked_rows(rows_of, table, fields, count):
    rows = lax.broadcasted_iota(jnp.int32, (count, rows_of.shape[1]), 0)
    hit = rows == rows_of
    return [
        jnp.sum(
            jnp.where(hit, table[field * count : (field + 1) * count], 0.0), axis=0, keepdims=True
        )
        for field in range(fields)
    ]


def send_kernel(
    capacity, subdomain, table, element, profile, share, out, home, tally, split_table, numbers
):
    devices = tally.shape[0]
    blocks = element.shape[0]
    high_rows = table.shape[0] // 4

    def clear(i, carry):
        tally[i] = 0
        return carry

    lax.fori_loop(0, devices, clear, 0)
    number_rows(numbers)
    out[...] = jnp.full(out.shape, -1.0, jnp.float32)
    high, low = two_terms(table[...])
    split_table[:, :LANES] = high
    split_table[:, LANES:] = low

    def group(g, carry):
        base = pl.multiple_of(g * SEND_GROUP, SEND_GROUP)
        cells = element[pl.ds(base, SEND_GROUP), :]
        near = narrow(cells & (LANES - 1))
        far = cells >> 7
        address = profile[pl.ds(base, SEND_GROUP), :].astype(jnp.float32)
        weight = share[pl.ds(base, SEND_GROUP), :]
        for first in range(0, SEND_GROUP, PAIR):
            names = range(first, first + PAIR)
            hot = jnp.concatenate([one_hot(near[b : b + 1], numbers[...]) for b in names], axis=1)
            found = jnp.dot(
                split_table[...],
                jnp.concatenate([hot, hot], axis=0),
                preferred_element_type=jnp.float32,
            )
            far_row = jnp.concatenate([far[b : b + 1] for b in names], axis=1)
            values = picked_rows(far_row, found, 4, high_rows)
            for turn, b in enumerate(names):
                tile = subdomain[base + b]
                place = tally[tile]
                tally[tile] = place + 1
                home[base + b] = tile * (4 * capacity) + place
                row = tile * (5 * capacity) + place
                for field in range(4):
                    out[pl.ds(row + field * capacity, 1), :] = (
                        values[field][:, turn * LANES : (turn + 1) * LANES] * weight[b : b + 1]
                    )
                out[pl.ds(row + 4 * capacity, 1), :] = address[b : b + 1]
        return carry

    lax.fori_loop(0, blocks // SEND_GROUP, group, 0)


def gather_kernel_params(flops):
    return dict(
        compiler_params=pltpu.CompilerParams(vmem_limit_bytes=VMEM_BYTES),
        cost_estimate=pl.CostEstimate(flops=flops, bytes_accessed=4_000_000, transcendentals=0),
    )


def land_kernel(
    capacity,
    parallels,
    meridians,
    counts,
    arrived,
    remapped,
    places,
    slots,
    values,
    total,
    numbers,
):
    sources = counts.shape[0]
    last = slots.shape[0] - 1
    long_rows = parallels * (meridians // HALF)
    places[...] = jnp.full(places.shape, -1.0, jnp.float32)
    total[...] = jnp.zeros(total.shape, jnp.float32)

    def from_source(source, count):
        row = source * (5 * capacity)
        for field in range(4):
            values[field, pl.ds(count, capacity), :] = arrived[
                pl.ds(row + field * capacity, capacity), :
            ]
        places[pl.ds(count, capacity), :] = arrived[pl.ds(row + 4 * capacity, capacity), :]
        for place in range(capacity):
            slots[count + place] = source * (4 * capacity) + place
        return count + counts[source]

    filled = lax.fori_loop(0, sources, from_source, 0)
    slots[last] = filled
    for extra in range(LAND_GROUP):
        slots[filled + extra] = sources * (4 * capacity)
    number_rows(numbers)

    def group(g, carry):
        base = pl.multiple_of(g * LAND_GROUP, LAND_GROUP)
        address = places[pl.ds(base, LAND_GROUP), :].astype(jnp.int32)
        row, column = halves_of(address, parallels, meridians)
        row, column = narrow(row), narrow(column)
        split = [two_terms(values[field, pl.ds(base, LAND_GROUP), :]) for field in range(4)]
        terms = [split[field][term] for term in range(2) for field in range(4)]
        names = range(LAND_GROUP)
        left = jnp.concatenate(
            [
                spread(row[b : b + 1], [term[b : b + 1] for term in terms], numbers[:long_rows])
                for b in names
            ],
            axis=1,
        )
        right = jnp.concatenate([one_hot(column[b : b + 1], numbers[...]) for b in names], axis=1)
        total[...] += lax.dot_general(
            left, right, CONTRACT_LAST, preferred_element_type=jnp.float32
        )
        return carry

    lax.fori_loop(0, (filled + LAND_GROUP - 1) // LAND_GROUP, group, 0)
    for field in range(4):
        for part in range(meridians // HALF):
            at = field * long_rows + part * parallels
            remapped[field * parallels : (field + 1) * parallels, part * HALF : (part + 1) * HALF] = (
                total[at : at + parallels]
                + total[4 * long_rows + at : 4 * long_rows + at + parallels]
            )


def pick_kernel(capacity, parallels, meridians, slots, surface, places, out, split_table, numbers, found_rows):
    last = slots.shape[0] - 1
    long_rows = parallels * (meridians // HALF)
    half = 4 * long_rows
    filled = slots[last]
    for field in range(4):
        for part in range(meridians // HALF):
            high, low = two_terms(
                surface[
                    field * parallels : (field + 1) * parallels, part * HALF : (part + 1) * HALF
                ]
            )
            at = field * long_rows + part * parallels
            split_table[at : at + parallels] = high
            split_table[half + at : half + at + parallels] = low
    found_rows[...] = jnp.zeros(found_rows.shape, jnp.float32)
    number_rows(numbers)

    def group(g, carry):
        base = pl.multiple_of(g * PICK_GROUP, PICK_GROUP)
        address = places[pl.ds(base, PICK_GROUP), :].astype(jnp.int32)
        row, column = halves_of(address, parallels, meridians)
        column = narrow(column)
        for first in range(0, PICK_GROUP, PAIR):
            names = range(first, first + PAIR)
            hot = jnp.concatenate([one_hot(column[b : b + 1], numbers[...]) for b in names], axis=1)
            found = jnp.dot(split_table[...], hot, preferred_element_type=jnp.float32)
            found = found[:half] + found[half:]
            wide_row = jnp.concatenate([row[b : b + 1] for b in names], axis=1)
            values = picked_rows(wide_row, found, 4, long_rows)
            for turn, b in enumerate(names):
                target = slots[base + b]
                for field in range(4):
                    found_rows[pl.ds(target + field * capacity, 1), :] = values[field][
                        :, turn * LANES : (turn + 1) * LANES
                    ]
        return carry

    lax.fori_loop(0, (filled + PICK_GROUP - 1) // PICK_GROUP, group, 0)
    out[...] = found_rows[: out.shape[0]]


def back_kernel(capacity, home, returned, element, share, out, total, numbers):
    blocks = element.shape[0]
    high_rows = out.shape[0] // 4
    total[...] = jnp.zeros(total.shape, jnp.float32)
    number_rows(numbers)

    def group(g, carry):
        base = pl.multiple_of(g * BACK_GROUP, BACK_GROUP)
        cells = element[pl.ds(base, BACK_GROUP), :]
        near = narrow(cells & (LANES - 1))
        far = narrow(cells >> 7)
        weight = share[pl.ds(base, BACK_GROUP), :]
        names = range(BACK_GROUP)
        lefts = []
        for b in names:
            row = home[base + b]
            split = [
                two_terms(returned[pl.ds(row + field * capacity, 1), :] * weight[b : b + 1])
                for field in range(4)
            ]
            terms = [split[field][term] for term in range(2) for field in range(4)]
            lefts.append(spread(far[b : b + 1], terms, numbers[:high_rows]))
        left = jnp.concatenate(lefts, axis=1)
        right = jnp.concatenate([one_hot(near[b : b + 1], numbers[...]) for b in names], axis=1)
        total[...] += lax.dot_general(
            left, right, CONTRACT_LAST, preferred_element_type=jnp.float32
        )
        return carry

    lax.fori_loop(0, blocks // BACK_GROUP, group, 0)
    half = 4 * high_rows
    out[...] = total[:half] + total[half:]


def next_column(x):
    return pltpu.roll(x, x.shape[1] - 1, axis=1)


def next_row(x):
    return pltpu.roll(x, x.shape[0] - 1, axis=0)


EDGE = 2
SIDE_CHANNELS = LANES // EDGE
END_CHANNELS = 8 // EDGE


def edge_kernel(home, temper, saline, east, north, ocean_mask, first, last, low, high):
    depth, rows, columns = temper.shape
    lane = lax.broadcasted_iota(jnp.int32, (rows, LANES), 1)
    heads, tails = [None] * first.shape[0], [None] * first.shape[0]
    mask = ocean_mask[...].astype(jnp.float32)
    for c in range(4 * depth + 1):
        if c < 4 * depth:
            source, k = (temper, saline, east, north)[c // depth], c % depth
            left, right = source[k, :, :LANES], source[k, :, columns - LANES :]
            top_rows, end_rows = source[k, :EDGE, :], source[k, rows - EDGE :, :]
        else:
            left, right = mask[:, :LANES], mask[:, columns - LANES :]
            top_rows, end_rows = mask[:EDGE], mask[rows - EDGE :]
        tile, at = c // SIDE_CHANNELS, EDGE * (c % SIDE_CHANNELS)
        here = (lane >= at) & (lane < at + EDGE)
        head = left if at == 0 else pltpu.roll(left, at, axis=1)
        tail = pltpu.roll(right, (at + EDGE) % LANES, axis=1) if at + EDGE < LANES else right
        heads[tile] = head if at == 0 else jnp.where(here, head, heads[tile])
        tails[tile] = tail if at == 0 else jnp.where(here, tail, tails[tile])
        spot = EDGE * (c % END_CHANNELS)
        low[c // END_CHANNELS, spot : spot + EDGE, :] = top_rows
        high[c // END_CHANNELS, spot : spot + EDGE, :] = end_rows
    for c in range(4 * depth + 1, END_CHANNELS * low.shape[0]):
        spot = EDGE * (c % END_CHANNELS)
        low[c // END_CHANNELS, spot : spot + EDGE, :] = jnp.zeros((EDGE, columns), jnp.float32)
        high[c // END_CHANNELS, spot : spot + EDGE, :] = jnp.zeros((EDGE, columns), jnp.float32)
    for tile in range(first.shape[0]):
        first[tile] = heads[tile]
        last[tile] = tails[tile]


def rolled(x, shift, axis):
    shift = shift % x.shape[axis]
    return x if shift == 0 else pltpu.roll(x, shift, axis=axis)


def side_of(channel, from_east, from_west):
    at = EDGE * (channel % SIDE_CHANNELS)
    lane = lax.broadcasted_iota(jnp.int32, from_east.shape, 1)
    return jnp.where(
        lane < LANES // 2, rolled(from_east, -at, 1), rolled(from_west, LANES - EDGE - at, 1)
    )


def reversed_tiles(x):
    back = LANES - 1 - lax.broadcasted_iota(jnp.int32, (x.shape[0], LANES), 1)
    pieces = [
        jnp.take_along_axis(x[:, at : at + LANES], back, axis=1, mode="promise_in_bounds")
        for at in range(0, x.shape[1], LANES)
    ]
    return jnp.concatenate(pieces[::-1], axis=1)


def mirrored(across, kind):
    if kind == 2:
        across = -next_column(across)
    last_row, row_before = across[7:8], across[6:7]
    if kind == 3:
        last_row, row_before = -row_before, -row_before
    upper = lax.broadcasted_iota(jnp.int32, across.shape, 0)
    return jnp.where(upper == 0, last_row, row_before)


def turned_corners(corner_f):
    return [reversed_tiles(corner_f[tile]) for tile in range(corner_f.shape[0])]


def fill_channel(target, k, channel, kind, halo, top, turned_rows, turned_ends):
    from_east, from_west, from_north, from_south, _, corner_n, corner_s, _ = halo
    rows = from_east.shape[1]
    columns = from_north.shape[2]
    tile, group = channel // SIDE_CHANNELS, channel // END_CHANNELS
    spot = EDGE * (channel % END_CHANNELS)
    at = EDGE * (channel % SIDE_CHANNELS)
    tiles = from_east.shape[0]
    target[k, :rows, columns:] = side_of(channel, from_east[tile], from_west[tile])

    def end_of(part, corner, shift):
        return jnp.concatenate(
            [
                rolled(part[group], shift, 0),
                side_of(channel, corner[tile], corner[tiles + tile]),
            ],
            axis=1,
        )

    upper = lax.broadcasted_iota(jnp.int32, (8, columns + LANES), 0)
    lane = lax.broadcasted_iota(jnp.int32, (8, LANES), 1)
    above = end_of(from_north, corner_n, -spot)
    turned_side = jnp.where(
        lane < LANES // 2,
        rolled(turned_ends[tiles + tile], EDGE + at - LANES, 1),
        rolled(turned_ends[tile], at, 1),
    )
    across = mirrored(
        jnp.concatenate([rolled(turned_rows, 8 - EDGE - spot, 0), turned_side], axis=1), kind
    )
    above = jnp.where(top[0] == 1, across, above)
    below = end_of(from_south, corner_s, 8 - EDGE - spot)
    target[k, rows:, :] = jnp.where(upper < 4, above, below)


def fill_wide(targets, sources, depth, halo, top):
    turned_ends = turned_corners(halo[7])
    for kind, (target, source) in enumerate(zip(targets, sources)):
        levels, rows, columns = source.shape
        target[:, :rows, :columns] = source[...]
        turned_rows, group = None, None
        for k in range(levels):
            channel = kind * depth + k
            if channel // END_CHANNELS != group:
                group = channel // END_CHANNELS
                turned_rows = reversed_tiles(halo[4][group])
            fill_channel(target, k, channel, kind, halo, top, turned_rows, turned_ends)


def fill_opens(opens, top, ocean_mask, channel, halo):
    rows, columns = ocean_mask.shape
    opens[0, :rows, :columns] = ocean_mask[...].astype(jnp.float32)
    turned_rows = reversed_tiles(halo[4][channel // END_CHANNELS])
    fill_channel(opens, 0, channel, 0, halo, top, turned_rows, turned_corners(halo[7]))
    here = opens[0]
    opens[1] = here * next_column(here)
    opens[2] = here * next_row(here)
    row_ids = lax.broadcasted_iota(jnp.int32, here.shape, 0)
    opens[3] = jnp.where((row_ids == rows - 1) & (top[0] == 1), 0.0, 1.0)


def mixing_at(t, s, t_below, s_below, mask):
    return (
        mixing_base
        + mixing_extra * jax.nn.sigmoid(4.0 * (density(t, s) - density(t_below, s_below)))
    ) * mask


def step(source, speeds, opens, first, stop, floor, keep, forcing=None, shape=None):
    source_t, source_s = source
    east_all, north_all = speeds
    rows, columns = shape or source_t.shape[1:]

    def kept(x):
        return x[:rows, :columns]

    def weights(speed, open_faces):
        return open_faces * (0.5 * speed + diffuse_rate), open_faces * (0.5 * speed - diffuse_rate)

    def level(k, carry):
        below = jnp.minimum(k + 1, floor)
        pair = (source_t[k], source_s[k])
        mask = opens[0, :rows, :columns]
        t, s = kept(pair[0]), kept(pair[1])
        t_below, s_below = source_t[below, :rows, :columns], source_s[below, :rows, :columns]
        mixing = mixing_at(t, s, t_below, s_below, mask)
        east_near, east_far = weights(east_all[k], opens[1])
        north_near, north_far = weights(north_all[k] * opens[3], opens[2])
        new_gains = []
        for turn, (x, own, x_below) in enumerate(
            ((pair[0], t, t_below), (pair[1], s, s_below))
        ):
            gradient = mixing * (x_below - own)
            east_flux = east_near * x + east_far * next_column(x)
            north_flux = north_near * x + north_far * next_row(x)
            change = (
                kept(pltpu.roll(east_flux, 1, axis=1))
                - kept(east_flux)
                + kept(pltpu.roll(north_flux, 1, axis=0))
                - kept(north_flux)
                + (gradient - carry[turn])
            )
            if forcing is not None:
                change = change + jnp.where(k == 0, kept(forcing[turn]), 0.0)
            keep(turn, k, own + mask * change)
            new_gains.append(gradient)
        return tuple(new_gains)

    if first == 0:
        nothing = jnp.zeros((rows, columns), jnp.float32)
        gains = (nothing, nothing)
    else:
        t, s, t_below, s_below = (
            x[k, :rows, :columns] for k in (first - 1, first) for x in source
        )
        mixing = mixing_at(t, s, t_below, s_below, opens[0, :rows, :columns])
        gains = (mixing * (t_below - t), mixing * (s_below - s))
    lax.fori_loop(first, stop, level, gains)


def turned(x):
    columns = x.shape[1] - LANES
    return jnp.concatenate([reversed_tiles(x[:, :columns]), reversed_tiles(x[:, columns:])], axis=1)


def near_kernel(
    depth,
    top,
    temper,
    saline,
    east,
    north,
    ocean_mask,
    from_east,
    from_west,
    from_north_all,
    from_south_all,
    folded_all,
    corner_n,
    corner_s,
    corner_f,
    remapped,
    remap_sides,
    from_north,
    from_south,
    folded,
    temper_out,
    saline_out,
    surface,
    first_t,
    first_s,
    second_t,
    second_s,
    east_all,
    north_all,
    remap_all,
    opens,
):
    levels, rows, columns = temper.shape
    halo = (
        from_east,
        from_west,
        from_north_all,
        from_south_all,
        folded_all,
        corner_n,
        corner_s,
        corner_f,
    )
    targets, sources = (first_t, first_s, east_all, north_all), (temper, saline, east, north)
    fill_wide(targets, sources, depth, halo, top)
    fill_opens(opens, top, ocean_mask, 4 * depth, halo)
    upper = lax.broadcasted_iota(jnp.int32, (8, columns + LANES), 0)
    remap_all[:, :rows, :columns] = remapped[...]
    remap_all[:, :rows, columns:] = remap_sides[...]
    for field in range(4):
        across = mirrored(turned(folded[field]), field)
        above = jnp.where(top[0] == 1, across, from_north[field])
        remap_all[field, rows:, :] = jnp.where(upper < 4, above, from_south[field])
    east_all[0] = east_all[0] + stress_factor * remap_all[2]
    north_all[0] = north_all[0] + stress_factor * remap_all[3]
    remap_all[0] = heat_factor * remap_all[0]
    remap_all[1] = fresh_factor * remap_all[1]
    forcing = (remap_all[0], remap_all[1])

    def keep_first(target, k, value):
        (second_t, second_s)[target][k] = value

    def keep_last(target, k, value):
        (temper_out, saline_out)[target][k] = value

    speeds = (east_all, north_all)
    step((first_t, first_s), speeds, opens, 0, levels - 1, levels - 1, keep_first, forcing)
    step((second_t, second_s), speeds, opens, 0, levels - 2, levels - 1, keep_last, forcing, (rows, columns))
    mask = opens[0, :rows, :columns]
    t, s = temper_out[0], saline_out[0]
    surface[0] = t * mask
    surface[1] = s * mask
    surface[2] = density(t, s) * mask
    surface[3] = east_all[0, :rows, :columns] * mask


def deep_kernel(
    top,
    temper,
    saline,
    east,
    north,
    ocean_mask,
    from_east,
    from_west,
    from_north,
    from_south,
    folded,
    corner_n,
    corner_s,
    corner_f,
    temper_near,
    saline_near,
    temper_out,
    saline_out,
    first_t,
    first_s,
    second_t,
    second_s,
    east_all,
    north_all,
    opens,
):
    depth, rows, columns = temper.shape
    near = temper_near.shape[0]
    halo = (from_east, from_west, from_north, from_south, folded, corner_n, corner_s, corner_f)
    targets, sources = (first_t, first_s, east_all, north_all), (temper, saline, east, north)
    fill_wide(targets, sources, depth, halo, top)
    fill_opens(opens, top, ocean_mask, 4 * depth, halo)
    temper_out[:near] = temper_near[...]
    saline_out[:near] = saline_near[...]

    def keep_first(target, k, value):
        (second_t, second_s)[target][k] = value

    def keep_last(target, k, value):
        (temper_out, saline_out)[target][k] = value

    speeds = (east_all, north_all)
    step((first_t, first_s), speeds, opens, near - 1, depth, depth - 1, keep_first)
    step((second_t, second_s), speeds, opens, near, depth, depth - 1, keep_last, None, (rows, columns))


def across_fold(count_gx, count_gy):
    return [
        (i * count_gy + count_gy - 1, (count_gx - 1 - i) * count_gy + count_gy - 1)
        for i in range(count_gx)
    ]


def edge_halo(first, last, low, high):
    count_gx, count_gy = lax.axis_size("gx"), lax.axis_size("gy")
    north_of = [(i + 1, i) for i in range(count_gy - 1)]
    south_of = [(i, i + 1) for i in range(count_gy - 1)]
    across = across_fold(count_gx, count_gy)
    from_west = lax.ppermute(last, "gx", [(i, (i + 1) % count_gx) for i in range(count_gx)])
    from_east = lax.ppermute(first, "gx", [((i + 1) % count_gx, i) for i in range(count_gx)])
    from_south = lax.ppermute(high, "gy", south_of)
    from_north = lax.ppermute(low, "gy", north_of)
    folded = lax.ppermute(high, ("gx", "gy"), across)
    corner_low = jnp.concatenate([from_east[:, :8], from_west[:, :8]], axis=0)
    corner_high = jnp.concatenate([from_east[:, -8:], from_west[:, -8:]], axis=0)
    return (
        from_east,
        from_west,
        from_north,
        from_south,
        folded,
        lax.ppermute(corner_low, "gy", north_of),
        lax.ppermute(corner_high, "gy", south_of),
        lax.ppermute(corner_high, ("gx", "gy"), across),
    )


def tile_halo(x):
    rows, columns = x.shape[1:]
    count_gx, count_gy = lax.axis_size("gx"), lax.axis_size("gy")
    from_west = lax.ppermute(
        x[:, :, -LANES:], "gx", [(i, (i + 1) % count_gx) for i in range(count_gx)]
    )
    from_east = lax.ppermute(
        x[:, :, :LANES], "gx", [((i + 1) % count_gx, i) for i in range(count_gx)]
    )
    lane = lax.broadcasted_iota(jnp.int32, from_west.shape, 2)
    sides = jnp.where(lane < LANES // 2, from_east, from_west)
    low = jnp.concatenate([x[:, :8], sides[:, :8]], axis=2)
    high = jnp.concatenate([x[:, -8:], sides[:, -8:]], axis=2)
    from_south = lax.ppermute(high, "gy", [(i, i + 1) for i in range(count_gy - 1)])
    from_north = lax.ppermute(low, "gy", [(i + 1, i) for i in range(count_gy - 1)])
    folded = lax.ppermute(high, ("gx", "gy"), across_fold(count_gx, count_gy))
    return sides, from_north, from_south, folded


def body(
    air_forcing_quantities,
    segment_sea_subdomain,
    overlay_air_element,
    overlay_sea_profile,
    overlay_fraction_share,
    thermal_deviation,
    saltiness_deviation,
    zonal_interface_speed,
    poleward_interface_speed,
    sea_profile_indicator,
):
    devices = lax.axis_size("gx") * lax.axis_size("gy")
    blocks = segment_sea_subdomain.shape[0]
    atm_cells = air_forcing_quantities.shape[1]
    depth, parallels, meridians = thermal_deviation.shape
    capacity = max(2, 2 * blocks // devices)
    slot_count = devices * capacity
    spare = max(LAND_GROUP, PICK_GROUP, capacity)
    f32 = jnp.float32
    air = air_forcing_quantities
    table = jnp.stack([air[0] + air[1] + air[2] + air[3], air[5] - air[4], air[6], air[7]])
    table = table.reshape(4 * atm_cells // LANES, LANES)

    outgoing, home = pl.pallas_call(
        functools.partial(send_kernel, capacity),
        out_shape=(
            jax.ShapeDtypeStruct((slot_count * 5, LANES), f32),
            jax.ShapeDtypeStruct((blocks,), jnp.int32),
        ),
        in_specs=[SMEM, VMEM, VMEM, VMEM, VMEM],
        out_specs=(VMEM, SMEM),
        scratch_shapes=[
            pltpu.SMEM((devices,), jnp.int32),
            pltpu.VMEM((table.shape[0], 2 * LANES), jnp.bfloat16),
            pltpu.VMEM((LANES, LANES), jnp.bfloat16),
        ],
        **gather_kernel_params(10**9),
    )(
        segment_sea_subdomain.reshape(blocks),
        table,
        overlay_air_element,
        overlay_sea_profile,
        overlay_fraction_share,
    )

    arrived = lax.all_to_all(outgoing, ("gx", "gy"), split_axis=0, concat_axis=0, tiled=True)
    channels = 4 * depth + 1
    packed = jax.ShapeDtypeStruct((-(-channels // SIDE_CHANNELS), parallels, LANES), f32)
    stacked = jax.ShapeDtypeStruct((-(-channels // END_CHANNELS), 8, meridians), f32)
    edges = pl.pallas_call(
        edge_kernel,
        out_shape=(packed, packed, stacked, stacked),
        in_specs=[SMEM] + [VMEM] * 5,
        out_specs=(VMEM,) * 4,
        **gather_kernel_params(10**7),
    )(
        home,
        thermal_deviation,
        saltiness_deviation,
        zonal_interface_speed,
        poleward_interface_speed,
        sea_profile_indicator,
    )
    halo = edge_halo(*edges)

    counts = jnp.sum(
        (arrived.reshape(devices, 5, capacity, LANES)[:, 4, :, 0] >= 0).astype(jnp.int32), axis=1
    )
    remapped, places, slots = pl.pallas_call(
        functools.partial(land_kernel, capacity, parallels, meridians),
        out_shape=(
            jax.ShapeDtypeStruct((4 * parallels, meridians), f32),
            jax.ShapeDtypeStruct((slot_count + spare, LANES), f32),
            jax.ShapeDtypeStruct((slot_count + spare + 1,), jnp.int32),
        ),
        in_specs=[SMEM, VMEM],
        out_specs=(VMEM, VMEM, SMEM),
        scratch_shapes=[
            pltpu.VMEM((4, slot_count + spare, LANES), f32),
            pltpu.VMEM((8 * parallels * (meridians // HALF), HALF), f32),
            pltpu.VMEM((HALF, LANES), jnp.bfloat16),
        ],
        **gather_kernel_params(2 * 10**10),
    )(counts, arrived)
    remapped = remapped.reshape(4, parallels, meridians)
    around = tile_halo(remapped)

    top = (lax.axis_index("gy") == lax.axis_size("gy") - 1).astype(jnp.int32).reshape(1)
    wide = (parallels + 8, meridians + LANES)
    near, levels = 2, 4
    first_levels = pl.BlockSpec((levels, parallels, meridians), lambda i: (0, 0, 0))
    cube = jax.ShapeDtypeStruct((depth, parallels, meridians), f32)
    slab = jax.ShapeDtypeStruct((near, parallels, meridians), f32)
    temper_near, saline_near, surface = pl.pallas_call(
        functools.partial(near_kernel, depth),
        grid=(1,),
        out_shape=(slab, slab, jax.ShapeDtypeStruct((4, parallels, meridians), f32)),
        in_specs=[SMEM] + [first_levels] * 4 + [VMEM] * 14,
        out_specs=(VMEM, VMEM, VMEM),
        scratch_shapes=[pltpu.VMEM((levels,) + wide, f32)] * 6
        + [pltpu.VMEM((4,) + wide, f32)] * 2,
        **gather_kernel_params(10**8),
    )(
        top,
        thermal_deviation,
        saltiness_deviation,
        zonal_interface_speed,
        poleward_interface_speed,
        sea_profile_indicator,
        *halo,
        remapped,
        *around,
    )

    picked = pl.pallas_call(
        functools.partial(pick_kernel, capacity, parallels, meridians),
        out_shape=jax.ShapeDtypeStruct((slot_count * 4, LANES), f32),
        in_specs=[SMEM, VMEM, VMEM],
        out_specs=VMEM,
        scratch_shapes=[
            pltpu.VMEM((8 * parallels * (meridians // HALF), HALF), jnp.bfloat16),
            pltpu.VMEM((HALF, LANES), jnp.bfloat16),
            pltpu.VMEM(((slot_count + capacity) * 4, LANES), f32),
        ],
        **gather_kernel_params(2 * 10**10),
    )(slots, surface.reshape(4 * parallels, meridians), places)
    picked, top = lax.optimization_barrier((picked, top))
    returned = lax.all_to_all(picked, ("gx", "gy"), split_axis=0, concat_axis=0, tiled=True)
    temper, saline = pl.pallas_call(
        deep_kernel,
        out_shape=(cube, cube),
        in_specs=[SMEM] + [VMEM] * 15,
        out_specs=(VMEM, VMEM),
        scratch_shapes=[pltpu.VMEM((depth,) + wide, f32)] * 6 + [pltpu.VMEM((4,) + wide, f32)],
        **gather_kernel_params(10**9),
    )(
        top,
        thermal_deviation,
        saltiness_deviation,
        zonal_interface_speed,
        poleward_interface_speed,
        sea_profile_indicator,
        *halo,
        temper_near,
        saline_near,
    )
    back_fields = pl.pallas_call(
        functools.partial(back_kernel, capacity),
        out_shape=jax.ShapeDtypeStruct((4 * atm_cells // LANES, LANES), f32),
        in_specs=[SMEM, VMEM, VMEM, VMEM],
        out_specs=VMEM,
        scratch_shapes=[
            pltpu.VMEM((8 * atm_cells // LANES, LANES), f32),
            pltpu.VMEM((LANES, LANES), jnp.bfloat16),
        ],
        **gather_kernel_params(2 * 10**9),
    )(home, returned, overlay_air_element, overlay_fraction_share)
    return temper, saline, back_fields.reshape(4, atm_cells)


def solution(mesh):
    return jax.shard_map(
        body,
        mesh=mesh,
        in_specs=(
            P(None, ("gx", "gy")),
            P(("gx", "gy"), None),
            P(("gx", "gy"), None),
            P(("gx", "gy"), None),
            P(("gx", "gy"), None),
            P(None, "gy", "gx"),
            P(None, "gy", "gx"),
            P(None, "gy", "gx"),
            P(None, "gy", "gx"),
            P("gy", "gx"),
        ),
        out_specs=(P(None, "gy", "gx"), P(None, "gy", "gx"), P(None, ("gx", "gy"))),
        check_vma=False,
    )
```
